256 devices in a mesh: grp: 8 (over y, core), brick: 32 (over x, z).
Axes of the slice: x: 4, y: 4, z: 8, core: 2. Of those that a mesh axis runs over, the one named last changes fastest.
Arguments:
- right_side: float32 [3, 128, 512, 128], P(None, 'grp', 'brick'), may hold values from -24 to 24
- stiffness: float32 [128, 512, 128], P('grp', 'brick'), may hold values from 1 to 10
- reaction: float32 [128, 512, 128], P('grp', 'brick'), may hold values from 0.1 to 1
Outputs:
- correction: float32 [3, 128, 512, 128], P(None, 'grp', 'brick')
The draws below stay inside these ranges and needn't reach their ends.
All inputs are finite; a program needn't handle non-finite values.
Results may differ from the reference program's by a relative error of at most 0.00025.
Values sent between devices are 32-bit elements; how exact they have to be, the bound alone decides.
No kernel may reach another device: no remote copies, remote signals or barrier semaphores. Data moves between devices by JAX's collectives and lax.ppermute only.
A program may use at most 128 MiB of HBM per device.

```python
import math
import jax
import jax.numpy as jnp

NZ = 128
LEVELS = 4
NX = 128
NY = 512


def draw_right_side(key, part):
    key = jax.random.fold_in(key, 11)
    return 6.0 * jax.random.truncated_normal(key, -4.0, 4.0, (3, NX, NY, NZ), jnp.float32)


def level_of(rng, shape, shards, low, largest):
    loudness = 1.0
    for dim, blocks in shards:
        draws = jax.random.uniform(jax.random.fold_in(jax.random.fold_in(rng, 6), dim), (blocks,), jnp.float32, low / len(shards), largest / len(shards))
        loudness = loudness * jnp.repeat(jnp.exp(draws), shape[dim] // blocks).reshape((-1,) + (1,) * (len(shape) - 1 - dim))
    return loudness


def setup_inputs(seed: int = 0) -> dict:
    key_of = jax.random.split(jax.random.key(seed), 4)
    right_side = draw_right_side(jax.random.fold_in(key_of[3], 71), 0)
    stiffness = jnp.clip(jnp.exp(math.log(10.0) - 2.3025851 * jax.random.uniform(key_of[1], (NX, NY, NZ), jnp.float32) ** level_of(key_of[1], (NX, NY, NZ), ((0, 8), (1, 32)), -0.2, 0.2)), 1.0, 10.0)
    reaction = jnp.clip(jnp.exp(math.log(1.0) - 2.3025851 * jax.random.uniform(key_of[2], (NX, NY, NZ), jnp.float32) ** level_of(key_of[2], (NX, NY, NZ), ((0, 8), (1, 32)), -0.2, 0.2)), 0.1, 1.0)
    return dict(right_side=right_side, stiffness=stiffness, reaction=reaction)


BETA = 1.0
THETA = 1.5
DELTA = 1.0
SIGMA = 1.5


def rate_list():
    rates = [1.0 / SIGMA]
    for number in range(3):
        rates.append(1.0 / (2.0 * SIGMA - rates[-1]))
    return rates


def advance(step, old, resid, inverse):
    rates = rate_list()
    return rates[step] * rates[step - 1] * old + (2.0 * rates[step] / DELTA) * (inverse * resid)


def offset_of(axis, sign):
    return tuple(sign if index == axis else 0 for index in range(3))


def view(array, shift, rows, cols, depth):
    return array[..., 1 + shift[0]:1 + shift[0] + rows, 1 + shift[1]:1 + shift[1] + cols, 1 + shift[2]:1 + shift[2] + depth]


def face_total(stiff, rows, cols, depth):
    centre = view(stiff, (0, 0, 0), rows, cols, depth)
    total = jnp.zeros_like(centre)
    for axis in range(3):
        total = total + 0.5 * (centre + view(stiff, offset_of(axis, 1), rows, cols, depth))
        total = total + 0.5 * (centre + view(stiff, offset_of(axis, -1), rows, cols, depth))
    return total


def inverse_diagonal(coeff, scale):
    rows = coeff.shape[1] - 2
    cols = coeff.shape[2] - 2
    depth = coeff.shape[3]
    stiff = jnp.pad(coeff[0], ((0, 0), (0, 0), (1, 1)))
    react = coeff[1, 1:-1, 1:-1, :]
    faces = face_total(stiff, rows, cols, depth)
    return (1.0 / (scale * (faces + 2.0 * BETA) + react))[None]


def operate(field, coeff, scale):
    rows = field.shape[1] - 2
    cols = field.shape[2] - 2
    depth = field.shape[3]
    padded = jnp.pad(field, ((0, 0), (0, 0), (0, 0), (1, 1)))
    stiff = jnp.pad(coeff[0], ((0, 0), (0, 0), (1, 1)))
    react = coeff[1, 1:-1, 1:-1, :]
    centre = view(stiff, (0, 0, 0), rows, cols, depth)
    middle = view(padded, (0, 0, 0), rows, cols, depth)
    laplace = jnp.zeros_like(middle)
    for axis in range(3):
        ahead = offset_of(axis, 1)
        behind = offset_of(axis, -1)
        upper = 0.5 * (centre + view(stiff, ahead, rows, cols, depth))
        lower = 0.5 * (centre + view(stiff, behind, rows, cols, depth))
        laplace = laplace + upper * (middle - view(padded, ahead, rows, cols, depth))
        laplace = laplace + lower * (middle - view(padded, behind, rows, cols, depth))

    def divergence(anchor):
        total = jnp.zeros_like(centre)
        for axis in range(3):
            moved = tuple(anchor[index] + offset_of(axis, 1)[index] for index in range(3))
            total = total + view(padded[axis], moved, rows, cols, depth) - view(padded[axis], anchor, rows, cols, depth)
        return total

    centre_div = divergence((0, 0, 0))
    parts = []
    for axis in range(3):
        graddiv = divergence(offset_of(axis, -1)) - centre_div
        parts.append(scale * (laplace[axis] + BETA * graddiv) + react * middle[axis])
    return jnp.stack(parts)


def shrink(array):
    comps, rows, cols, depth = array.shape
    blocks = array.reshape(comps, rows // 2, 2, cols // 2, 2, depth // 2, 2)
    return blocks.mean(axis=(2, 4, 6))


def grow(array):
    return jnp.repeat(jnp.repeat(jnp.repeat(array, 2, axis=1), 2, axis=2), 2, axis=3)


def widen(array, width):
    return jnp.pad(array, ((0, 0), (width, width), (width, width), (0, 0)))


def reference(right_side, stiffness, reaction):
    coeff = jnp.stack([stiffness, reaction])
    levels = []
    for level in range(LEVELS):
        if level > 0:
            coeff = shrink(coeff)
        padded = widen(coeff, 1)
        scale = 0.25 ** level
        levels.append((padded, inverse_diagonal(padded, scale), scale))

    def product(field, level):
        padded, inverse, scale = levels[level]
        return operate(widen(field, 1), padded, scale)

    def relax(source, start, level):
        inverse = levels[level][1]
        if start is None:
            resid = source
            state = jnp.zeros_like(source)
        else:
            resid = source - product(start, level)
            state = start
        step_dir = inverse * resid / THETA
        for step in range(1, 4):
            state = state + step_dir
            resid = source - product(state, level)
            step_dir = advance(step, step_dir, resid, inverse)
        return state + step_dir

    sources = [right_side]
    saved = []
    for level in range(LEVELS - 1):
        smooth = relax(sources[level], None, level)
        saved.append(smooth)
        resid = sources[level] - product(smooth, level)
        sources.append(shrink(resid))
    answer = relax(sources[-1], None, LEVELS - 1)
    for level in reversed(range(LEVELS - 1)):
        answer = relax(sources[level], saved[level] + grow(answer), level)
    return answer
```

```python
import jax
import jax.numpy as jnp
from jax import lax
from jax.experimental import pallas as pl
from jax.experimental.pallas import tpu as pltpu
from jax.sharding import PartitionSpec as P

BETA = 1.0
THETA = 1.5
DELTA = 1.0
SIGMA = 1.5
LANES = 128
HALO = 8
NEAR = 10
SKIRT = 12
REACH = 5
F32 = jnp.float32


def rate_list():
    rates = [1.0 / SIGMA]
    for number in range(3):
        rates.append(1.0 / (2.0 * SIGMA - rates[-1]))
    return rates


RATES = rate_list()
STEPS = [(0.0, 1.0 / THETA)] + [
    (RATES[k] * RATES[k - 1], 2.0 * RATES[k] / DELTA) for k in (1, 2, 3)
]


def lane_of(shape):
    return lax.broadcasted_iota(jnp.int32, shape, len(shape) - 1)


def row_of(shape):
    return lax.broadcasted_iota(jnp.int32, shape, len(shape) - 2)


def ahead_y(v):
    return pltpu.roll(v, v.shape[0] - 1, 0)


def behind_y(v):
    return pltpu.roll(v, 1, 0)


def ahead_z(v):
    return pltpu.roll(v, LANES - 1, 1)


def behind_z(v):
    return pltpu.roll(v, 1, 1)


class Level:
    def __init__(self, scale, depth, rows, height):
        self.scale = scale
        self.depth = depth
        self.groups = LANES // depth
        self.rows = rows
        self.height = height

    def shape(self, *lead):
        return (*lead, self.rows + 2, self.height, LANES)

    def lanes(self):
        z = lane_of((self.height, LANES)) % self.depth
        return z == 0, z == self.depth - 1


def ghosts(level, ref, index=()):
    if level.groups == 1:
        return
    lane = lane_of((level.height, LANES))
    first = ref[(*index, 1)]
    last = ref[(*index, level.rows)]
    ref[(*index, 0)] = jnp.where(lane < level.depth, 0.0, pltpu.roll(last, level.depth, 1))
    ref[(*index, level.rows + 1)] = jnp.where(
        lane >= LANES - level.depth, 0.0, pltpu.roll(first, LANES - level.depth, 1)
    )


def setup(level, stiff, react, coef, inside, lo, hi):
    kx, ky, kym, kz, kzm, diag, inv = coef
    half = 0.5 * level.scale
    front, back = level.lanes()
    kx[lo - 1] = half * (stiff(lo - 1) + stiff(lo))

    def body(i, _):
        centre = stiff(i)
        xp = half * (centre + stiff(i + 1))
        xm = kx[i - 1]
        yp = half * (centre + ahead_y(centre))
        ym = behind_y(yp)
        zp = half * (centre + jnp.where(back, 0.0, ahead_z(centre)))
        zm = half * (centre + jnp.where(front, 0.0, behind_z(centre)))
        total = ((xp + xm) + (yp + ym)) + (zp + zm) + react(i)
        kx[i] = xp
        ky[i] = yp
        kym[i] = ym
        kz[i] = jnp.where(back, 0.0, zp)
        kzm[i] = jnp.where(front, 0.0, zm)
        diag[i] = total
        inv[i] = jnp.where(inside(i), 1.0 / (total + 2.0 * BETA * level.scale), 0.0)
        return 0

    lax.fori_loop(lo, hi, body, 0)


def begin(level, src, coef, state, direction, lo, hi):
    inv = coef[6]

    def body(i, _):
        scaled = inv[i] * (1.0 / THETA)
        for c in range(3):
            value = scaled * src[c, i]
            state[c, i] = value
            direction[c, i] = value
        return 0

    lax.fori_loop(lo, hi, body, 0)
    for c in range(3):
        ghosts(level, state, (c,))


def sweep(level, src, coef, state, lo, hi, emit):
    kx, ky, kym, kz, kzm, diag, inv = coef
    front, back = level.lanes()
    bulk = BETA * level.scale

    def spread(i):
        ux, uy, uz = state[0, i], state[1, i], state[2, i]
        return (
            (state[0, i + 1] - ux)
            + (ahead_y(uy) - uy)
            + (jnp.where(back, 0.0, ahead_z(uz)) - uz)
        ) * bulk

    def body(i, before):
        here = spread(i)
        for c in range(3):
            u = state[c, i]
            flux = kx[i] * state[c, i + 1] + kx[i - 1] * state[c, i - 1]
            flux = flux + (ky[i] * ahead_y(u) + kym[i] * behind_y(u))
            flux = flux + (kz[i] * ahead_z(u) + kzm[i] * behind_z(u))
            if c == 0:
                other = before
            elif c == 1:
                other = behind_y(here)
            else:
                other = jnp.where(front, bulk * u, behind_z(here))
            resid = src[c, i] - diag[i] * u + flux + (here - other)
            emit(i, c, u, resid)
        return here

    lax.fori_loop(lo, hi, body, spread(lo - 1))


def step(level, number, src, coef, state, fresh, direction, lo, hi):
    keep, gain = STEPS[number]
    inv = coef[6]

    def emit(i, c, u, resid):
        move = (gain * inv[i]) * resid
        if number > 0:
            move = move + keep * direction[c, i]
        direction[c, i] = move
        fresh[c, i] = u + move

    sweep(level, src, coef, state, lo, hi, emit)
    for c in range(3):
        ghosts(level, fresh, (c,))


def residual(level, src, coef, state, out, lo, hi):
    def emit(i, c, u, resid):
        out[c, i] = resid

    sweep(level, src, coef, state, lo, hi, emit)


def pick(rows, cols, rule, value):
    shape = (rows, cols)
    return jnp.where(rule(row_of(shape), lane_of(shape)), value, 0.0).astype(F32)


def mix(values, matrix):
    return jnp.dot(values, matrix, precision=lax.Precision.HIGHEST, preferred_element_type=F32)


def pairs(ref, index, start, count):
    return ref[(*index, pl.ds(start, count, 2))] + ref[(*index, pl.ds(start + 1, count, 2))]


def vmem(count):
    return [pl.BlockSpec(memory_space=pltpu.VMEM)] * count


def call(kernel, outs, scratch, *args, name):
    smem = pl.BlockSpec(memory_space=pltpu.SMEM)
    return pl.pallas_call(
        kernel,
        out_shape=[jax.ShapeDtypeStruct(s, F32) for s in outs],
        in_specs=[smem] + vmem(len(args) - 1),
        out_specs=vmem(len(outs)),
        scratch_shapes=[pltpu.VMEM(s, F32) for s in scratch],
        compiler_params=pltpu.CompilerParams(vmem_limit_bytes=50 * 2**20),
        name=name,
    )(*args)


def cut_kernel(place, f, k, r, lo, hi):
    for q in range(5):
        part = (lambda s: f[q, :, s]) if q < 3 else (lambda s: (k, r)[q - 3][:, s])
        lo[q] = part(slice(0, HALO))
        hi[q] = part(slice(HALO, 2 * HALO))


def join_kernel(place, f, k, r, lo, hi, first, second):
    for q in range(5):
        for half, out in enumerate((first, second)):
            rows = slice(8 * half, 8 * half + 8)
            part = f[q, rows] if q < 3 else (k, r)[q - 3][rows]
            out[q, :, 0:8] = lo[q, rows]
            out[q, :, 8:24] = part
            out[q, :, 24:32] = hi[q, rows]


FINE = Level(1.0, 128, 30, 32)
MIDDLE = Level(0.25, 64, 14, 32)
COARSE = Level(0.0625, 32, 8, 48)
LAST = Level(0.015625, 16, 2, 24)


def coef_shapes(level):
    return [level.shape()] * 7


def fine_inside(place):
    y = place[1] * 16 - HALO + row_of((32, LANES))
    fits = (y >= 0) & (y < place[3] * 16)

    def inside(i):
        x = place[0] * 16 + i - HALO
        return fits & (x >= 0) & (x < place[2] * 16)

    return inside


def fine_down(place, first, second, lo, hi, data, saved, packed, s0, d0, t0, sums, *coef):
    for q in range(5):
        data[q, 0:8] = lo[q]
        data[q, 8:16] = first[q]
        data[q, 16:24] = second[q]
        data[q, 24:32] = hi[q]
    inside = fine_inside(place)
    setup(FINE, lambda i: data[3, i], lambda i: data[4, i], coef, inside, 1, 31)
    begin(FINE, data, coef, s0, d0, 1, 31)
    step(FINE, 1, data, coef, s0, t0, d0, 2, 30)
    step(FINE, 2, data, coef, t0, s0, d0, 3, 29)
    step(FINE, 3, data, coef, s0, t0, d0, 4, 28)
    saved[...] = t0[:, 4:28]
    residual(FINE, data, coef, t0, d0, 6, 26)
    pair = s0.at[0]
    wide = sums
    for q in range(5):
        for t in range(16):
            half, i = divmod(t, 8)
            where = (q, i, slice(None), slice(half * LANES, half * LANES + LANES))
            if q >= 3:
                pair[t] = data[q, 2 * t] + data[q, 2 * t + 1]
            elif 3 <= t <= 12:
                pair[t] = d0[q, 2 * t] + d0[q, 2 * t + 1]
            else:
                wide[where] = jnp.zeros((16, LANES), F32)
                continue
            wide[where] = pairs(pair, (t,), 0, 16)
    matrix = pick(
        2 * LANES, LANES, lambda a, b: (a % LANES) // 2 + 64 * (a // LANES) == b, 0.125
    )
    packed[...] = mix(wide[...].reshape(5 * 8 * 16, 2 * LANES), matrix).reshape(5, 8, 16, LANES)


def middle_cut(place, own, left, right, up, down, centre):
    lane = lane_of((32, LANES))

    for q in range(5):
        for i in range(8):
            centre[q, i, 0:12] = left[q, i, 0:12]
            centre[q, i, 12:20] = own[q, i, 4:12]
            centre[q, i, 20:32] = right[q, i, 4:16]
        for t in range(5):
            tail = pltpu.roll(centre[q, 7], 64, 1) if t == 0 else centre[q, t - 1]
            up[q, t] = jnp.where(lane < 64, centre[q, 2 + t], tail)
            head = pltpu.roll(centre[q, 0], 64, 1) if t == 4 else centre[q, 4 + t]
            down[q, t] = jnp.where(lane < 64, head, centre[q, 1 + t])


def middle_inside(place):
    y = place[1] * 8 - SKIRT + row_of((32, LANES))
    fits = (y >= 0) & (y < place[3] * 8)
    x0 = place[0] * 8 - NEAR + 14 * (lane_of((32, LANES)) // 64)

    def inside(i):
        x = x0 + (i - 1)
        return fits & (x >= 0) & (x < place[2] * 8)

    return inside


def middle_down(place, centre, lo, hi, data, saved, packed, s1, d1, t1, pair, sums, *coef):
    lane = lane_of((32, LANES))
    low = lane < 64
    for q in range(5):
        for i in range(14):
            if i < 5:
                a = lo[q, i]
            elif i < 10:
                a = pltpu.roll(lo[q, i - 5], 64, 1)
            else:
                a = centre[q, i - 6]
            if i < 4:
                b = centre[q, i]
            elif i < 9:
                b = pltpu.roll(hi[q, i - 4], 64, 1)
            else:
                b = hi[q, i - 9]
            data[q, i + 1] = jnp.where(low, a, b)
        ghosts(MIDDLE, data, (q,))
    setup(MIDDLE, lambda i: data[3, i], lambda i: data[4, i], coef, middle_inside(place), 1, 15)
    begin(MIDDLE, data, coef, s1, d1, 1, 15)
    step(MIDDLE, 1, data, coef, s1, t1, d1, 1, 15)
    step(MIDDLE, 2, data, coef, t1, s1, d1, 1, 15)
    step(MIDDLE, 3, data, coef, s1, saved, d1, 1, 15)
    residual(MIDDLE, data, coef, saved, d1, 11, 15)
    residual(MIDDLE, data, coef, saved, d1, 1, 5)
    for q in range(5):
        from_, at = (d1, q) if q < 3 else (data, q)
        for m in range(2):
            a = from_[at, 11 + 2 * m] + from_[at, 12 + 2 * m]
            b = from_[at, 1 + 2 * m] + from_[at, 2 + 2 * m]
            pair[q, m] = jnp.where(low, a, b)
            sums[q, :, m * LANES : m * LANES + LANES] = pairs(pair, (q, m), 0, 16)
    matrix = pick(
        2 * LANES,
        LANES,
        lambda a, b: (a // LANES) * 32 + ((a % LANES) // 64) * 64 + (a % 64) // 2 == b,
        0.125,
    )
    packed[...] = mix(sums[...].reshape(5 * 16, 2 * LANES), matrix).reshape(5, 16, LANES)


def column_kernel(place, parts, out):
    zero = jnp.zeros((4, LANES), F32)
    for q in range(5):
        out[q, 0:2] = zero[0:2]
        out[q, 46:48] = zero[0:2]
    for d in range(2 * REACH + 1):
        at = place[1] + (d - REACH)
        valid = (at >= 0) & (at < place[3])
        safe = jnp.clip(at, 0, place[3] - 1)
        for q in range(5):
            block = parts[safe, 4 * q : 4 * q + 4]
            out[q, 2 + 4 * d : 6 + 4 * d] = jnp.where(valid, block, zero)


def coarse_inside(place):
    sub = row_of((48, LANES))
    y = place[1] * 4 - 22 + sub
    fits = (y >= 0) & (y < place[3] * 4)
    return lambda i: fits


def last_inside(place):
    y = place[1] * 2 - 11 + row_of((24, LANES))
    fits = (y >= 0) & (y < place[3] * 2)
    return lambda i: fits


def climb(place, parts, data1, saved1, data0, saved0, out, *scratch):
    scratch = list(scratch)

    def take(count):
        got, scratch[:] = scratch[:count], scratch[count:]
        return got

    data2, s2, t2, d2, keep2 = take(5)
    coef2 = take(7)
    sums3 = take(1)[0]
    data3, s3, t3, d3 = take(4)
    coef3 = take(7)
    grown3, grown2, grown1 = take(3)
    s1, t1, d1 = take(3)
    coef1 = take(7)
    s0, t0, d0 = take(3)
    coef0 = take(7)

    lane = lane_of((48, LANES))
    group = lane // 32
    for q in range(5):
        for i in range(8):
            row = None
            for g in range(4):
                block = parts[2 * g + i // 4, q]
                shift = ((g - i % 4) * 32) % LANES
                block = pltpu.roll(block, shift, 1) if shift else block
                row = block if row is None else jnp.where(group == g, block, row)
            data2[q, i + 1] = row
        ghosts(COARSE, data2, (q,))
    setup(COARSE, lambda i: data2[3, i], lambda i: data2[4, i], coef2, coarse_inside(place), 1, 9)
    begin(COARSE, data2, coef2, s2, d2, 1, 9)
    step(COARSE, 1, data2, coef2, s2, t2, d2, 1, 9)
    step(COARSE, 2, data2, coef2, t2, s2, d2, 1, 9)
    step(COARSE, 3, data2, coef2, s2, keep2, d2, 1, 9)
    residual(COARSE, data2, coef2, keep2, d2, 1, 9)

    pair = s2.at[0]
    for q in range(5):
        from_ = d2 if q < 3 else data2
        for t in range(4):
            half, i = divmod(t, 2)
            pair[t] = from_[q, 1 + 2 * t] + from_[q, 2 + 2 * t]
            sums3[q, i, :, half * LANES : half * LANES + LANES] = pairs(pair, (t,), 0, 24)
    matrix = pick(
        2 * LANES,
        LANES,
        lambda a, b: (2 * ((a % LANES) // 32) + a // LANES) * 16 + (a % 32) // 2 == b,
        0.125,
    )
    shrunk = mix(sums3[...].reshape(5 * 2 * 24, 2 * LANES), matrix).reshape(5, 2, 24, LANES)
    for q in range(5):
        for i in range(2):
            data3[q, i + 1] = shrunk[q, i]
        ghosts(LAST, data3, (q,))
    setup(LAST, lambda i: data3[3, i], lambda i: data3[4, i], coef3, last_inside(place), 1, 3)
    begin(LAST, data3, coef3, s3, d3, 1, 3)
    step(LAST, 1, data3, coef3, s3, t3, d3, 1, 3)
    step(LAST, 2, data3, coef3, t3, s3, d3, 1, 3)
    step(LAST, 3, data3, coef3, s3, t3, d3, 1, 3)

    matrix = pick(
        LANES,
        2 * LANES,
        lambda a, b: (2 * ((b % LANES) // 32) + b // LANES == a // 16) & ((b % 32) // 2 == a % 16),
        1.0,
    )
    flat = jnp.concatenate([t3[c, i + 1] for c in range(3) for i in range(2)], axis=0)
    wide = mix(flat, matrix)
    for c in range(3):
        for t in range(4):
            half, i = divmod(t, 2)
            at = (c * 2 + i) * 24
            piece = wide[at : at + 24, half * LANES : half * LANES + LANES]
            grown3[c, t, pl.ds(0, 24, 2)] = piece
            grown3[c, t, pl.ds(1, 24, 2)] = piece
            more = grown3[c, t]
            s2[c, 1 + 2 * t] = keep2[c, 1 + 2 * t] + more
            s2[c, 2 + 2 * t] = keep2[c, 2 + 2 * t] + more
        ghosts(COARSE, s2, (c,))
    step(COARSE, 0, data2, coef2, s2, t2, d2, 1, 9)
    step(COARSE, 1, data2, coef2, t2, s2, d2, 1, 9)
    step(COARSE, 2, data2, coef2, s2, t2, d2, 1, 9)
    step(COARSE, 3, data2, coef2, t2, s2, d2, 1, 9)

    setup(MIDDLE, lambda i: data1[3, i], lambda i: data1[4, i], coef1, middle_inside(place), 1, 15)
    matrix = pick(
        LANES,
        LANES,
        lambda a, b: (a < 64) & (b // 64 == a // 32) & ((b % 64) // 2 == a % 32),
        1.0,
    )
    small = lane_of((16, LANES)) < 32

    def window(c, x, slot):
        valid = (x >= 0) & (x < place[2] * 4)
        safe = jnp.clip(x, 0, place[2] * 4 - 1)
        value = s2[c, 1 + safe % 8, 16:32]
        value = pltpu.roll(value, (slot * 32 + LANES - (safe // 8) * 32) % LANES, 1)
        return jnp.where(valid, value, 0.0)

    pieces = []
    for c in range(3):
        for m in range(7):
            x = place[0] * 4 - 5 + m
            pieces.append(jnp.where(small, window(c, x, 0), window(c, x + 7, 1)))
    wide = mix(jnp.concatenate(pieces, axis=0), matrix)
    for c in range(3):
        for m in range(7):
            at = (c * 7 + m) * 16
            piece = wide[at : at + 16]
            grown2[c, m, pl.ds(0, 16, 2)] = piece
            grown2[c, m, pl.ds(1, 16, 2)] = piece
            more = grown2[c, m]
            s1[c, 1 + 2 * m] = saved1[c, 1 + 2 * m] + more
            s1[c, 2 + 2 * m] = saved1[c, 2 + 2 * m] + more
        ghosts(MIDDLE, s1, (c,))
    step(MIDDLE, 0, data1, coef1, s1, t1, d1, 1, 15)
    step(MIDDLE, 1, data1, coef1, t1, s1, d1, 1, 15)
    step(MIDDLE, 2, data1, coef1, s1, t1, d1, 1, 15)
    step(MIDDLE, 3, data1, coef1, t1, s1, d1, 1, 15)

    setup(FINE, lambda i: data0[3, i], lambda i: data0[4, i], coef0, fine_inside(place), 5, 27)
    for half in range(2):
        matrix = pick(LANES, LANES, lambda a, b: a == 64 * half + b // 2, 1.0)
        rows = [9 + t for t in range(6)] if half == 0 else [1 + t for t in range(6)]
        flat = jnp.concatenate([s1[c, i, 8:24] for c in range(3) for i in rows], axis=0)
        wide = mix(flat, matrix)
        for c in range(3):
            for t in range(6):
                at = (c * 6 + t) * 16
                piece = wide[at : at + 16]
                grown1[c, t, pl.ds(0, 16, 2)] = piece
                grown1[c, t, pl.ds(1, 16, 2)] = piece
                more = grown1[c, t]
                row = 2 * (t + 6 * half)
                s0[c, 4 + row] = saved0[c, row] + more
                s0[c, 5 + row] = saved0[c, row + 1] + more
    step(FINE, 0, data0, coef0, s0, t0, d0, 5, 27)
    step(FINE, 1, data0, coef0, t0, s0, d0, 6, 26)
    step(FINE, 2, data0, coef0, s0, t0, d0, 7, 25)
    keep, gain = STEPS[3]

    def emit(i, c, u, resid):
        move = (gain * coef0[6][i]) * resid + keep * d0[c, i]
        out[c, i - 8] = (u + move)[8:24]

    sweep(FINE, data0, coef0, t0, 8, 24, emit)


def shift(value, axis, by):
    count = lax.axis_size(axis)
    return lax.ppermute(
        value, axis, [(i, i + by) for i in range(count) if 0 <= i + by < count]
    )


def on_device(right_side, stiffness, reaction):
    place = jnp.stack(
        [
            lax.axis_index("grp"),
            lax.axis_index("brick"),
            jnp.int32(lax.axis_size("grp")),
            jnp.int32(lax.axis_size("brick")),
        ]
    ).astype(jnp.int32)
    local = (right_side, stiffness, reaction)
    low, high = call(cut_kernel, [(5, 16, 8, 128)] * 2, [], place, *local, name="cut0")
    left = shift(high, "brick", 1)
    right = shift(low, "brick", -1)
    first, second = call(
        join_kernel, [(5, 8, 32, 128)] * 2, [], place, *local, left, right, name="join0"
    )
    below = shift(second, "grp", 1)
    above = shift(first, "grp", -1)
    fine = [FINE.shape(3)] * 3
    data0, saved0, packed1 = call(
        fine_down,
        [FINE.shape(5), (3, 24, 32, 128), (5, 8, 16, 128)],
        fine + [(5, 8, 16, 256)] + coef_shapes(FINE),
        place,
        first,
        second,
        below,
        above,
        name="down0",
    )
    left = shift(packed1, "brick", 1)
    right = shift(packed1, "brick", -1)
    up, down, centre = call(
        middle_cut,
        [(5, 5, 32, 128)] * 2 + [(5, 8, 32, 128)],
        [],
        place,
        packed1,
        left,
        right,
        name="cut1",
    )
    below = shift(up, "grp", 1)
    above = shift(down, "grp", -1)
    middle = [MIDDLE.shape(3)] * 3
    data1, saved1, packed2 = call(
        middle_down,
        [MIDDLE.shape(5), MIDDLE.shape(3), (5, 16, 128)],
        middle + [(5, 2, 32, 128), (5, 16, 256)] + coef_shapes(MIDDLE),
        place,
        centre,
        below,
        above,
        name="down1",
    )
    block = packed2[:, 6:10].reshape(1, 20, 128)
    parts = lax.all_to_all(
        jnp.broadcast_to(block, (lax.axis_size("brick"), 20, 128)), "brick", 0, 0
    )
    (column,) = call(column_kernel, [(5, 48, 128)], [], place, parts, name="column")
    parts = lax.all_to_all(
        jnp.broadcast_to(column[None], (lax.axis_size("grp"), 5, 48, 128)), "grp", 0, 0
    )
    coarse = [COARSE.shape(5)] + [COARSE.shape(3)] * 4 + coef_shapes(COARSE)
    last = [(5, 2, 24, 256), LAST.shape(5)] + [LAST.shape(3)] * 3 + coef_shapes(LAST)
    grown = [(3, 4, 48, 128), (3, 7, 32, 128), (3, 6, 32, 128)]
    (answer,) = call(
        climb,
        [(3, 16, 16, 128)],
        coarse + last + grown + middle + coef_shapes(MIDDLE) + fine + coef_shapes(FINE),
        place,
        parts,
        data1,
        saved1,
        data0,
        saved0,
        name="climb",
    )
    return answer


def solution(mesh):
    in_specs = (P(None, "grp", "brick", None), P("grp", "brick", None), P("grp", "brick", None))
    out_specs = P(None, "grp", "brick", None)
    return jax.shard_map(
        on_device, mesh=mesh, in_specs=in_specs, out_specs=out_specs, check_vma=False
    )
```

```python
import jax
import jax.numpy as jnp
from jax import lax
from jax.experimental import pallas as pl
from jax.experimental.pallas import tpu as pltpu
from jax.sharding import PartitionSpec as P

BETA = 1.0
THETA = 1.5
DELTA = 1.0
SIGMA = 1.5
LANES = 128
HALO = 8
NEAR = 10
SKIRT = 12
REACH = 5
F32 = jnp.float32


def rate_list():
    rates = [1.0 / SIGMA]
    for number in range(3):
        rates.append(1.0 / (2.0 * SIGMA - rates[-1]))
    return rates


RATES = rate_list()
STEPS = [(0.0, 1.0 / THETA)] + [
    (RATES[k] * RATES[k - 1], 2.0 * RATES[k] / DELTA) for k in (1, 2, 3)
]


def lane_of(shape):
    return lax.broadcasted_iota(jnp.int32, shape, len(shape) - 1)


def row_of(shape):
    return lax.broadcasted_iota(jnp.int32, shape, len(shape) - 2)


def ahead_y(v):
    return pltpu.roll(v, v.shape[0] - 1, 0)


def behind_y(v):
    return pltpu.roll(v, 1, 0)


def ahead_z(v):
    return pltpu.roll(v, LANES - 1, 1)


def behind_z(v):
    return pltpu.roll(v, 1, 1)


class Level:
    def __init__(self, scale, depth, rows, height):
        self.scale = scale
        self.depth = depth
        self.groups = LANES // depth
        self.rows = rows
        self.height = height

    def shape(self, *lead):
        return (*lead, self.rows + 2, self.height, LANES)

    def lanes(self):
        z = lane_of((self.height, LANES)) % self.depth
        return z == 0, z == self.depth - 1


def ghosts(level, ref, index=()):
    if level.groups == 1:
        return
    lane = lane_of((level.height, LANES))
    first = ref[(*index, 1)]
    last = ref[(*index, level.rows)]
    ref[(*index, 0)] = jnp.where(lane < level.depth, 0.0, pltpu.roll(last, level.depth, 1))
    ref[(*index, level.rows + 1)] = jnp.where(
        lane >= LANES - level.depth, 0.0, pltpu.roll(first, LANES - level.depth, 1)
    )


def setup(level, stiff, react, coef, inside, lo, hi):
    kx, ky, kym, kz, kzm, diag, inv = coef
    half = 0.5 * level.scale
    front, back = level.lanes()
    kx[lo - 1] = half * (stiff(lo - 1) + stiff(lo))

    def body(i, _):
        centre = stiff(i)
        xp = half * (centre + stiff(i + 1))
        xm = kx[i - 1]
        yp = half * (centre + ahead_y(centre))
        ym = behind_y(yp)
        zp = half * (centre + jnp.where(back, 0.0, ahead_z(centre)))
        zm = half * (centre + jnp.where(front, 0.0, behind_z(centre)))
        total = ((xp + xm) + (yp + ym)) + (zp + zm) + react(i)
        kx[i] = xp
        ky[i] = yp
        kym[i] = ym
        kz[i] = jnp.where(back, 0.0, zp)
        kzm[i] = jnp.where(front, 0.0, zm)
        diag[i] = total
        inv[i] = jnp.where(inside(i), 1.0 / (total + 2.0 * BETA * level.scale), 0.0)
        return 0

    lax.fori_loop(lo, hi, body, 0, unroll=2)


def begin(level, src, coef, state, direction, lo, hi):
    inv = coef[6]

    def body(i, _):
        scaled = inv[i] * (1.0 / THETA)
        for c in range(3):
            value = scaled * src[c, i]
            state[c, i] = value
            direction[c, i] = value
        return 0

    lax.fori_loop(lo, hi, body, 0, unroll=2)
    for c in range(3):
        ghosts(level, state, (c,))


def sweep(level, src, coef, state, lo, hi, emit):
    kx, ky, kym, kz, kzm, diag, inv = coef
    front, back = level.lanes()
    bulk = BETA * level.scale

    def spread(i):
        ux, uy, uz = state[0, i], state[1, i], state[2, i]
        return (
            (state[0, i + 1] - ux)
            + (ahead_y(uy) - uy)
            + (jnp.where(back, 0.0, ahead_z(uz)) - uz)
        ) * bulk

    def body(i, before):
        here = spread(i)
        for c in range(3):
            u = state[c, i]
            flux = kx[i] * state[c, i + 1] + kx[i - 1] * state[c, i - 1]
            flux = flux + (ky[i] * ahead_y(u) + kym[i] * behind_y(u))
            flux = flux + (kz[i] * ahead_z(u) + kzm[i] * behind_z(u))
            if c == 0:
                other = before
            elif c == 1:
                other = behind_y(here)
            else:
                other = jnp.where(front, bulk * u, behind_z(here))
            resid = src[c, i] - diag[i] * u + flux + (here - other)
            emit(i, c, u, resid)
        return here

    lax.fori_loop(lo, hi, body, spread(lo - 1), unroll=4)


def step(level, number, src, coef, state, fresh, direction, lo, hi):
    keep, gain = STEPS[number]
    inv = coef[6]

    def emit(i, c, u, resid):
        move = (gain * inv[i]) * resid
        if number > 0:
            move = move + keep * direction[c, i]
        direction[c, i] = move
        fresh[c, i] = u + move

    sweep(level, src, coef, state, lo, hi, emit)
    for c in range(3):
        ghosts(level, fresh, (c,))


def residual(level, src, coef, state, out, lo, hi):
    def emit(i, c, u, resid):
        out[c, i] = resid

    sweep(level, src, coef, state, lo, hi, emit)


def pick(rows, cols, rule, value):
    shape = (rows, cols)
    return jnp.where(rule(row_of(shape), lane_of(shape)), value, 0.0).astype(F32)


def mix(values, matrix):
    return jnp.dot(values, matrix, precision=lax.Precision.HIGHEST, preferred_element_type=F32)


def pairs(ref, index, start, count):
    return ref[(*index, pl.ds(start, count, 2))] + ref[(*index, pl.ds(start + 1, count, 2))]


def vmem(count):
    return [pl.BlockSpec(memory_space=pltpu.VMEM)] * count


def call(kernel, outs, scratch, *args, name):
    smem = pl.BlockSpec(memory_space=pltpu.SMEM)
    return pl.pallas_call(
        kernel,
        out_shape=[jax.ShapeDtypeStruct(s, F32) for s in outs],
        in_specs=[smem] + vmem(len(args) - 1),
        out_specs=vmem(len(outs)),
        scratch_shapes=[pltpu.VMEM(s, F32) for s in scratch],
        compiler_params=pltpu.CompilerParams(vmem_limit_bytes=28 * 2**20),
        name=name,
    )(*args)


def cut_kernel(f, k, r, own, lo, hi, sems):
    copies = [
        pltpu.make_async_copy(f, own.at[0:3], sems.at[0]),
        pltpu.make_async_copy(k, own.at[3], sems.at[1]),
        pltpu.make_async_copy(r, own.at[4], sems.at[2]),
    ]
    for copy in copies:
        copy.start()
    for copy in copies:
        copy.wait()
    lo[...] = own[:, :, 0:HALO]
    hi[...] = own[:, :, HALO : 2 * HALO]


def cut(f, k, r):
    block = (5, 16, 16, LANES)
    strip = (5, 16, HALO, LANES)
    return pl.pallas_call(
        cut_kernel,
        out_shape=[jax.ShapeDtypeStruct(shape, F32) for shape in (block, strip, strip)],
        in_specs=[pl.BlockSpec(memory_space=pl.ANY)] * 3,
        out_specs=vmem(3),
        scratch_shapes=[pltpu.SemaphoreType.DMA((3,))],
        compiler_params=pltpu.CompilerParams(vmem_limit_bytes=28 * 2**20),
        name="cut0",
    )(f, k, r)


def by_parity(place, act):
    odd = place[0] % 2

    @pl.when(odd == 0)
    def _():
        act(True)

    @pl.when(odd == 1)
    def _():
        act(False)


def join_kernel(place, own, lo, hi, near, far):
    def act(even):
        for half, out in enumerate((far, near) if even else (near, far)):
            rows = slice(8 * half, 8 * half + 8)
            for q in range(5):
                out[q, :, 0:8] = lo[q, rows]
                out[q, :, 8:24] = own[q, rows]
                out[q, :, 24:32] = hi[q, rows]

    by_parity(place, act)


FINE = Level(1.0, 128, 30, 32)
MIDDLE = Level(0.25, 64, 14, 32)
COARSE = Level(0.0625, 32, 8, 48)
LAST = Level(0.015625, 16, 2, 24)


def coef_shapes(level):
    return [level.shape()] * 7


def fine_inside(place):
    y = place[1] * 16 - HALO + row_of((32, LANES))
    fits = (y >= 0) & (y < place[3] * 16)

    def inside(i):
        x = place[0] * 16 + i - HALO
        return fits & (x >= 0) & (x < place[2] * 16)

    return inside


def fine_down(place, near, far, near_in, far_in, data, saved, packed, kept, s0, d0, t0, sums):
    coef = [kept.at[j] for j in range(7)]

    def act(even):
        order = (far_in, far, near, near_in) if even else (near_in, near, far, far_in)
        for number, part in enumerate(order):
            data[:, 8 * number : 8 * number + 8] = part[...]

    by_parity(place, act)
    inside = fine_inside(place)
    setup(FINE, lambda i: data[3, i], lambda i: data[4, i], coef, inside, 1, 31)
    begin(FINE, data, coef, s0, d0, 1, 31)
    step(FINE, 1, data, coef, s0, t0, d0, 2, 30)
    step(FINE, 2, data, coef, t0, s0, d0, 3, 29)
    step(FINE, 3, data, coef, s0, t0, d0, 4, 28)
    saved[...] = t0[:, 4:28]
    residual(FINE, data, coef, t0, d0, 6, 26)
    pair = s0.at[0]
    wide = sums
    for q in range(5):
        for t in range(16):
            half, i = divmod(t, 8)
            where = (q, i, slice(None), slice(half * LANES, half * LANES + LANES))
            if q >= 3:
                pair[t] = data[q, 2 * t] + data[q, 2 * t + 1]
            elif 3 <= t <= 12:
                pair[t] = d0[q, 2 * t] + d0[q, 2 * t + 1]
            else:
                wide[where] = jnp.zeros((16, LANES), F32)
                continue
            wide[where] = pairs(pair, (t,), 0, 16)
    matrix = pick(
        2 * LANES, LANES, lambda a, b: (a % LANES) // 2 + 64 * (a // LANES) == b, 0.125
    )
    packed[...] = mix(wide[...].reshape(5 * 8 * 16, 2 * LANES), matrix).reshape(5, 8, 16, LANES)


def middle_cut(place, own, left, right, near, far, centre):
    lane = lane_of((32, LANES))

    for q in range(5):
        for i in range(8):
            centre[q, i, 0:12] = left[q, i, 0:12]
            centre[q, i, 12:20] = own[q, i, 4:12]
            centre[q, i, 20:32] = right[q, i, 4:16]

    def act(even):
        up, down = (near, far) if even else (far, near)
        for q in range(5):
            for t in range(5):
                tail = pltpu.roll(centre[q, 7], 64, 1) if t == 0 else centre[q, t - 1]
                up[q, t] = jnp.where(lane < 64, centre[q, 2 + t], tail)
                head = pltpu.roll(centre[q, 0], 64, 1) if t == 4 else centre[q, 4 + t]
                down[q, t] = jnp.where(lane < 64, head, centre[q, 1 + t])

    by_parity(place, act)


def middle_inside(place):
    y = place[1] * 8 - SKIRT + row_of((32, LANES))
    fits = (y >= 0) & (y < place[3] * 8)
    x0 = place[0] * 8 - NEAR + 14 * (lane_of((32, LANES)) // 64)

    def inside(i):
        x = x0 + (i - 1)
        return fits & (x >= 0) & (x < place[2] * 8)

    return inside


def middle_join(centre, lo, hi, data):
    low = lane_of((32, LANES)) < 64
    for q in range(5):
        for i in range(14):
            if i < 5:
                a = lo[q, i]
            elif i < 10:
                a = pltpu.roll(lo[q, i - 5], 64, 1)
            else:
                a = centre[q, i - 6]
            if i < 4:
                b = centre[q, i]
            elif i < 9:
                b = pltpu.roll(hi[q, i - 4], 64, 1)
            else:
                b = hi[q, i - 9]
            data[q, i + 1] = jnp.where(low, a, b)
        ghosts(MIDDLE, data, (q,))


def middle_down(place, centre, near, far, data, saved, packed, kept, s1, d1, t1, pair, sums):
    coef = [kept.at[j] for j in range(7)]
    lane = lane_of((32, LANES))
    low = lane < 64
    by_parity(place, lambda even: middle_join(centre, *((far, near) if even else (near, far)), data))
    setup(MIDDLE, lambda i: data[3, i], lambda i: data[4, i], coef, middle_inside(place), 1, 15)
    begin(MIDDLE, data, coef, s1, d1, 1, 15)
    step(MIDDLE, 1, data, coef, s1, t1, d1, 1, 15)
    step(MIDDLE, 2, data, coef, t1, s1, d1, 1, 15)
    step(MIDDLE, 3, data, coef, s1, saved, d1, 1, 15)
    residual(MIDDLE, data, coef, saved, d1, 11, 15)
    residual(MIDDLE, data, coef, saved, d1, 1, 5)
    for q in range(5):
        from_, at = (d1, q) if q < 3 else (data, q)
        for m in range(2):
            a = from_[at, 11 + 2 * m] + from_[at, 12 + 2 * m]
            b = from_[at, 1 + 2 * m] + from_[at, 2 + 2 * m]
            pair[q, m] = jnp.where(low, a, b)
            sums[q, :, m * LANES : m * LANES + LANES] = pairs(pair, (q, m), 0, 16)
    matrix = pick(
        2 * LANES,
        LANES,
        lambda a, b: (a // LANES) * 32 + ((a % LANES) // 64) * 64 + (a % 64) // 2 == b,
        0.125,
    )
    packed[...] = mix(sums[...].reshape(5 * 16, 2 * LANES), matrix).reshape(5, 16, LANES)


def column_kernel(place, parts, out):
    zero = jnp.zeros((4, LANES), F32)
    for q in range(5):
        out[q, 0:2] = zero[0:2]
        out[q, 46:48] = zero[0:2]
    for d in range(2 * REACH + 1):
        at = place[1] + (d - REACH)
        valid = (at >= 0) & (at < place[3])
        safe = jnp.clip(at, 0, place[3] - 1)
        for q in range(5):
            block = parts[safe, q]
            out[q, 2 + 4 * d : 6 + 4 * d] = jnp.where(valid, block, zero)


def coarse_inside(place):
    sub = row_of((48, LANES))
    y = place[1] * 4 - 22 + sub
    fits = (y >= 0) & (y < place[3] * 4)
    return lambda i: fits


def last_inside(place):
    y = place[1] * 2 - 11 + row_of((24, LANES))
    fits = (y >= 0) & (y < place[3] * 2)
    return lambda i: fits


def climb(place, mine, other, data1, saved1, kept1, data0, saved0, kept0, out, *scratch):
    scratch = list(scratch)

    def take(count):
        got, scratch[:] = scratch[:count], scratch[count:]
        return got

    data2, s2, t2, d2, keep2 = take(5)
    coef2 = take(7)
    sums3 = take(1)[0]
    data3, s3, t3, d3 = take(4)
    coef3 = take(7)
    grown3, grown2, grown1 = take(3)
    s1, t1, d1 = take(3)
    s0, t0, d0 = take(3)
    coef1 = [kept1.at[j] for j in range(7)]
    coef0 = [kept0.at[j] for j in range(7)]

    group = lane_of((48, LANES)) // 32

    def act(even):
        order = (mine, other) if even else (other, mine)
        for q in range(5):
            for i in range(8):
                row = None
                for g in range(4):
                    block = order[i // 4][g, q]
                    shift = ((g - i % 4) * 32) % LANES
                    block = pltpu.roll(block, shift, 1) if shift else block
                    row = block if row is None else jnp.where(group == g, block, row)
                data2[q, i + 1] = row
            ghosts(COARSE, data2, (q,))

    by_parity(place, act)
    setup(COARSE, lambda i: data2[3, i], lambda i: data2[4, i], coef2, coarse_inside(place), 1, 9)
    begin(COARSE, data2, coef2, s2, d2, 1, 9)
    step(COARSE, 1, data2, coef2, s2, t2, d2, 1, 9)
    step(COARSE, 2, data2, coef2, t2, s2, d2, 1, 9)
    step(COARSE, 3, data2, coef2, s2, keep2, d2, 1, 9)
    residual(COARSE, data2, coef2, keep2, d2, 1, 9)

    pair = s2.at[0]
    for q in range(5):
        from_ = d2 if q < 3 else data2
        for t in range(4):
            half, i = divmod(t, 2)
            pair[t] = from_[q, 1 + 2 * t] + from_[q, 2 + 2 * t]
            sums3[q, i, :, half * LANES : half * LANES + LANES] = pairs(pair, (t,), 0, 24)
    matrix = pick(
        2 * LANES,
        LANES,
        lambda a, b: (2 * ((a % LANES) // 32) + a // LANES) * 16 + (a % 32) // 2 == b,
        0.125,
    )
    shrunk = mix(sums3[...].reshape(5 * 2 * 24, 2 * LANES), matrix).reshape(5, 2, 24, LANES)
    for q in range(5):
        for i in range(2):
            data3[q, i + 1] = shrunk[q, i]
        ghosts(LAST, data3, (q,))
    setup(LAST, lambda i: data3[3, i], lambda i: data3[4, i], coef3, last_inside(place), 1, 3)
    begin(LAST, data3, coef3, s3, d3, 1, 3)
    step(LAST, 1, data3, coef3, s3, t3, d3, 1, 3)
    step(LAST, 2, data3, coef3, t3, s3, d3, 1, 3)
    step(LAST, 3, data3, coef3, s3, t3, d3, 1, 3)

    matrix = pick(
        LANES,
        2 * LANES,
        lambda a, b: (2 * ((b % LANES) // 32) + b // LANES == a // 16) & ((b % 32) // 2 == a % 16),
        1.0,
    )
    flat = jnp.concatenate([t3[c, i + 1] for c in range(3) for i in range(2)], axis=0)
    wide = mix(flat, matrix)
    for c in range(3):
        for t in range(4):
            half, i = divmod(t, 2)
            at = (c * 2 + i) * 24
            piece = wide[at : at + 24, half * LANES : half * LANES + LANES]
            grown3[c, t, pl.ds(0, 24, 2)] = piece
            grown3[c, t, pl.ds(1, 24, 2)] = piece
            more = grown3[c, t]
            s2[c, 1 + 2 * t] = keep2[c, 1 + 2 * t] + more
            s2[c, 2 + 2 * t] = keep2[c, 2 + 2 * t] + more
        ghosts(COARSE, s2, (c,))
    step(COARSE, 0, data2, coef2, s2, t2, d2, 1, 9)
    step(COARSE, 1, data2, coef2, t2, s2, d2, 1, 9)
    step(COARSE, 2, data2, coef2, s2, t2, d2, 1, 9)
    step(COARSE, 3, data2, coef2, t2, s2, d2, 1, 9)

    matrix = pick(
        LANES,
        LANES,
        lambda a, b: (a < 64) & (b // 64 == a // 32) & ((b % 64) // 2 == a % 32),
        1.0,
    )
    small = lane_of((16, LANES)) < 32

    def window(c, x, slot):
        valid = (x >= 0) & (x < place[2] * 4)
        safe = jnp.clip(x, 0, place[2] * 4 - 1)
        value = s2[c, 1 + safe % 8, 16:32]
        value = pltpu.roll(value, (slot * 32 + LANES - (safe // 8) * 32) % LANES, 1)
        return jnp.where(valid, value, 0.0)

    pieces = []
    for c in range(3):
        for m in range(7):
            x = place[0] * 4 - 5 + m
            pieces.append(jnp.where(small, window(c, x, 0), window(c, x + 7, 1)))
    wide = mix(jnp.concatenate(pieces, axis=0), matrix)
    for c in range(3):
        for m in range(7):
            at = (c * 7 + m) * 16
            piece = wide[at : at + 16]
            grown2[c, m, pl.ds(0, 16, 2)] = piece
            grown2[c, m, pl.ds(1, 16, 2)] = piece
            more = grown2[c, m]
            s1[c, 1 + 2 * m] = saved1[c, 1 + 2 * m] + more
            s1[c, 2 + 2 * m] = saved1[c, 2 + 2 * m] + more
        ghosts(MIDDLE, s1, (c,))
    step(MIDDLE, 0, data1, coef1, s1, t1, d1, 1, 15)
    step(MIDDLE, 1, data1, coef1, t1, s1, d1, 1, 15)
    step(MIDDLE, 2, data1, coef1, s1, t1, d1, 1, 15)
    step(MIDDLE, 3, data1, coef1, t1, s1, d1, 1, 15)

    for half in range(2):
        matrix = pick(LANES, LANES, lambda a, b: a == 64 * half + b // 2, 1.0)
        rows = [9 + t for t in range(6)] if half == 0 else [1 + t for t in range(6)]
        flat = jnp.concatenate([s1[c, i, 8:24] for c in range(3) for i in rows], axis=0)
        wide = mix(flat, matrix)
        for c in range(3):
            for t in range(6):
                at = (c * 6 + t) * 16
                piece = wide[at : at + 16]
                grown1[c, t, pl.ds(0, 16, 2)] = piece
                grown1[c, t, pl.ds(1, 16, 2)] = piece
                more = grown1[c, t]
                row = 2 * (t + 6 * half)
                s0[c, 4 + row] = saved0[c, row] + more
                s0[c, 5 + row] = saved0[c, row + 1] + more
    step(FINE, 0, data0, coef0, s0, t0, d0, 5, 27)
    step(FINE, 1, data0, coef0, t0, s0, d0, 6, 26)
    step(FINE, 2, data0, coef0, s0, t0, d0, 7, 25)
    keep, gain = STEPS[3]

    def emit(i, c, u, resid):
        move = (gain * coef0[6][i]) * resid + keep * d0[c, i]
        out[c, i - 8] = (u + move)[8:24]

    sweep(FINE, data0, coef0, t0, 8, 24, emit)


def shift(value, axis, by):
    count = lax.axis_size(axis)
    return lax.ppermute(
        value, axis, [(i, i + by) for i in range(count) if 0 <= i + by < count]
    )


def swap(value, first):
    count = lax.axis_size("grp")
    ends = [(i, i + 1) for i in range(first, count - 1, 2)]
    return lax.ppermute(value, "grp", ends + [(b, a) for a, b in ends])


def on_device(right_side, stiffness, reaction):
    bricks = lax.axis_size("brick")
    count = lax.axis_size("grp")
    place = jnp.stack(
        [lax.axis_index("grp"), lax.axis_index("brick"), jnp.int32(count), jnp.int32(bricks)]
    ).astype(jnp.int32)
    own, low, high = cut(right_side, stiffness, reaction)
    left = shift(high, "brick", 1)
    right = shift(low, "brick", -1)
    near, far = call(join_kernel, [(5, 8, 32, 128)] * 2, [], place, own, left, right, name="join0")
    far_in = swap(far, 1)
    near_in = swap(near, 0)
    fine = [FINE.shape(3)] * 3
    data0, saved0, packed1, kept0 = call(
        fine_down,
        [FINE.shape(5), (3, 24, 32, 128), (5, 8, 16, 128), FINE.shape(7)],
        fine + [(5, 8, 16, 256)],
        place,
        near,
        far,
        near_in,
        far_in,
        name="down0",
    )
    left = shift(packed1, "brick", 1)
    right = shift(packed1, "brick", -1)
    near, far, centre = call(
        middle_cut,
        [(5, 5, 32, 128)] * 2 + [(5, 8, 32, 128)],
        [],
        place,
        packed1,
        left,
        right,
        name="cut1",
    )
    far_in = swap(far, 1)
    near_in = swap(near, 0)
    middle = [MIDDLE.shape(3)] * 3
    data1, saved1, packed2, kept1 = call(
        middle_down,
        [MIDDLE.shape(5), MIDDLE.shape(3), (5, 16, 128), MIDDLE.shape(7)],
        middle + [(5, 2, 32, 128), (5, 16, 256)],
        place,
        centre,
        near_in,
        far_in,
        name="down1",
    )
    block = packed2[:, 6:10]
    parts = lax.all_to_all(jnp.broadcast_to(block[None], (bricks, 5, 4, 128)), "brick", 0, 0)
    (column,) = call(column_kernel, [(5, 48, 128)], [], place, parts, name="column")
    mine = lax.all_to_all(
        jnp.broadcast_to(column[None], (count // 2, 5, 48, 128)),
        "grp",
        0,
        0,
        axis_index_groups=[list(range(core, count, 2)) for core in range(2)],
    )
    other = swap(mine, 0)
    coarse = [COARSE.shape(5)] + [COARSE.shape(3)] * 4 + coef_shapes(COARSE)
    last = [(5, 2, 24, 256), LAST.shape(5)] + [LAST.shape(3)] * 3 + coef_shapes(LAST)
    grown = [(3, 4, 48, 128), (3, 7, 32, 128), (3, 6, 32, 128)]
    (answer,) = call(
        climb,
        [(3, 16, 16, 128)],
        coarse + last + grown + middle + fine,
        place,
        mine,
        other,
        data1,
        saved1,
        kept1,
        data0,
        saved0,
        kept0,
        name="climb",
    )
    return answer


def solution(mesh):
    in_specs = (P(None, "grp", "brick", None), P("grp", "brick", None), P("grp", "brick", None))
    out_specs = P(None, "grp", "brick", None)
    return jax.shard_map(
        on_device, mesh=mesh, in_specs=in_specs, out_specs=out_specs, check_vma=False
    )
```

```python
import jax
import jax.numpy as jnp
from jax import lax
from jax.experimental import pallas as pl
from jax.experimental.pallas import tpu as pltpu
from jax.sharding import PartitionSpec as P

BETA = 1.0
THETA = 1.5
DELTA = 1.0
SIGMA = 1.5
LANES = 128
HALO = 8
NEAR = 10
SKIRT = 12
REACH = 5
F32 = jnp.float32


def rate_list():
    rates = [1.0 / SIGMA]
    for number in range(3):
        rates.append(1.0 / (2.0 * SIGMA - rates[-1]))
    return rates


RATES = rate_list()
STEPS = [(0.0, 1.0 / THETA)] + [
    (RATES[k] * RATES[k - 1], 2.0 * RATES[k] / DELTA) for k in (1, 2, 3)
]


def lane_of(shape):
    return lax.broadcasted_iota(jnp.int32, shape, len(shape) - 1)


def row_of(shape):
    return lax.broadcasted_iota(jnp.int32, shape, len(shape) - 2)


def ahead_y(v):
    return pltpu.roll(v, v.shape[0] - 1, 0)


def behind_y(v):
    return pltpu.roll(v, 1, 0)


def ahead_z(v):
    return pltpu.roll(v, LANES - 1, 1)


def behind_z(v):
    return pltpu.roll(v, 1, 1)


class Level:
    def __init__(self, scale, depth, rows, height):
        self.scale = scale
        self.depth = depth
        self.groups = LANES // depth
        self.rows = rows
        self.height = height

    def shape(self, *lead):
        return (*lead, self.rows + 2, self.height, LANES)

    def lanes(self):
        z = lane_of((self.height, LANES)) % self.depth
        return z == 0, z == self.depth - 1


def ghosts(level, ref, index=()):
    if level.groups == 1:
        return
    lane = lane_of((level.height, LANES))
    first = ref[(*index, 1)]
    last = ref[(*index, level.rows)]
    ref[(*index, 0)] = jnp.where(lane < level.depth, 0.0, pltpu.roll(last, level.depth, 1))
    ref[(*index, level.rows + 1)] = jnp.where(
        lane >= LANES - level.depth, 0.0, pltpu.roll(first, LANES - level.depth, 1)
    )


def setup(level, stiff, react, coef, inside, lo, hi):
    kx, ky, kym, kz, kzm, diag, inv = coef
    half = 0.5 * level.scale
    front, back = level.lanes()
    kx[lo - 1] = half * (stiff(lo - 1) + stiff(lo))

    def body(i, _):
        centre = stiff(i)
        xp = half * (centre + stiff(i + 1))
        xm = kx[i - 1]
        yp = half * (centre + ahead_y(centre))
        ym = behind_y(yp)
        zp = half * (centre + jnp.where(back, 0.0, ahead_z(centre)))
        zm = half * (centre + jnp.where(front, 0.0, behind_z(centre)))
        total = ((xp + xm) + (yp + ym)) + (zp + zm) + react(i)
        kx[i] = xp
        ky[i] = yp
        kym[i] = ym
        kz[i] = jnp.where(back, 0.0, zp)
        kzm[i] = jnp.where(front, 0.0, zm)
        diag[i] = total
        inv[i] = jnp.where(inside(i), 1.0 / (total + 2.0 * BETA * level.scale), 0.0)
        return 0

    lax.fori_loop(lo, hi, body, 0, unroll=2)


def begin(level, src, coef, state, direction, lo, hi):
    inv = coef[6]

    def body(i, _):
        scaled = inv[i] * (1.0 / THETA)
        for c in range(3):
            value = scaled * src[c, i]
            state[c, i] = value
            direction[c, i] = value
        return 0

    lax.fori_loop(lo, hi, body, 0, unroll=2)
    for c in range(3):
        ghosts(level, state, (c,))


def sweep(level, src, coef, state, lo, hi, emit):
    kx, ky, kym, kz, kzm, diag, inv = coef
    front, back = level.lanes()
    bulk = BETA * level.scale

    def spread(i):
        ux, uy, uz = state[0, i], state[1, i], state[2, i]
        return (
            (state[0, i + 1] - ux)
            + (ahead_y(uy) - uy)
            + (jnp.where(back, 0.0, ahead_z(uz)) - uz)
        ) * bulk

    def body(i, before):
        here = spread(i)
        for c in range(3):
            u = state[c, i]
            flux = kx[i] * state[c, i + 1] + kx[i - 1] * state[c, i - 1]
            flux = flux + (ky[i] * ahead_y(u) + kym[i] * behind_y(u))
            flux = flux + (kz[i] * ahead_z(u) + kzm[i] * behind_z(u))
            if c == 0:
                other = before
            elif c == 1:
                other = behind_y(here)
            else:
                other = jnp.where(front, bulk * u, behind_z(here))
            resid = src[c, i] - diag[i] * u + flux + (here - other)
            emit(i, c, u, resid)
        return here

    lax.fori_loop(lo, hi, body, spread(lo - 1), unroll=4)


def step(level, number, src, coef, state, fresh, direction, lo, hi):
    keep, gain = STEPS[number]
    inv = coef[6]

    def emit(i, c, u, resid):
        move = (gain * inv[i]) * resid
        if number > 0:
            move = move + keep * direction[c, i]
        direction[c, i] = move
        fresh[c, i] = u + move

    sweep(level, src, coef, state, lo, hi, emit)
    for c in range(3):
        ghosts(level, fresh, (c,))


def residual(level, src, coef, state, out, lo, hi):
    def emit(i, c, u, resid):
        out[c, i] = resid

    sweep(level, src, coef, state, lo, hi, emit)


def pick(rows, cols, rule, value):
    shape = (rows, cols)
    return jnp.where(rule(row_of(shape), lane_of(shape)), value, 0.0).astype(F32)


def mix(values, matrix):
    return jnp.dot(values, matrix, precision=lax.Precision.HIGHEST, preferred_element_type=F32)


def pairs(ref, index, start, count):
    return ref[(*index, pl.ds(start, count, 2))] + ref[(*index, pl.ds(start + 1, count, 2))]


def vmem(count):
    return [pl.BlockSpec(memory_space=pltpu.VMEM)] * count


def call(kernel, outs, scratch, *args, name, aliases={}):
    smem = pl.BlockSpec(memory_space=pltpu.SMEM)
    return pl.pallas_call(
        kernel,
        out_shape=[jax.ShapeDtypeStruct(s, F32) for s in outs],
        in_specs=[smem] + vmem(len(args) - 1),
        out_specs=vmem(len(outs)),
        scratch_shapes=[pltpu.VMEM(s, F32) for s in scratch],
        compiler_params=pltpu.CompilerParams(vmem_limit_bytes=28 * 2**20),
        input_output_aliases=aliases,
        name=name,
    )(*args)


def by_parity(index, act):
    odd = index % 2

    @pl.when(odd == 0)
    def _():
        act(True)

    @pl.when(odd == 1)
    def _():
        act(False)


def cut_kernel(place, f, k, r, own, first, second, sems):
    copies = [
        pltpu.make_async_copy(f, own.at[0:3], sems.at[0]),
        pltpu.make_async_copy(k, own.at[3], sems.at[1]),
        pltpu.make_async_copy(r, own.at[4], sems.at[2]),
    ]
    for copy in copies:
        copy.start()
    for copy in copies:
        copy.wait()

    def act(even):
        lo, hi = (second, first) if even else (first, second)
        lo[...] = own[:, :, 0:HALO]
        hi[...] = own[:, :, HALO : 2 * HALO]

    by_parity(place[1], act)


def cut(place, f, k, r):
    block = (5, 16, 16, LANES)
    strip = (5, 16, HALO, LANES)
    return pl.pallas_call(
        cut_kernel,
        out_shape=[jax.ShapeDtypeStruct(shape, F32) for shape in (block, strip, strip)],
        in_specs=[pl.BlockSpec(memory_space=pltpu.SMEM)]
        + [pl.BlockSpec(memory_space=pltpu.HBM)] * 3,
        out_specs=vmem(3),
        scratch_shapes=[pltpu.SemaphoreType.DMA((3,))],
        compiler_params=pltpu.CompilerParams(vmem_limit_bytes=28 * 2**20),
        name="cut0",
    )(place, f, k, r)


def join_kernel(place, own, first, second, near, far):
    def sides(swapped):
        lo, hi = (second, first) if swapped else (first, second)

        def act(even):
            for half, out in enumerate((far, near) if even else (near, far)):
                rows = slice(8 * half, 8 * half + 8)
                for q in range(5):
                    out[q, :, 0:8] = lo[q, rows]
                    out[q, :, 8:24] = own[q, rows]
                    out[q, :, 24:32] = hi[q, rows]

        by_parity(place[0], act)

    by_parity(place[1], sides)


FINE = Level(1.0, 128, 30, 32)
FINE_UP = Level(1.0, 128, 22, 24)
MIDDLE = Level(0.25, 64, 14, 32)
MIDDLE_UP = Level(0.25, 64, 10, 24)
COARSE = Level(0.0625, 32, 8, 48)
COARSE_UP = Level(0.0625, 32, 8, 32)
LAST = Level(0.015625, 16, 2, 24)


def coef_shapes(level):
    return [level.shape()] * 7


def fine_inside(place):
    y = place[1] * 16 - HALO + row_of((32, LANES))
    fits = (y >= 0) & (y < place[3] * 16)

    def inside(i):
        x = place[0] * 16 + i - HALO
        return fits & (x >= 0) & (x < place[2] * 16)

    return inside


def fine_inner(place, near, far, data, kept, s0, d0, t0):
    coef = [kept.at[j] for j in range(7)]

    def act(even):
        for number, part in enumerate((far, near) if even else (near, far)):
            data[:, 8 * number + 8 : 8 * number + 16] = part[...]

    by_parity(place[0], act)
    setup(FINE, lambda i: data[3, i], lambda i: data[4, i], coef, fine_inside(place), 9, 23)
    begin(FINE, data, coef, s0, d0, 9, 23)
    step(FINE, 1, data, coef, s0, t0, d0, 10, 22)
    step(FINE, 2, data, coef, t0, s0, d0, 11, 21)
    step(FINE, 3, data, coef, s0, t0, d0, 12, 20)


def fine_outer(place, near, far, *refs):
    data, kept, s0, d0, t0, saved, packed, first, second, sums, resid = refs[5:]
    coef = [kept.at[j] for j in range(7)]

    def act(even):
        lo, hi = (far, near) if even else (near, far)
        data[:, 0:8] = lo[...]
        data[:, 24:32] = hi[...]

    by_parity(place[0], act)
    inside = fine_inside(place)
    for lo, hi in ((1, 9), (23, 31)):
        setup(FINE, lambda i: data[3, i], lambda i: data[4, i], coef, inside, lo, hi)
        begin(FINE, data, coef, s0, d0, lo, hi)
    for lo, hi in ((2, 10), (22, 30)):
        step(FINE, 1, data, coef, s0, t0, d0, lo, hi)
    for lo, hi in ((3, 11), (21, 29)):
        step(FINE, 2, data, coef, t0, s0, d0, lo, hi)
    for lo, hi in ((4, 12), (20, 28)):
        step(FINE, 3, data, coef, s0, t0, d0, lo, hi)
    saved[...] = t0[:, 4:28, 4:28]
    residual(FINE, data, coef, t0, resid, 6, 26)
    pair = s0.at[0]
    wide = sums
    for q in range(5):
        for t in range(16):
            half, i = divmod(t, 8)
            where = (q, i, slice(None), slice(half * LANES, half * LANES + LANES))
            if q >= 3:
                pair[t] = data[q, 2 * t] + data[q, 2 * t + 1]
            elif 3 <= t <= 12:
                pair[t] = resid[q, 2 * t] + resid[q, 2 * t + 1]
            else:
                wide[where] = jnp.zeros((16, LANES), F32)
                continue
            wide[where] = pairs(pair, (t,), 0, 16)
    matrix = pick(
        2 * LANES, LANES, lambda a, b: (a % LANES) // 2 + 64 * (a // LANES) == b, 0.125
    )
    packed[...] = mix(wide[...].reshape(5 * 8 * 16, 2 * LANES), matrix).reshape(5, 8, 16, LANES)

    def send(even):
        left, right = (second, first) if even else (first, second)
        for q in range(5):
            skip = 1 if q < 3 else 2
            left[q] = packed[q, :, 4 + skip : 12 + skip]
            right[q] = packed[q, :, 4 - skip : 12 - skip]

    by_parity(place[1], send)


def fine_trim(place, data, kept, data_up, kept_up):
    for q in range(3):
        data_up[q] = data[q, 4:28, 4:28]
    for j in range(7):
        kept_up[j] = kept[j, 4:28, 4:28]


def middle_cut(place, own, first, second, near, far, centre):
    low = lane_of((32, LANES)) < 64
    zero = jnp.zeros((4, LANES), F32)

    def sides(even):
        left, right = (second, first) if even else (first, second)
        for q in range(5):
            skip = 1 if q < 3 else 2
            for i in range(8):
                centre[q, i, 0 : 4 - skip] = zero[0 : 4 - skip]
                centre[q, i, 4 - skip : 12 - skip] = left[q, i]
                centre[q, i, 12 - skip : 20 + skip] = own[q, i, 4 - skip : 12 + skip]
                centre[q, i, 20 + skip : 28 + skip] = right[q, i]
                centre[q, i, 28 + skip : 32] = zero[0 : 4 - skip]

    by_parity(place[1], sides)

    def at(q, x, half):
        value = centre[q, x + 4 if x < 4 else x - 4]
        return value if (x >= 4) == (half == 1) else pltpu.roll(value, 64, 1)

    def act(even):
        up, down = (near, far) if even else (far, near)
        for q in range(5):
            skip = 1 if q < 3 else 2
            for t in range(4):
                up[q, t] = jnp.where(low, at(q, t - skip, 0), at(q, t - skip + 4, 1))
                down[q, t] = jnp.where(low, at(q, t + skip, 0), at(q, t + skip + 4, 1))

    by_parity(place[0], act)


def middle_inside(place):
    y = place[1] * 8 - SKIRT + row_of((32, LANES))
    fits = (y >= 0) & (y < place[3] * 8)
    x0 = place[0] * 8 - NEAR + 14 * (lane_of((32, LANES)) // 64)

    def inside(i):
        x = x0 + (i - 1)
        return fits & (x >= 0) & (x < place[2] * 8)

    return inside


def middle_join(centre, lo, hi, data):
    low = lane_of((32, LANES)) < 64
    zero = jnp.zeros((32, LANES), F32)

    def moved(ref, q, t, half):
        value = ref[q, t % 4]
        return value if t // 4 == half else pltpu.roll(value, 64, 1)

    for q in range(5):
        skip = 1 if q < 3 else 2
        for i in range(14):
            t = i - (2 - skip)
            if t < 0:
                a = zero
            elif t < 8:
                a = moved(lo, q, t, 0)
            else:
                a = centre[q, i - 6]
            t = i - (4 + skip)
            if t < 0:
                b = centre[q, i]
            elif t < 8:
                b = moved(hi, q, t, 1)
            else:
                b = zero
            data[q, i + 1] = jnp.where(low, a, b)
        ghosts(MIDDLE, data, (q,))


def middle_down(place, centre, near, far, data, saved, packed, kept, s1, d1, t1, pair, sums):
    coef = [kept.at[j] for j in range(7)]
    lane = lane_of((32, LANES))
    low = lane < 64
    by_parity(
        place[0],
        lambda even: middle_join(centre, *((far, near) if even else (near, far)), data),
    )
    setup(MIDDLE, lambda i: data[3, i], lambda i: data[4, i], coef, middle_inside(place), 1, 15)
    begin(MIDDLE, data, coef, s1, d1, 1, 15)
    step(MIDDLE, 1, data, coef, s1, t1, d1, 1, 15)
    step(MIDDLE, 2, data, coef, t1, s1, d1, 1, 15)
    step(MIDDLE, 3, data, coef, s1, saved, d1, 1, 15)
    residual(MIDDLE, data, coef, saved, d1, 11, 15)
    residual(MIDDLE, data, coef, saved, d1, 1, 5)
    for q in range(5):
        from_, at = (d1, q) if q < 3 else (data, q)
        for m in range(2):
            a = from_[at, 11 + 2 * m] + from_[at, 12 + 2 * m]
            b = from_[at, 1 + 2 * m] + from_[at, 2 + 2 * m]
            pair[q, m] = jnp.where(low, a, b)
            sums[q, :, m * LANES : m * LANES + LANES] = pairs(pair, (q, m), 0, 16)
    matrix = pick(
        2 * LANES,
        LANES,
        lambda a, b: (a // LANES) * 32 + ((a % LANES) // 64) * 64 + (a % 64) // 2 == b,
        0.125,
    )
    packed[...] = mix(sums[...].reshape(5 * 16, 2 * LANES), matrix).reshape(5, 16, LANES)


def middle_trim(place, data, saved, kept, data_up, saved_up, kept_up):
    low = lane_of((24, LANES)) < 64
    groups = [(data, data_up, 3), (saved, saved_up, 3), (kept, kept_up, 7)]
    for old, new, count in groups:
        for q in range(count):
            for j in range(12):
                new[q, j] = jnp.where(low, old[q, 4 + j, 2:26], old[q, j, 2:26])


def column_kernel(place, parts, out):
    zero = jnp.zeros((4, LANES), F32)
    for q in range(5):
        out[q, 0:2] = zero[0:2]
        out[q, 46:48] = zero[0:2]
    for d in range(2 * REACH + 1):
        at = place[1] + (d - REACH)
        valid = (at >= 0) & (at < place[3])
        safe = jnp.clip(at, 0, place[3] - 1)
        for q in range(5):
            block = parts[safe, q]
            out[q, 2 + 4 * d : 6 + 4 * d] = jnp.where(valid, block, zero)


def coarse_inside(place):
    sub = row_of((48, LANES))
    y = place[1] * 4 - 22 + sub
    fits = (y >= 0) & (y < place[3] * 4)
    return lambda i: fits


def last_inside(place):
    y = place[1] * 2 - 11 + row_of((24, LANES))
    fits = (y >= 0) & (y < place[3] * 2)
    return lambda i: fits


def climb(place, mine, other, data1, saved1, kept1, data0, saved0, kept0, out, *scratch):
    scratch = list(scratch)

    def take(count):
        got, scratch[:] = scratch[:count], scratch[count:]
        return got

    data2, s2, t2, d2, keep2 = take(5)
    coef2 = take(7)
    sums3 = take(1)[0]
    data3, s3, t3, d3 = take(4)
    coef3 = take(7)
    grown3, grown2, grown1 = take(3)
    s1, t1, d1 = take(3)
    s0, t0, d0 = take(3)
    coef1 = [kept1.at[j] for j in range(7)]
    coef0 = [kept0.at[j] for j in range(7)]

    group = lane_of((48, LANES)) // 32

    def act(even):
        order = (mine, other) if even else (other, mine)
        for q in range(5):
            for i in range(8):
                row = None
                for g in range(4):
                    block = order[i // 4][g, q]
                    shift = ((g - i % 4) * 32) % LANES
                    block = pltpu.roll(block, shift, 1) if shift else block
                    row = block if row is None else jnp.where(group == g, block, row)
                data2[q, i + 1] = row
            ghosts(COARSE, data2, (q,))

    by_parity(place[0], act)
    setup(COARSE, lambda i: data2[3, i], lambda i: data2[4, i], coef2, coarse_inside(place), 1, 9)
    begin(COARSE, data2, coef2, s2, d2, 1, 9)
    step(COARSE, 1, data2, coef2, s2, t2, d2, 1, 9)
    step(COARSE, 2, data2, coef2, t2, s2, d2, 1, 9)
    step(COARSE, 3, data2, coef2, s2, keep2, d2, 1, 9)
    residual(COARSE, data2, coef2, keep2, d2, 1, 9)

    pair = s2.at[0]
    for q in range(5):
        from_ = d2 if q < 3 else data2
        for t in range(4):
            half, i = divmod(t, 2)
            pair[t] = from_[q, 1 + 2 * t] + from_[q, 2 + 2 * t]
            sums3[q, i, :, half * LANES : half * LANES + LANES] = pairs(pair, (t,), 0, 24)
    matrix = pick(
        2 * LANES,
        LANES,
        lambda a, b: (2 * ((a % LANES) // 32) + a // LANES) * 16 + (a % 32) // 2 == b,
        0.125,
    )
    shrunk = mix(sums3[...].reshape(5 * 2 * 24, 2 * LANES), matrix).reshape(5, 2, 24, LANES)
    for q in range(5):
        for i in range(2):
            data3[q, i + 1] = shrunk[q, i]
        ghosts(LAST, data3, (q,))
    setup(LAST, lambda i: data3[3, i], lambda i: data3[4, i], coef3, last_inside(place), 1, 3)
    begin(LAST, data3, coef3, s3, d3, 1, 3)
    step(LAST, 1, data3, coef3, s3, t3, d3, 1, 3)
    step(LAST, 2, data3, coef3, t3, s3, d3, 1, 3)
    step(LAST, 3, data3, coef3, s3, t3, d3, 1, 3)

    data2u, s2u, t2u, d2u = (ref.at[:, :, 8:40] for ref in (data2, s2, t2, d2))
    coef2u = [ref.at[:, 8:40] for ref in coef2]
    matrix = pick(
        LANES,
        2 * LANES,
        lambda a, b: (2 * ((b % LANES) // 32) + b // LANES == a // 16) & ((b % 32) // 2 == a % 16),
        1.0,
    )
    flat = jnp.concatenate([t3[c, i + 1] for c in range(3) for i in range(2)], axis=0)
    wide = mix(flat, matrix)
    for c in range(3):
        for t in range(4):
            half, i = divmod(t, 2)
            at = (c * 2 + i) * 24
            piece = wide[at : at + 24, half * LANES : half * LANES + LANES]
            grown3[c, t, pl.ds(0, 24, 2)] = piece
            grown3[c, t, pl.ds(1, 24, 2)] = piece
            more = grown3[c, t, 8:40]
            s2u[c, 1 + 2 * t] = keep2[c, 1 + 2 * t, 8:40] + more
            s2u[c, 2 + 2 * t] = keep2[c, 2 + 2 * t, 8:40] + more
        ghosts(COARSE_UP, s2u, (c,))
    step(COARSE_UP, 0, data2u, coef2u, s2u, t2u, d2u, 1, 9)
    step(COARSE_UP, 1, data2u, coef2u, t2u, s2u, d2u, 1, 9)
    step(COARSE_UP, 2, data2u, coef2u, s2u, t2u, d2u, 1, 9)
    step(COARSE_UP, 3, data2u, coef2u, t2u, s2u, d2u, 1, 9)

    matrix = pick(
        LANES,
        LANES,
        lambda a, b: (a < 64) & (b // 64 == a // 32) & ((b % 64) // 2 == a % 32),
        1.0,
    )
    small = lane_of((16, LANES)) < 32

    def window(c, x, slot):
        valid = (x >= 0) & (x < place[2] * 4)
        safe = jnp.clip(x, 0, place[2] * 4 - 1)
        value = s2[c, 1 + safe % 8, 16:32]
        value = pltpu.roll(value, (slot * 32 + LANES - (safe // 8) * 32) % LANES, 1)
        return jnp.where(valid, value, 0.0)

    pieces = []
    for c in range(3):
        for m in range(5):
            x = place[0] * 4 - 3 + m
            pieces.append(jnp.where(small, window(c, x, 0), window(c, x + 5, 1)))
    wide = mix(jnp.concatenate(pieces, axis=0), matrix)
    for c in range(3):
        for m in range(5):
            at = (c * 5 + m) * 16
            piece = wide[at : at + 16]
            grown2[c, m, pl.ds(0, 16, 2)] = piece
            grown2[c, m, pl.ds(1, 16, 2)] = piece
            more = grown2[c, m, 2:26]
            s1[c, 1 + 2 * m] = saved1[c, 1 + 2 * m] + more
            s1[c, 2 + 2 * m] = saved1[c, 2 + 2 * m] + more
        ghosts(MIDDLE_UP, s1, (c,))
    step(MIDDLE_UP, 0, data1, coef1, s1, t1, d1, 1, 11)
    step(MIDDLE_UP, 1, data1, coef1, t1, s1, d1, 1, 11)
    step(MIDDLE_UP, 2, data1, coef1, s1, t1, d1, 1, 11)
    step(MIDDLE_UP, 3, data1, coef1, t1, s1, d1, 1, 11)

    for half in range(2):
        matrix = pick(LANES, LANES, lambda a, b: a == 64 * half + b // 2, 1.0)
        rows = [5 + t for t in range(6)] if half == 0 else [1 + t for t in range(6)]
        flat = jnp.concatenate([s1[c, i, 8:24] for c in range(3) for i in rows], axis=0)
        wide = mix(flat, matrix)
        for c in range(3):
            for t in range(6):
                at = (c * 6 + t) * 16
                piece = wide[at : at + 16]
                grown1[c, t, pl.ds(0, 16, 2)] = piece
                grown1[c, t, pl.ds(1, 16, 2)] = piece
                more = grown1[c, t, 0:24]
                row = 2 * (t + 6 * half)
                s0[c, row] = saved0[c, row] + more
                s0[c, row + 1] = saved0[c, row + 1] + more
    step(FINE_UP, 0, data0, coef0, s0, t0, d0, 1, 23)
    step(FINE_UP, 1, data0, coef0, t0, s0, d0, 2, 22)
    step(FINE_UP, 2, data0, coef0, s0, t0, d0, 3, 21)
    keep, gain = STEPS[3]

    def emit(i, c, u, resid):
        move = (gain * coef0[6][i]) * resid + keep * d0[c, i]
        out[c, i - 4] = (u + move)[4:20]

    sweep(FINE_UP, data0, coef0, t0, 4, 20, emit)


def swap(value, axis, first):
    count = lax.axis_size(axis)
    ends = [(i, i + 1) for i in range(first, count - 1, 2)]
    return lax.ppermute(value, axis, ends + [(b, a) for a, b in ends])


def on_device(right_side, stiffness, reaction):
    bricks = lax.axis_size("brick")
    count = lax.axis_size("grp")
    place = jnp.stack(
        [lax.axis_index("grp"), lax.axis_index("brick"), jnp.int32(count), jnp.int32(bricks)]
    ).astype(jnp.int32)
    own, first, second = cut(place, right_side, stiffness, reaction)
    first = swap(first, "brick", 0)
    second = swap(second, "brick", 1)
    near, far = call(
        join_kernel, [(5, 8, 32, 128)] * 2, [], place, own, first, second, name="join0"
    )
    far_in = swap(far, "grp", 1)
    near_in = swap(near, "grp", 0)
    states = [FINE.shape(5), FINE.shape(7)] + [FINE.shape(3)] * 3
    inner = call(fine_inner, states, [], place, near, far, name="inner0")
    data0, kept0, _, _, _, saved0, packed1, first, second = call(
        fine_outer,
        states + [(3, 24, 24, 128), (5, 8, 16, 128)] + [(5, 8, 8, 128)] * 2,
        [(5, 8, 16, 256), FINE.shape(3)],
        place,
        near_in,
        far_in,
        *inner,
        name="outer0",
        aliases={3 + j: j for j in range(5)},
    )
    first = swap(first, "brick", 0)
    second = swap(second, "brick", 1)
    data0, kept0 = call(
        fine_trim, [FINE_UP.shape(3), FINE_UP.shape(7)], [], place, data0, kept0, name="trim0"
    )
    near, far, centre = call(
        middle_cut,
        [(5, 4, 32, 128)] * 2 + [(5, 8, 32, 128)],
        [],
        place,
        packed1,
        first,
        second,
        name="cut1",
    )
    far_in = swap(far, "grp", 1)
    near_in = swap(near, "grp", 0)
    data1, saved1, packed2, kept1 = call(
        middle_down,
        [MIDDLE.shape(5), MIDDLE.shape(3), (5, 16, 128), MIDDLE.shape(7)],
        [MIDDLE.shape(3)] * 3 + [(5, 2, 32, 128), (5, 16, 256)],
        place,
        centre,
        near_in,
        far_in,
        name="down1",
    )
    block = packed2[:, 6:10]
    parts = lax.all_to_all(jnp.broadcast_to(block[None], (bricks, 5, 4, 128)), "brick", 0, 0)
    (column,) = call(column_kernel, [(5, 48, 128)], [], place, parts, name="column")
    mine = lax.all_to_all(
        jnp.broadcast_to(column[None], (count // 2, 5, 48, 128)),
        "grp",
        0,
        0,
        axis_index_groups=[list(range(core, count, 2)) for core in range(2)],
    )
    other = swap(mine, "grp", 0)
    data1, saved1, kept1 = call(
        middle_trim,
        [MIDDLE_UP.shape(3)] * 2 + [MIDDLE_UP.shape(7)],
        [],
        place,
        data1,
        saved1,
        kept1,
        name="trim1",
    )
    coarse = [COARSE.shape(5)] + [COARSE.shape(3)] * 4 + coef_shapes(COARSE)
    last = [(5, 2, 24, 256), LAST.shape(5)] + [LAST.shape(3)] * 3 + coef_shapes(LAST)
    grown = [(3, 4, 48, 128), (3, 5, 32, 128), (3, 6, 32, 128)]
    (answer,) = call(
        climb,
        [(3, 16, 16, 128)],
        coarse + last + grown + [MIDDLE_UP.shape(3)] * 3 + [FINE_UP.shape(3)] * 3,
        place,
        mine,
        other,
        data1,
        saved1,
        kept1,
        data0,
        saved0,
        kept0,
        name="climb",
    )
    return answer


def solution(mesh):
    in_specs = (P(None, "grp", "brick", None), P("grp", "brick", None), P("grp", "brick", None))
    out_specs = P(None, "grp", "brick", None)
    return jax.shard_map(
        on_device, mesh=mesh, in_specs=in_specs, out_specs=out_specs, check_vma=False
    )
```

```python
import jax
import jax.numpy as jnp
from jax import lax
from jax.experimental import pallas as pl
from jax.experimental.pallas import tpu as pltpu
from jax.sharding import PartitionSpec as P

BETA = 1.0
THETA = 1.5
DELTA = 1.0
SIGMA = 1.5
LANES = 128
HALO = 8
NEAR = 10
SKIRT = 12
REACH = 5
CUT_LIMIT = 28 * 2**20
F32 = jnp.float32


def rate_list():
    rates = [1.0 / SIGMA]
    for number in range(3):
        rates.append(1.0 / (2.0 * SIGMA - rates[-1]))
    return rates


RATES = rate_list()
STEPS = [(0.0, 1.0 / THETA)] + [
    (RATES[k] * RATES[k - 1], 2.0 * RATES[k] / DELTA) for k in (1, 2, 3)
]


def lane_of(shape):
    return lax.broadcasted_iota(jnp.int32, shape, len(shape) - 1)


def row_of(shape):
    return lax.broadcasted_iota(jnp.int32, shape, len(shape) - 2)


def ahead_y(v):
    return pltpu.roll(v, v.shape[0] - 1, 0)


def behind_y(v):
    return pltpu.roll(v, 1, 0)


def ahead_z(v):
    return pltpu.roll(v, LANES - 1, 1)


def behind_z(v):
    return pltpu.roll(v, 1, 1)


class Level:
    def __init__(self, scale, depth, rows, height, unroll=4):
        self.unroll = unroll
        self.scale = scale
        self.depth = depth
        self.groups = LANES // depth
        self.rows = rows
        self.height = height

    def shape(self, *lead):
        return (*lead, self.rows + 2, self.height, LANES)

    def lanes(self):
        z = lane_of((self.height, LANES)) % self.depth
        return z == 0, z == self.depth - 1


def ghosts(level, ref, index=()):
    if level.groups == 1:
        return
    lane = lane_of((level.height, LANES))
    first = ref[(*index, 1)]
    last = ref[(*index, level.rows)]
    ref[(*index, 0)] = jnp.where(lane < level.depth, 0.0, pltpu.roll(last, level.depth, 1))
    ref[(*index, level.rows + 1)] = jnp.where(
        lane >= LANES - level.depth, 0.0, pltpu.roll(first, LANES - level.depth, 1)
    )


def setup(level, stiff, react, coef, inside, lo, hi):
    kx, ky, kym, kz, kzm, diag, inv = coef
    half = 0.5 * level.scale
    front, back = level.lanes()
    kx[lo - 1] = half * (stiff(lo - 1) + stiff(lo))

    def body(i, _):
        centre = stiff(i)
        xp = half * (centre + stiff(i + 1))
        xm = kx[i - 1]
        yp = half * (centre + ahead_y(centre))
        ym = behind_y(yp)
        zp = half * (centre + jnp.where(back, 0.0, ahead_z(centre)))
        zm = half * (centre + jnp.where(front, 0.0, behind_z(centre)))
        total = ((xp + xm) + (yp + ym)) + (zp + zm) + react(i)
        kx[i] = xp
        ky[i] = yp
        kym[i] = ym
        kz[i] = jnp.where(back, 0.0, zp)
        kzm[i] = jnp.where(front, 0.0, zm)
        diag[i] = total
        inv[i] = jnp.where(inside(i), 1.0 / (total + 2.0 * BETA * level.scale), 0.0)
        return 0

    lax.fori_loop(lo, hi, body, 0, unroll=2)


def begin(level, src, coef, state, direction, lo, hi):
    inv = coef[6]

    def body(i, _):
        scaled = inv[i] * (1.0 / THETA)
        for c in range(3):
            value = scaled * src[c, i]
            state[c, i] = value
            direction[c, i] = value
        return 0

    lax.fori_loop(lo, hi, body, 0, unroll=2)
    for c in range(3):
        ghosts(level, state, (c,))


def sweep(level, src, coef, state, lo, hi, prepare, emit):
    kx, ky, kym, kz, kzm, diag, inv = coef
    front, back = level.lanes()
    bulk = BETA * level.scale

    def spread(i):
        ux, uy, uz = state[0, i], state[1, i], state[2, i]
        return (
            (state[0, i + 1] - ux)
            + (ahead_y(uy) - uy)
            + (jnp.where(back, 0.0, ahead_z(uz)) - uz)
        ) * bulk

    def body(i, before):
        here = spread(i)
        extra = prepare(i)
        for c in range(3):
            u = state[c, i]
            flux = kx[i] * state[c, i + 1] + kx[i - 1] * state[c, i - 1]
            flux = flux + (ky[i] * ahead_y(u) + kym[i] * behind_y(u))
            flux = flux + (kz[i] * ahead_z(u) + kzm[i] * behind_z(u))
            if c == 0:
                other = before
            elif c == 1:
                other = behind_y(here)
            else:
                other = jnp.where(front, bulk * u, behind_z(here))
            resid = src[c, i] - diag[i] * u + flux + (here - other)
            emit(i, c, u, resid, extra)
        return here

    lax.fori_loop(lo, hi, body, spread(lo - 1), unroll=level.unroll)


def step(level, number, src, coef, state, fresh, direction, lo, hi):
    keep, gain = STEPS[number]
    inv = coef[6]

    def emit(i, c, u, resid, scaled):
        move = scaled * resid
        if number > 0:
            move = move + keep * direction[c, i]
        direction[c, i] = move
        fresh[c, i] = u + move

    sweep(level, src, coef, state, lo, hi, lambda i: gain * inv[i], emit)
    for c in range(3):
        ghosts(level, fresh, (c,))


def residual(level, src, coef, state, out, lo, hi):
    def emit(i, c, u, resid, extra):
        out[c, i] = resid

    sweep(level, src, coef, state, lo, hi, lambda i: None, emit)


def pick(rows, cols, rule, value):
    shape = (rows, cols)
    return jnp.where(rule(row_of(shape), lane_of(shape)), value, 0.0).astype(F32)


def mix(values, matrix):
    return jnp.dot(values, matrix, precision=lax.Precision.HIGHEST, preferred_element_type=F32)


def pairs(ref, index, start, count):
    return ref[(*index, pl.ds(start, count, 2))] + ref[(*index, pl.ds(start + 1, count, 2))]


def vmem(count):
    return [pl.BlockSpec(memory_space=pltpu.VMEM)] * count


def call(kernel, outs, scratch, *args, name, aliases={}):
    smem = pl.BlockSpec(memory_space=pltpu.SMEM)
    return pl.pallas_call(
        kernel,
        out_shape=[jax.ShapeDtypeStruct(s, F32) for s in outs],
        in_specs=[smem] + vmem(len(args) - 1),
        out_specs=vmem(len(outs)),
        scratch_shapes=[pltpu.VMEM(s, F32) for s in scratch],
        compiler_params=pltpu.CompilerParams(vmem_limit_bytes=28 * 2**20),
        input_output_aliases=aliases,
        name=name,
    )(*args)


def by_parity(index, act):
    odd = index % 2

    @pl.when(odd == 0)
    def _():
        act(True)

    @pl.when(odd == 1)
    def _():
        act(False)


def cut_kernel(place, f, k, r, first, second, sems):
    def act(even):
        copies = []
        for side, out in enumerate((second, first) if even else (first, second)):
            rows = pl.ds(HALO * side, HALO)
            copies += [
                pltpu.make_async_copy(f.at[:, :, rows], out.at[0:3], sems.at[3 * side]),
                pltpu.make_async_copy(k.at[:, rows], out.at[3], sems.at[3 * side + 1]),
                pltpu.make_async_copy(r.at[:, rows], out.at[4], sems.at[3 * side + 2]),
            ]
        for copy in copies:
            copy.start()
        for copy in copies:
            copy.wait()

    by_parity(place[1], act)


def cut(place, f, k, r):
    return pl.pallas_call(
        cut_kernel,
        out_shape=[jax.ShapeDtypeStruct((5, 16, HALO, LANES), F32)] * 2,
        in_specs=[pl.BlockSpec(memory_space=pltpu.SMEM)]
        + [pl.BlockSpec(memory_space=pltpu.HBM)] * 3,
        out_specs=vmem(2),
        scratch_shapes=[pltpu.SemaphoreType.DMA((6,))],
        compiler_params=pltpu.CompilerParams(vmem_limit_bytes=CUT_LIMIT),
        name="cut0",
    )(place, f, k, r)


MESSAGE = [(0, 0, 7), (1, 7, 7), (2, 14, 7), (4, 21, 7), (3, 28, 8)]


def join_kernel(place, f, k, r, first, second, data, near, far):
    def sides(even):
        lo, hi = (second, first) if even else (first, second)
        for q in range(5):
            data[q, 8:24, 0:8] = lo[q]
            data[q, 8:24, 8:24] = f[q] if q < 3 else (k, r)[q - 3][...]
            data[q, 8:24, 24:32] = hi[q]

    by_parity(place[1], sides)

    def act(even):
        up, down = (near, far) if even else (far, near)
        for q, at, rows in MESSAGE:
            down[at : at + rows] = data[q, 8 : 8 + rows]
            up[at : at + rows] = data[q, 24 - rows : 24]

    by_parity(place[0], act)


FINE = Level(1.0, 128, 30, 32)
FINE_UP = Level(1.0, 128, 22, 24)
MIDDLE = Level(0.25, 64, 14, 32)
MIDDLE_UP = Level(0.25, 64, 10, 24, 5)
COARSE = Level(0.0625, 32, 8, 48, 8)
COARSE_UP = Level(0.0625, 32, 8, 32, 8)
LAST = Level(0.015625, 16, 2, 24)


def coef_shapes(level):
    return [level.shape()] * 7


def fine_inside(place):
    y = place[1] * 16 - HALO + row_of((32, LANES))
    fits = (y >= 0) & (y < place[3] * 16)

    def inside(i):
        x = place[0] * 16 + i - HALO
        return fits & (x >= 0) & (x < place[2] * 16)

    return inside


def fine_inner(place, given, near_in, data, kept, s0, d0, t0, resid, near):
    coef = [kept.at[j] for j in range(7)]
    setup(FINE, lambda i: data[3, i], lambda i: data[4, i], coef, fine_inside(place), 9, 23)
    begin(FINE, data, coef, s0, d0, 9, 23)
    step(FINE, 1, data, coef, s0, t0, d0, 10, 22)
    step(FINE, 2, data, coef, t0, s0, d0, 11, 21)
    step(FINE, 3, data, coef, s0, t0, d0, 12, 20)
    residual(FINE, data, coef, t0, resid, 13, 19)


def fine_outer(place, near, far, *refs):
    data, kept, s0, d0, t0, resid, saved, packed, first, second, sums = refs[6:]
    coef = [kept.at[j] for j in range(7)]
    zero = jnp.zeros((32, LANES), F32)

    def act(even):
        lo, hi = (far, near) if even else (near, far)
        for q, at, rows in MESSAGE:
            data[q, 8 - rows : 8] = lo[at : at + rows]
            data[q, 24 : 24 + rows] = hi[at : at + rows]
            if rows < 8:
                data[q, 0] = zero
                data[q, 31] = zero

    by_parity(place[0], act)
    inside = fine_inside(place)
    for lo, hi in ((1, 9), (23, 31)):
        setup(FINE, lambda i: data[3, i], lambda i: data[4, i], coef, inside, lo, hi)
        begin(FINE, data, coef, s0, d0, lo, hi)
    for lo, hi in ((2, 10), (22, 30)):
        step(FINE, 1, data, coef, s0, t0, d0, lo, hi)
    for lo, hi in ((3, 11), (21, 29)):
        step(FINE, 2, data, coef, t0, s0, d0, lo, hi)
    for lo, hi in ((4, 12), (20, 28)):
        step(FINE, 3, data, coef, s0, t0, d0, lo, hi)
    saved[...] = t0[:, 4:28, 4:28]
    residual(FINE, data, coef, t0, resid, 6, 13)
    residual(FINE, data, coef, t0, resid, 19, 26)
    pair = s0.at[0]
    wide = sums
    for q in range(5):
        for t in range(16):
            half, i = divmod(t, 8)
            where = (q, i, slice(None), slice(half * LANES, half * LANES + LANES))
            if q >= 3:
                pair[t] = data[q, 2 * t] + data[q, 2 * t + 1]
            elif 3 <= t <= 12:
                pair[t] = resid[q, 2 * t] + resid[q, 2 * t + 1]
            else:
                wide[where] = jnp.zeros((16, LANES), F32)
                continue
            wide[where] = pairs(pair, (t,), 0, 16)
    matrix = pick(
        2 * LANES, LANES, lambda a, b: (a % LANES) // 2 + 64 * (a // LANES) == b, 0.125
    )
    packed[...] = mix(wide[...].reshape(5 * 8 * 16, 2 * LANES), matrix).reshape(5, 8, 16, LANES)

    def send(even):
        left, right = (second, first) if even else (first, second)
        for q in range(5):
            skip = 1 if q < 3 else 2
            left[q] = packed[q, :, 4 + skip : 12 + skip]
            right[q] = packed[q, :, 4 - skip : 12 - skip]

    by_parity(place[1], send)


def fine_trim(place, data, kept, data_up, kept_up):
    for q in range(3):
        data_up[q] = data[q, 4:28, 4:28]
    for j in range(7):
        kept_up[j] = kept[j, 4:28, 4:28]


def middle_cut(place, own, first, second, trimmed, near, far, centre):
    low = lane_of((32, LANES)) < 64
    zero = jnp.zeros((4, LANES), F32)

    def sides(even):
        left, right = (second, first) if even else (first, second)
        for q in range(5):
            skip = 1 if q < 3 else 2
            for i in range(8):
                centre[q, i, 0 : 4 - skip] = zero[0 : 4 - skip]
                centre[q, i, 4 - skip : 12 - skip] = left[q, i]
                centre[q, i, 12 - skip : 20 + skip] = own[q, i, 4 - skip : 12 + skip]
                centre[q, i, 20 + skip : 28 + skip] = right[q, i]
                centre[q, i, 28 + skip : 32] = zero[0 : 4 - skip]

    by_parity(place[1], sides)

    def at(q, x, half):
        value = centre[q, x + 4 if x < 4 else x - 4]
        return value if (x >= 4) == (half == 1) else pltpu.roll(value, 64, 1)

    def act(even):
        up, down = (near, far) if even else (far, near)
        for q in range(5):
            skip = 1 if q < 3 else 2
            for t in range(4):
                up[q, t] = jnp.where(low, at(q, t - skip, 0), at(q, t - skip + 4, 1))
                down[q, t] = jnp.where(low, at(q, t + skip, 0), at(q, t + skip + 4, 1))

    by_parity(place[0], act)


def middle_inside(place):
    y = place[1] * 8 - SKIRT + row_of((32, LANES))
    fits = (y >= 0) & (y < place[3] * 8)
    x0 = place[0] * 8 - NEAR + 14 * (lane_of((32, LANES)) // 64)

    def inside(i):
        x = x0 + (i - 1)
        return fits & (x >= 0) & (x < place[2] * 8)

    return inside


def middle_join(centre, lo, hi, data):
    low = lane_of((32, LANES)) < 64
    zero = jnp.zeros((32, LANES), F32)

    def moved(ref, q, t, half):
        value = ref[q, t % 4]
        return value if t // 4 == half else pltpu.roll(value, 64, 1)

    for q in range(5):
        skip = 1 if q < 3 else 2
        for i in range(14):
            t = i - (2 - skip)
            if t < 0:
                a = zero
            elif t < 8:
                a = moved(lo, q, t, 0)
            else:
                a = centre[q, i - 6]
            t = i - (4 + skip)
            if t < 0:
                b = centre[q, i]
            elif t < 8:
                b = moved(hi, q, t, 1)
            else:
                b = zero
            data[q, i + 1] = jnp.where(low, a, b)
        ghosts(MIDDLE, data, (q,))


def middle_down(place, centre, near, far, data, saved, packed, kept, s1, d1, t1, pair, sums):
    coef = [kept.at[j] for j in range(7)]
    lane = lane_of((32, LANES))
    low = lane < 64
    by_parity(
        place[0],
        lambda even: middle_join(centre, *((far, near) if even else (near, far)), data),
    )
    setup(MIDDLE, lambda i: data[3, i], lambda i: data[4, i], coef, middle_inside(place), 1, 15)
    begin(MIDDLE, data, coef, s1, d1, 1, 15)
    step(MIDDLE, 1, data, coef, s1, t1, d1, 1, 15)
    step(MIDDLE, 2, data, coef, t1, s1, d1, 1, 15)
    step(MIDDLE, 3, data, coef, s1, saved, d1, 1, 15)
    residual(MIDDLE, data, coef, saved, d1, 11, 15)
    residual(MIDDLE, data, coef, saved, d1, 1, 5)
    for q in range(5):
        from_, at = (d1, q) if q < 3 else (data, q)
        for m in range(2):
            a = from_[at, 11 + 2 * m] + from_[at, 12 + 2 * m]
            b = from_[at, 1 + 2 * m] + from_[at, 2 + 2 * m]
            pair[q, m] = jnp.where(low, a, b)
            sums[q, :, m * LANES : m * LANES + LANES] = pairs(pair, (q, m), 0, 16)
    matrix = pick(
        2 * LANES,
        LANES,
        lambda a, b: (a // LANES) * 32 + ((a % LANES) // 64) * 64 + (a % 64) // 2 == b,
        0.125,
    )
    packed[...] = mix(sums[...].reshape(5 * 16, 2 * LANES), matrix).reshape(5, 16, LANES)


def middle_trim(place, data, saved, kept, data_up, saved_up, kept_up):
    low = lane_of((24, LANES)) < 64
    groups = [(data, data_up, 3), (saved, saved_up, 3), (kept, kept_up, 7)]
    for old, new, count in groups:
        for q in range(count):
            for j in range(12):
                new[q, j] = jnp.where(low, old[q, 4 + j, 2:26], old[q, j, 2:26])


def column_kernel(place, parts, out):
    zero = jnp.zeros((4, LANES), F32)
    for q in range(5):
        out[q, 0:2] = zero[0:2]
        out[q, 46:48] = zero[0:2]
    for d in range(2 * REACH + 1):
        at = place[1] + (d - REACH)
        valid = (at >= 0) & (at < place[3])
        safe = jnp.clip(at, 0, place[3] - 1)
        for q in range(5):
            block = parts[safe, q]
            out[q, 2 + 4 * d : 6 + 4 * d] = jnp.where(valid, block, zero)


def coarse_inside(place):
    sub = row_of((48, LANES))
    y = place[1] * 4 - 22 + sub
    fits = (y >= 0) & (y < place[3] * 4)
    return lambda i: fits


def last_inside(place):
    y = place[1] * 2 - 11 + row_of((24, LANES))
    fits = (y >= 0) & (y < place[3] * 2)
    return lambda i: fits


def climb(place, mine, other, data1, saved1, kept1, data0, saved0, kept0, out, *scratch):
    scratch = list(scratch)

    def take(count):
        got, scratch[:] = scratch[:count], scratch[count:]
        return got

    data2, s2, t2, d2, keep2 = take(5)
    coef2 = take(7)
    sums3 = take(1)[0]
    data3, s3, t3, d3 = take(4)
    coef3 = take(7)
    grown3, grown2, grown1 = take(3)
    s1, t1, d1 = take(3)
    s0, t0, d0 = take(3)
    coef1 = [kept1.at[j] for j in range(7)]
    coef0 = [kept0.at[j] for j in range(7)]

    group = lane_of((48, LANES)) // 32

    def act(even):
        order = (mine, other) if even else (other, mine)
        for q in range(5):
            for i in range(8):
                row = None
                for g in range(4):
                    block = order[i // 4][g, q]
                    shift = ((g - i % 4) * 32) % LANES
                    block = pltpu.roll(block, shift, 1) if shift else block
                    row = block if row is None else jnp.where(group == g, block, row)
                data2[q, i + 1] = row
            ghosts(COARSE, data2, (q,))

    by_parity(place[0], act)
    setup(COARSE, lambda i: data2[3, i], lambda i: data2[4, i], coef2, coarse_inside(place), 1, 9)
    begin(COARSE, data2, coef2, s2, d2, 1, 9)
    step(COARSE, 1, data2, coef2, s2, t2, d2, 1, 9)
    step(COARSE, 2, data2, coef2, t2, s2, d2, 1, 9)
    step(COARSE, 3, data2, coef2, s2, keep2, d2, 1, 9)
    residual(COARSE, data2, coef2, keep2, d2, 1, 9)

    pair = s2.at[0]
    for q in range(5):
        from_ = d2 if q < 3 else data2
        for t in range(4):
            half, i = divmod(t, 2)
            pair[t] = from_[q, 1 + 2 * t] + from_[q, 2 + 2 * t]
            sums3[q, i, :, half * LANES : half * LANES + LANES] = pairs(pair, (t,), 0, 24)
    matrix = pick(
        2 * LANES,
        LANES,
        lambda a, b: (2 * ((a % LANES) // 32) + a // LANES) * 16 + (a % 32) // 2 == b,
        0.125,
    )
    shrunk = mix(sums3[...].reshape(5 * 2 * 24, 2 * LANES), matrix).reshape(5, 2, 24, LANES)
    for q in range(5):
        for i in range(2):
            data3[q, i + 1] = shrunk[q, i]
        ghosts(LAST, data3, (q,))
    setup(LAST, lambda i: data3[3, i], lambda i: data3[4, i], coef3, last_inside(place), 1, 3)
    begin(LAST, data3, coef3, s3, d3, 1, 3)
    step(LAST, 1, data3, coef3, s3, t3, d3, 1, 3)
    step(LAST, 2, data3, coef3, t3, s3, d3, 1, 3)
    step(LAST, 3, data3, coef3, s3, t3, d3, 1, 3)

    data2u, s2u, t2u, d2u = (ref.at[:, :, 8:40] for ref in (data2, s2, t2, d2))
    coef2u = [ref.at[:, 8:40] for ref in coef2]
    matrix = pick(
        LANES,
        2 * LANES,
        lambda a, b: (2 * ((b % LANES) // 32) + b // LANES == a // 16) & ((b % 32) // 2 == a % 16),
        1.0,
    )
    flat = jnp.concatenate([t3[c, i + 1] for c in range(3) for i in range(2)], axis=0)
    wide = mix(flat, matrix)
    for c in range(3):
        for t in range(4):
            half, i = divmod(t, 2)
            at = (c * 2 + i) * 24
            piece = wide[at : at + 24, half * LANES : half * LANES + LANES]
            grown3[c, t, pl.ds(0, 24, 2)] = piece
            grown3[c, t, pl.ds(1, 24, 2)] = piece
            more = grown3[c, t, 8:40]
            s2u[c, 1 + 2 * t] = keep2[c, 1 + 2 * t, 8:40] + more
            s2u[c, 2 + 2 * t] = keep2[c, 2 + 2 * t, 8:40] + more
        ghosts(COARSE_UP, s2u, (c,))
    step(COARSE_UP, 0, data2u, coef2u, s2u, t2u, d2u, 1, 9)
    step(COARSE_UP, 1, data2u, coef2u, t2u, s2u, d2u, 1, 9)
    step(COARSE_UP, 2, data2u, coef2u, s2u, t2u, d2u, 1, 9)
    step(COARSE_UP, 3, data2u, coef2u, t2u, s2u, d2u, 1, 9)

    matrix = pick(
        LANES,
        LANES,
        lambda a, b: (a < 64) & (b // 64 == a // 32) & ((b % 64) // 2 == a % 32),
        1.0,
    )
    small = lane_of((16, LANES)) < 32

    def window(c, x, slot):
        valid = (x >= 0) & (x < place[2] * 4)
        safe = jnp.clip(x, 0, place[2] * 4 - 1)
        value = s2[c, 1 + safe % 8, 16:32]
        value = pltpu.roll(value, (slot * 32 + LANES - (safe // 8) * 32) % LANES, 1)
        return jnp.where(valid, value, 0.0)

    pieces = []
    for c in range(3):
        for m in range(5):
            x = place[0] * 4 - 3 + m
            pieces.append(jnp.where(small, window(c, x, 0), window(c, x + 5, 1)))
    wide = mix(jnp.concatenate(pieces, axis=0), matrix)
    for c in range(3):
        for m in range(5):
            at = (c * 5 + m) * 16
            piece = wide[at : at + 16]
            grown2[c, m, pl.ds(0, 16, 2)] = piece
            grown2[c, m, pl.ds(1, 16, 2)] = piece
            more = grown2[c, m, 2:26]
            s1[c, 1 + 2 * m] = saved1[c, 1 + 2 * m] + more
            s1[c, 2 + 2 * m] = saved1[c, 2 + 2 * m] + more
        ghosts(MIDDLE_UP, s1, (c,))
    step(MIDDLE_UP, 0, data1, coef1, s1, t1, d1, 1, 11)
    step(MIDDLE_UP, 1, data1, coef1, t1, s1, d1, 1, 11)
    step(MIDDLE_UP, 2, data1, coef1, s1, t1, d1, 1, 11)
    step(MIDDLE_UP, 3, data1, coef1, t1, s1, d1, 1, 11)

    for half in range(2):
        matrix = pick(LANES, LANES, lambda a, b: a == 64 * half + b // 2, 1.0)
        rows = [5 + t for t in range(6)] if half == 0 else [1 + t for t in range(6)]
        flat = jnp.concatenate([s1[c, i, 8:24] for c in range(3) for i in rows], axis=0)
        wide = mix(flat, matrix)
        for c in range(3):
            for t in range(6):
                at = (c * 6 + t) * 16
                piece = wide[at : at + 16]
                grown1[c, t, pl.ds(0, 16, 2)] = piece
                grown1[c, t, pl.ds(1, 16, 2)] = piece
                more = grown1[c, t, 0:24]
                row = 2 * (t + 6 * half)
                s0[c, row] = saved0[c, row] + more
                s0[c, row + 1] = saved0[c, row + 1] + more
    step(FINE_UP, 0, data0, coef0, s0, t0, d0, 1, 23)
    step(FINE_UP, 1, data0, coef0, t0, s0, d0, 2, 22)
    step(FINE_UP, 2, data0, coef0, s0, t0, d0, 3, 21)
    keep, gain = STEPS[3]

    def emit(i, c, u, resid, scaled):
        move = scaled * resid + keep * d0[c, i]
        out[c, i - 4] = (u + move)[4:20]

    sweep(FINE_UP, data0, coef0, t0, 4, 20, lambda i: gain * coef0[6][i], emit)


def swap(value, axis, first):
    count = lax.axis_size(axis)
    ends = [(i, i + 1) for i in range(first, count - 1, 2)]
    return lax.ppermute(value, axis, ends + [(b, a) for a, b in ends])


def on_device(right_side, stiffness, reaction):
    bricks = lax.axis_size("brick")
    count = lax.axis_size("grp")
    place = jnp.stack(
        [lax.axis_index("grp"), lax.axis_index("brick"), jnp.int32(count), jnp.int32(bricks)]
    ).astype(jnp.int32)
    local = (right_side, stiffness, reaction)
    first, second = cut(place, *local)
    first = swap(first, "brick", 0)
    second = swap(second, "brick", 1)
    data0, near, far = call(
        join_kernel,
        [FINE.shape(5)] + [(36, 32, 128)] * 2,
        [],
        place,
        *local,
        first,
        second,
        name="join0",
    )
    far_in = swap(far, "grp", 1)
    states = [FINE.shape(5), FINE.shape(7)] + [FINE.shape(3)] * 4
    *inner, near = call(
        fine_inner,
        states + [(36, 32, 128)],
        [],
        place,
        data0,
        near,
        name="inner0",
        aliases={1: 0, 2: 6},
    )
    near_in = swap(near, "grp", 0)
    data0, kept0, _, _, _, _, saved0, packed1, first, second = call(
        fine_outer,
        states + [(3, 24, 24, 128), (5, 8, 16, 128)] + [(5, 8, 8, 128)] * 2,
        [(5, 8, 16, 256)],
        place,
        near_in,
        far_in,
        *inner,
        name="outer0",
        aliases={3 + j: j for j in range(6)},
    )
    first = swap(first, "brick", 0)
    second = swap(second, "brick", 1)
    data0, kept0 = call(
        fine_trim, [FINE_UP.shape(3), FINE_UP.shape(7)], [], place, data0, kept0, name="trim0"
    )
    near, far, centre = call(
        middle_cut,
        [(5, 4, 32, 128)] * 2 + [(5, 8, 32, 128)],
        [],
        place,
        packed1,
        first,
        second,
        data0,
        name="cut1",
    )
    far_in = swap(far, "grp", 1)
    near_in = swap(near, "grp", 0)
    data1, saved1, packed2, kept1 = call(
        middle_down,
        [MIDDLE.shape(5), MIDDLE.shape(3), (5, 16, 128), MIDDLE.shape(7)],
        [MIDDLE.shape(3)] * 3 + [(5, 2, 32, 128), (5, 16, 256)],
        place,
        centre,
        near_in,
        far_in,
        name="down1",
    )
    block = packed2[:, 6:10]
    parts = lax.all_to_all(jnp.broadcast_to(block[None], (bricks, 5, 4, 128)), "brick", 0, 0)
    (column,) = call(column_kernel, [(5, 48, 128)], [], place, parts, name="column")
    mine = lax.all_to_all(
        jnp.broadcast_to(column[None], (count // 2, 5, 48, 128)),
        "grp",
        0,
        0,
        axis_index_groups=[list(range(core, count, 2)) for core in range(2)],
    )
    other = swap(mine, "grp", 0)
    data1, saved1, kept1 = call(
        middle_trim,
        [MIDDLE_UP.shape(3)] * 2 + [MIDDLE_UP.shape(7)],
        [],
        place,
        data1,
        saved1,
        kept1,
        name="trim1",
    )
    coarse = [COARSE.shape(5)] + [COARSE.shape(3)] * 4 + coef_shapes(COARSE)
    last = [(5, 2, 24, 256), LAST.shape(5)] + [LAST.shape(3)] * 3 + coef_shapes(LAST)
    grown = [(3, 4, 48, 128), (3, 5, 32, 128), (3, 6, 32, 128)]
    (answer,) = call(
        climb,
        [(3, 16, 16, 128)],
        coarse + last + grown + [MIDDLE_UP.shape(3)] * 3 + [FINE_UP.shape(3)] * 3,
        place,
        mine,
        other,
        data1,
        saved1,
        kept1,
        data0,
        saved0,
        kept0,
        name="climb",
    )
    return answer


def solution(mesh):
    in_specs = (P(None, "grp", "brick", None), P("grp", "brick", None), P("grp", "brick", None))
    out_specs = P(None, "grp", "brick", None)
    return jax.shard_map(
        on_device, mesh=mesh, in_specs=in_specs, out_specs=out_specs, check_vma=False
    )
```

```python
import jax
import jax.numpy as jnp
from jax import lax
from jax.experimental import pallas as pl
from jax.experimental.pallas import tpu as pltpu
from jax.sharding import PartitionSpec as P

BETA = 1.0
THETA = 1.5
DELTA = 1.0
SIGMA = 1.5
LANES = 128
HALO = 8
NEAR = 10
SKIRT = 12
REACH = 5
CUT_LIMIT = 28 * 2**20
F32 = jnp.float32


def rate_list():
    rates = [1.0 / SIGMA]
    for number in range(3):
        rates.append(1.0 / (2.0 * SIGMA - rates[-1]))
    return rates


RATES = rate_list()
STEPS = [(0.0, 1.0 / THETA)] + [
    (RATES[k] * RATES[k - 1], 2.0 * RATES[k] / DELTA) for k in (1, 2, 3)
]


def lane_of(shape):
    return lax.broadcasted_iota(jnp.int32, shape, len(shape) - 1)


def row_of(shape):
    return lax.broadcasted_iota(jnp.int32, shape, len(shape) - 2)


def ahead_y(v):
    return pltpu.roll(v, v.shape[0] - 1, 0)


def behind_y(v):
    return pltpu.roll(v, 1, 0)


def ahead_z(v):
    return pltpu.roll(v, LANES - 1, 1)


def behind_z(v):
    return pltpu.roll(v, 1, 1)


class Level:
    def __init__(self, scale, depth, rows, height, unroll=4):
        self.unroll = unroll
        self.scale = scale
        self.depth = depth
        self.groups = LANES // depth
        self.rows = rows
        self.height = height

    def shape(self, *lead):
        return (*lead, self.rows + 2, self.height, LANES)

    def lanes(self):
        z = lane_of((self.height, LANES)) % self.depth
        return z == 0, z == self.depth - 1


def ghosts(level, ref, index=()):
    if level.groups == 1:
        return
    lane = lane_of((level.height, LANES))
    first = ref[(*index, 1)]
    last = ref[(*index, level.rows)]
    ref[(*index, 0)] = jnp.where(lane < level.depth, 0.0, pltpu.roll(last, level.depth, 1))
    ref[(*index, level.rows + 1)] = jnp.where(
        lane >= LANES - level.depth, 0.0, pltpu.roll(first, LANES - level.depth, 1)
    )


def setup(level, stiff, react, coef, inside, lo, hi):
    kx, ky, kym, kz, kzm, diag, inv = coef
    half = 0.5 * level.scale
    front, back = level.lanes()
    kx[lo - 1] = half * (stiff(lo - 1) + stiff(lo))

    def body(i, _):
        centre = stiff(i)
        xp = half * (centre + stiff(i + 1))
        xm = kx[i - 1]
        yp = half * (centre + ahead_y(centre))
        ym = behind_y(yp)
        zp = half * (centre + jnp.where(back, 0.0, ahead_z(centre)))
        zm = half * (centre + jnp.where(front, 0.0, behind_z(centre)))
        total = ((xp + xm) + (yp + ym)) + (zp + zm) + react(i)
        kx[i] = xp
        ky[i] = yp
        kym[i] = ym
        kz[i] = jnp.where(back, 0.0, zp)
        kzm[i] = jnp.where(front, 0.0, zm)
        diag[i] = total
        inv[i] = jnp.where(inside(i), 1.0 / (total + 2.0 * BETA * level.scale), 0.0)
        return 0

    lax.fori_loop(lo, hi, body, 0, unroll=4)


def begin(level, src, coef, state, direction, lo, hi):
    inv = coef[6]

    def body(i, _):
        scaled = inv[i] * (1.0 / THETA)
        for c in range(3):
            value = scaled * src[c, i]
            state[c, i] = value
            direction[c, i] = value
        return 0

    lax.fori_loop(lo, hi, body, 0, unroll=4)
    for c in range(3):
        ghosts(level, state, (c,))


def sweep(level, src, coef, state, lo, hi, prepare, emit):
    kx, ky, kym, kz, kzm, diag, inv = coef
    front, back = level.lanes()
    bulk = BETA * level.scale

    def spread(i):
        ux, uy, uz = state[0, i], state[1, i], state[2, i]
        return (
            (state[0, i + 1] - ux)
            + (ahead_y(uy) - uy)
            + (jnp.where(back, 0.0, ahead_z(uz)) - uz)
        ) * bulk

    def body(i, before):
        here = spread(i)
        extra = prepare(i)
        for c in range(3):
            u = state[c, i]
            flux = kx[i] * state[c, i + 1] + kx[i - 1] * state[c, i - 1]
            flux = flux + (ky[i] * ahead_y(u) + kym[i] * behind_y(u))
            flux = flux + (kz[i] * ahead_z(u) + kzm[i] * behind_z(u))
            if c == 0:
                other = before
            elif c == 1:
                other = behind_y(here)
            else:
                other = jnp.where(front, bulk * u, behind_z(here))
            resid = src[c, i] - diag[i] * u + flux + (here - other)
            emit(i, c, u, resid, extra)
        return here

    lax.fori_loop(lo, hi, body, spread(lo - 1), unroll=level.unroll)


def step(level, number, src, coef, state, fresh, direction, lo, hi):
    keep, gain = STEPS[number]
    inv = coef[6]

    def emit(i, c, u, resid, scaled):
        move = scaled * resid
        if number > 0:
            move = move + keep * direction[c, i]
        direction[c, i] = move
        fresh[c, i] = u + move

    sweep(level, src, coef, state, lo, hi, lambda i: gain * inv[i], emit)
    for c in range(3):
        ghosts(level, fresh, (c,))


def residual(level, src, coef, state, out, lo, hi):
    def emit(i, c, u, resid, extra):
        out[c, i] = resid

    sweep(level, src, coef, state, lo, hi, lambda i: None, emit)


def pick(rows, cols, rule, value):
    shape = (rows, cols)
    return jnp.where(rule(row_of(shape), lane_of(shape)), value, 0.0).astype(F32)


def mix(values, matrix):
    return jnp.dot(values, matrix, precision=lax.Precision.HIGH, preferred_element_type=F32)


def pairs(ref, index, start, count):
    return ref[(*index, pl.ds(start, count, 2))] + ref[(*index, pl.ds(start + 1, count, 2))]


def vmem(count):
    return [pl.BlockSpec(memory_space=pltpu.VMEM)] * count


def call(kernel, outs, scratch, *args, name, aliases={}):
    smem = pl.BlockSpec(memory_space=pltpu.SMEM)
    return pl.pallas_call(
        kernel,
        out_shape=[jax.ShapeDtypeStruct(s, F32) for s in outs],
        in_specs=[smem] + vmem(len(args) - 1),
        out_specs=vmem(len(outs)),
        scratch_shapes=[pltpu.VMEM(s, F32) for s in scratch],
        compiler_params=pltpu.CompilerParams(vmem_limit_bytes=28 * 2**20),
        input_output_aliases=aliases,
        name=name,
    )(*args)


def by_parity(index, act):
    odd = index % 2

    @pl.when(odd == 0)
    def _():
        act(True)

    @pl.when(odd == 1)
    def _():
        act(False)


def cut_kernel(place, f, k, r, first, second, sems):
    def act(even):
        copies = []
        for side, out in enumerate((second, first) if even else (first, second)):
            rows = pl.ds(HALO * side, HALO)
            copies += [
                pltpu.make_async_copy(f.at[:, :, rows], out.at[0:3], sems.at[3 * side]),
                pltpu.make_async_copy(k.at[:, rows], out.at[3], sems.at[3 * side + 1]),
                pltpu.make_async_copy(r.at[:, rows], out.at[4], sems.at[3 * side + 2]),
            ]
        for copy in copies:
            copy.start()
        for copy in copies:
            copy.wait()

    by_parity(place[1], act)


def cut(place, f, k, r):
    return pl.pallas_call(
        cut_kernel,
        out_shape=[jax.ShapeDtypeStruct((5, 16, HALO, LANES), F32)] * 2,
        in_specs=[pl.BlockSpec(memory_space=pltpu.SMEM)]
        + [pl.BlockSpec(memory_space=pltpu.HBM)] * 3,
        out_specs=vmem(2),
        scratch_shapes=[pltpu.SemaphoreType.DMA((6,))],
        compiler_params=pltpu.CompilerParams(vmem_limit_bytes=CUT_LIMIT),
        name="cut0",
    )(place, f, k, r)


MESSAGE = [(0, 0, 7), (1, 7, 7), (2, 14, 7), (4, 21, 7), (3, 28, 8)]


def join_kernel(place, f, k, r, first, second, data, near, far):
    def sides(even):
        lo, hi = (second, first) if even else (first, second)
        for q in range(5):
            data[q, 8:24, 0:8] = lo[q]
            data[q, 8:24, 8:24] = f[q] if q < 3 else (k, r)[q - 3][...]
            data[q, 8:24, 24:32] = hi[q]

    by_parity(place[1], sides)

    def act(even):
        up, down = (near, far) if even else (far, near)
        for q, at, rows in MESSAGE:
            down[at : at + rows] = data[q, 8 : 8 + rows]
            up[at : at + rows] = data[q, 24 - rows : 24]

    by_parity(place[0], act)


FINE = Level(1.0, 128, 30, 32)
FINE_UP = Level(1.0, 128, 22, 24)
MIDDLE = Level(0.25, 64, 14, 32)
MIDDLE_UP = Level(0.25, 64, 10, 24, 5)
COARSE = Level(0.0625, 32, 8, 48, 8)
COARSE_UP = Level(0.0625, 32, 8, 32, 8)
LAST = Level(0.015625, 16, 2, 24)


def coef_shapes(level):
    return [level.shape()] * 7


def fine_inside(place):
    y = place[1] * 16 - HALO + row_of((32, LANES))
    fits = (y >= 0) & (y < place[3] * 16)

    def inside(i):
        x = place[0] * 16 + i - HALO
        return fits & (x >= 0) & (x < place[2] * 16)

    return inside


def fine_take(data, message, low):
    zero = jnp.zeros((32, LANES), F32)
    for q, at, rows in MESSAGE:
        start = 8 - rows if low else 24
        data[q, start : start + rows] = message[at : at + rows]
        if rows < 8:
            data[q, 0 if low else 31] = zero


def fine_pass(place, refs, pair, ranges, known):
    data, kept, s0, d0, t0, resid, wide, saved = refs
    coef = [kept.at[j] for j in range(7)]
    setup(FINE, lambda i: data[3, i], lambda i: data[4, i], coef, fine_inside(place), *ranges[0])
    begin(FINE, data, coef, s0, d0, *ranges[0])
    step(FINE, 1, data, coef, s0, t0, d0, *ranges[1])
    step(FINE, 2, data, coef, t0, s0, d0, *ranges[2])
    step(FINE, 3, data, coef, s0, t0, d0, *ranges[3])
    lo, hi = ranges[3]
    saved[:, lo - 4 : hi - 4] = t0[:, lo:hi, 4:28]
    residual(FINE, data, coef, t0, resid, *ranges[4])
    for q in range(5):
        ref = resid if q < 3 else data
        for t in known[q < 3]:
            half, i = divmod(t, 8)
            pair[t] = ref[q, 2 * t] + ref[q, 2 * t + 1]
            wide[q, i, :, half * LANES : half * LANES + LANES] = pairs(pair, (t,), 0, 16)


def fine_inner(place, given, near, *refs):
    *refs, pair = refs
    data, wide = refs[0], refs[6]
    zero = jnp.zeros((16, LANES), F32)

    def act(even):
        fine_take(data, near, not even)
        for q in range(3):
            for t in (0, 1, 2, 13, 14, 15):
                half, i = divmod(t, 8)
                wide[q, i, :, half * LANES : half * LANES + LANES] = zero
        if even:
            ranges = ((9, 31), (10, 30), (11, 29), (12, 28), (13, 26))
            known = (range(4, 16), range(7, 13))
        else:
            ranges = ((1, 23), (2, 22), (3, 21), (4, 20), (6, 19))
            known = (range(0, 12), range(3, 9))
        fine_pass(place, refs, pair, ranges, known)

    by_parity(place[0], act)


def fine_outer(place, far, *refs):
    *refs, packed, first, second, pair = refs[8:]
    data, wide = refs[0], refs[6]

    def act(even):
        fine_take(data, far, even)
        if even:
            ranges = ((1, 9), (2, 10), (3, 11), (4, 12), (6, 13))
            known = (range(0, 4), range(3, 7))
        else:
            ranges = ((23, 31), (22, 30), (21, 29), (20, 28), (19, 26))
            known = (range(12, 16), range(9, 13))
        fine_pass(place, refs, pair, ranges, known)

    by_parity(place[0], act)
    matrix = pick(
        2 * LANES, LANES, lambda a, b: (a % LANES) // 2 + 64 * (a // LANES) == b, 0.125
    )
    packed[...] = mix(wide[...].reshape(5 * 8 * 16, 2 * LANES), matrix).reshape(5, 8, 16, LANES)

    def send(even):
        left, right = (second, first) if even else (first, second)
        for q in range(5):
            skip = 1 if q < 3 else 2
            left[q] = packed[q, :, 4 + skip : 12 + skip]
            right[q] = packed[q, :, 4 - skip : 12 - skip]

    by_parity(place[1], send)


def fine_trim(place, data, kept, data_up, kept_up):
    for q in range(3):
        data_up[q] = data[q, 4:28, 4:28]
    for j in range(7):
        kept_up[j] = kept[j, 4:28, 4:28]


def middle_cut(place, own, first, second, trimmed, near, far, centre):
    low = lane_of((32, LANES)) < 64
    zero = jnp.zeros((4, LANES), F32)

    def sides(even):
        left, right = (second, first) if even else (first, second)
        for q in range(5):
            skip = 1 if q < 3 else 2
            for i in range(8):
                centre[q, i, 0 : 4 - skip] = zero[0 : 4 - skip]
                centre[q, i, 4 - skip : 12 - skip] = left[q, i]
                centre[q, i, 12 - skip : 20 + skip] = own[q, i, 4 - skip : 12 + skip]
                centre[q, i, 20 + skip : 28 + skip] = right[q, i]
                centre[q, i, 28 + skip : 32] = zero[0 : 4 - skip]

    by_parity(place[1], sides)

    def at(q, x, half):
        value = centre[q, x + 4 if x < 4 else x - 4]
        return value if (x >= 4) == (half == 1) else pltpu.roll(value, 64, 1)

    def act(even):
        up, down = (near, far) if even else (far, near)
        for q in range(5):
            skip = 1 if q < 3 else 2
            for t in range(4):
                up[q, t] = jnp.where(low, at(q, t - skip, 0), at(q, t - skip + 4, 1))
                down[q, t] = jnp.where(low, at(q, t + skip, 0), at(q, t + skip + 4, 1))

    by_parity(place[0], act)


def middle_inside(place):
    y = place[1] * 8 - SKIRT + row_of((32, LANES))
    fits = (y >= 0) & (y < place[3] * 8)
    x0 = place[0] * 8 - NEAR + 14 * (lane_of((32, LANES)) // 64)

    def inside(i):
        x = x0 + (i - 1)
        return fits & (x >= 0) & (x < place[2] * 8)

    return inside


def middle_join(centre, lo, hi, data):
    low = lane_of((32, LANES)) < 64
    zero = jnp.zeros((32, LANES), F32)

    def moved(ref, q, t, half):
        value = ref[q, t % 4]
        return value if t // 4 == half else pltpu.roll(value, 64, 1)

    for q in range(5):
        skip = 1 if q < 3 else 2
        for i in range(14):
            t = i - (2 - skip)
            if t < 0:
                a = zero
            elif t < 8:
                a = moved(lo, q, t, 0)
            else:
                a = centre[q, i - 6]
            t = i - (4 + skip)
            if t < 0:
                b = centre[q, i]
            elif t < 8:
                b = moved(hi, q, t, 1)
            else:
                b = zero
            data[q, i + 1] = jnp.where(low, a, b)
        ghosts(MIDDLE, data, (q,))


def middle_down(place, centre, near, far, data, saved, packed, kept, s1, d1, t1, pair, sums):
    coef = [kept.at[j] for j in range(7)]
    lane = lane_of((32, LANES))
    low = lane < 64
    by_parity(
        place[0],
        lambda even: middle_join(centre, *((far, near) if even else (near, far)), data),
    )
    setup(MIDDLE, lambda i: data[3, i], lambda i: data[4, i], coef, middle_inside(place), 1, 15)
    begin(MIDDLE, data, coef, s1, d1, 1, 15)
    step(MIDDLE, 1, data, coef, s1, t1, d1, 1, 15)
    step(MIDDLE, 2, data, coef, t1, s1, d1, 1, 15)
    step(MIDDLE, 3, data, coef, s1, saved, d1, 1, 15)
    residual(MIDDLE, data, coef, saved, d1, 11, 15)
    residual(MIDDLE, data, coef, saved, d1, 1, 5)
    for q in range(5):
        from_, at = (d1, q) if q < 3 else (data, q)
        for m in range(2):
            a = from_[at, 11 + 2 * m] + from_[at, 12 + 2 * m]
            b = from_[at, 1 + 2 * m] + from_[at, 2 + 2 * m]
            pair[q, m] = jnp.where(low, a, b)
            sums[q, :, m * LANES : m * LANES + LANES] = pairs(pair, (q, m), 0, 16)
    matrix = pick(
        2 * LANES,
        LANES,
        lambda a, b: (a // LANES) * 32 + ((a % LANES) // 64) * 64 + (a % 64) // 2 == b,
        0.125,
    )
    packed[...] = mix(sums[...].reshape(5 * 16, 2 * LANES), matrix).reshape(5, 16, LANES)


def middle_trim(place, data, saved, kept, data_up, saved_up, kept_up):
    low = lane_of((24, LANES)) < 64
    groups = [(data, data_up, 3), (saved, saved_up, 3), (kept, kept_up, 7)]
    for old, new, count in groups:
        for q in range(count):
            for j in range(12):
                new[q, j] = jnp.where(low, old[q, 4 + j, 2:26], old[q, j, 2:26])


def column_kernel(place, parts, out):
    zero = jnp.zeros((4, LANES), F32)
    for q in range(5):
        out[q, 0:2] = zero[0:2]
        out[q, 46:48] = zero[0:2]
    for d in range(2 * REACH + 1):
        at = place[1] + (d - REACH)
        valid = (at >= 0) & (at < place[3])
        safe = jnp.clip(at, 0, place[3] - 1)
        for q in range(5):
            block = parts[safe, q]
            out[q, 2 + 4 * d : 6 + 4 * d] = jnp.where(valid, block, zero)


def coarse_inside(place):
    sub = row_of((48, LANES))
    y = place[1] * 4 - 22 + sub
    fits = (y >= 0) & (y < place[3] * 4)
    return lambda i: fits


def last_inside(place):
    y = place[1] * 2 - 11 + row_of((24, LANES))
    fits = (y >= 0) & (y < place[3] * 2)
    return lambda i: fits


def climb(place, mine, other, data1, saved1, kept1, data0, saved0, kept0, out, *scratch):
    scratch = list(scratch)

    def take(count):
        got, scratch[:] = scratch[:count], scratch[count:]
        return got

    data2, s2, t2, d2, keep2 = take(5)
    coef2 = take(7)
    sums3 = take(1)[0]
    data3, s3, t3, d3 = take(4)
    coef3 = take(7)
    grown3, grown2, grown1 = take(3)
    s1, t1, d1 = take(3)
    s0, t0, d0 = take(3)
    coef1 = [kept1.at[j] for j in range(7)]
    coef0 = [kept0.at[j] for j in range(7)]

    group = lane_of((48, LANES)) // 32

    def act(even):
        order = (mine, other) if even else (other, mine)
        for q in range(5):
            for i in range(8):
                row = None
                for g in range(4):
                    block = order[i // 4][g, q]
                    shift = ((g - i % 4) * 32) % LANES
                    block = pltpu.roll(block, shift, 1) if shift else block
                    row = block if row is None else jnp.where(group == g, block, row)
                data2[q, i + 1] = row
            ghosts(COARSE, data2, (q,))

    by_parity(place[0], act)
    setup(COARSE, lambda i: data2[3, i], lambda i: data2[4, i], coef2, coarse_inside(place), 1, 9)
    begin(COARSE, data2, coef2, s2, d2, 1, 9)
    step(COARSE, 1, data2, coef2, s2, t2, d2, 1, 9)
    step(COARSE, 2, data2, coef2, t2, s2, d2, 1, 9)
    step(COARSE, 3, data2, coef2, s2, keep2, d2, 1, 9)
    residual(COARSE, data2, coef2, keep2, d2, 1, 9)

    pair = s2.at[0]
    for q in range(5):
        from_ = d2 if q < 3 else data2
        for t in range(4):
            half, i = divmod(t, 2)
            pair[t] = from_[q, 1 + 2 * t] + from_[q, 2 + 2 * t]
            sums3[q, i, :, half * LANES : half * LANES + LANES] = pairs(pair, (t,), 0, 24)
    matrix = pick(
        2 * LANES,
        LANES,
        lambda a, b: (2 * ((a % LANES) // 32) + a // LANES) * 16 + (a % 32) // 2 == b,
        0.125,
    )
    shrunk = mix(sums3[...].reshape(5 * 2 * 24, 2 * LANES), matrix).reshape(5, 2, 24, LANES)
    for q in range(5):
        for i in range(2):
            data3[q, i + 1] = shrunk[q, i]
        ghosts(LAST, data3, (q,))
    setup(LAST, lambda i: data3[3, i], lambda i: data3[4, i], coef3, last_inside(place), 1, 3)
    begin(LAST, data3, coef3, s3, d3, 1, 3)
    step(LAST, 1, data3, coef3, s3, t3, d3, 1, 3)
    step(LAST, 2, data3, coef3, t3, s3, d3, 1, 3)
    step(LAST, 3, data3, coef3, s3, t3, d3, 1, 3)

    data2u, s2u, t2u, d2u = (ref.at[:, :, 8:40] for ref in (data2, s2, t2, d2))
    coef2u = [ref.at[:, 8:40] for ref in coef2]
    matrix = pick(
        LANES,
        2 * LANES,
        lambda a, b: (2 * ((b % LANES) // 32) + b // LANES == a // 16) & ((b % 32) // 2 == a % 16),
        1.0,
    )
    flat = jnp.concatenate([t3[c, i + 1] for c in range(3) for i in range(2)], axis=0)
    wide = mix(flat, matrix)
    for c in range(3):
        for t in range(4):
            half, i = divmod(t, 2)
            at = (c * 2 + i) * 24
            piece = wide[at : at + 24, half * LANES : half * LANES + LANES]
            grown3[c, t, pl.ds(0, 24, 2)] = piece
            grown3[c, t, pl.ds(1, 24, 2)] = piece
            more = grown3[c, t, 8:40]
            s2u[c, 1 + 2 * t] = keep2[c, 1 + 2 * t, 8:40] + more
            s2u[c, 2 + 2 * t] = keep2[c, 2 + 2 * t, 8:40] + more
        ghosts(COARSE_UP, s2u, (c,))
    step(COARSE_UP, 0, data2u, coef2u, s2u, t2u, d2u, 1, 9)
    step(COARSE_UP, 1, data2u, coef2u, t2u, s2u, d2u, 1, 9)
    step(COARSE_UP, 2, data2u, coef2u, s2u, t2u, d2u, 1, 9)
    step(COARSE_UP, 3, data2u, coef2u, t2u, s2u, d2u, 1, 9)

    matrix = pick(
        LANES,
        LANES,
        lambda a, b: (a < 64) & (b // 64 == a // 32) & ((b % 64) // 2 == a % 32),
        1.0,
    )
    small = lane_of((16, LANES)) < 32

    def window(c, x, slot):
        valid = (x >= 0) & (x < place[2] * 4)
        safe = jnp.clip(x, 0, place[2] * 4 - 1)
        value = s2[c, 1 + safe % 8, 16:32]
        value = pltpu.roll(value, (slot * 32 + LANES - (safe // 8) * 32) % LANES, 1)
        return jnp.where(valid, value, 0.0)

    pieces = []
    for c in range(3):
        for m in range(5):
            x = place[0] * 4 - 3 + m
            pieces.append(jnp.where(small, window(c, x, 0), window(c, x + 5, 1)))
    wide = mix(jnp.concatenate(pieces, axis=0), matrix)
    for c in range(3):
        for m in range(5):
            at = (c * 5 + m) * 16
            piece = wide[at : at + 16]
            grown2[c, m, pl.ds(0, 16, 2)] = piece
            grown2[c, m, pl.ds(1, 16, 2)] = piece
            more = grown2[c, m, 2:26]
            s1[c, 1 + 2 * m] = saved1[c, 1 + 2 * m] + more
            s1[c, 2 + 2 * m] = saved1[c, 2 + 2 * m] + more
        ghosts(MIDDLE_UP, s1, (c,))
    step(MIDDLE_UP, 0, data1, coef1, s1, t1, d1, 1, 11)
    step(MIDDLE_UP, 1, data1, coef1, t1, s1, d1, 1, 11)
    step(MIDDLE_UP, 2, data1, coef1, s1, t1, d1, 1, 11)
    step(MIDDLE_UP, 3, data1, coef1, t1, s1, d1, 1, 11)

    for half in range(2):
        matrix = pick(LANES, LANES, lambda a, b: a == 64 * half + b // 2, 1.0)
        rows = [5 + t for t in range(6)] if half == 0 else [1 + t for t in range(6)]
        flat = jnp.concatenate([s1[c, i, 8:24] for c in range(3) for i in rows], axis=0)
        wide = mix(flat, matrix)
        for c in range(3):
            for t in range(6):
                at = (c * 6 + t) * 16
                piece = wide[at : at + 16]
                grown1[c, t, pl.ds(0, 16, 2)] = piece
                grown1[c, t, pl.ds(1, 16, 2)] = piece
                more = grown1[c, t, 0:24]
                row = 2 * (t + 6 * half)
                s0[c, row] = saved0[c, row] + more
                s0[c, row + 1] = saved0[c, row + 1] + more
    step(FINE_UP, 0, data0, coef0, s0, t0, d0, 1, 23)
    step(FINE_UP, 1, data0, coef0, t0, s0, d0, 2, 22)
    step(FINE_UP, 2, data0, coef0, s0, t0, d0, 3, 21)
    keep, gain = STEPS[3]

    def emit(i, c, u, resid, scaled):
        move = scaled * resid + keep * d0[c, i]
        out[c, i - 4] = (u + move)[4:20]

    sweep(FINE_UP, data0, coef0, t0, 4, 20, lambda i: gain * coef0[6][i], emit)


def swap(value, axis, first):
    count = lax.axis_size(axis)
    ends = [(i, i + 1) for i in range(first, count - 1, 2)]
    return lax.ppermute(value, axis, ends + [(b, a) for a, b in ends])


def on_device(right_side, stiffness, reaction):
    bricks = lax.axis_size("brick")
    count = lax.axis_size("grp")
    place = jnp.stack(
        [lax.axis_index("grp"), lax.axis_index("brick"), jnp.int32(count), jnp.int32(bricks)]
    ).astype(jnp.int32)
    local = (right_side, stiffness, reaction)
    first, second = cut(place, *local)
    first = swap(first, "brick", 0)
    second = swap(second, "brick", 1)
    data0, near, far = call(
        join_kernel,
        [FINE.shape(5)] + [(36, 32, 128)] * 2,
        [],
        place,
        *local,
        first,
        second,
        name="join0",
    )
    far_in = swap(far, "grp", 1)
    near_in = swap(near, "grp", 0)
    states = [FINE.shape(5), FINE.shape(7)] + [FINE.shape(3)] * 4
    states += [(5, 8, 16, 256), (3, 24, 24, 128)]
    pair = [(16, 32, 128)]
    inner = call(fine_inner, states, pair, place, data0, near_in, name="inner0", aliases={1: 0})
    data0, kept0, _, _, _, _, _, saved0, packed1, first, second = call(
        fine_outer,
        states + [(5, 8, 16, 128)] + [(5, 8, 8, 128)] * 2,
        pair,
        place,
        far_in,
        *inner,
        name="outer0",
        aliases={2 + j: j for j in range(8)},
    )
    first = swap(first, "brick", 0)
    second = swap(second, "brick", 1)
    data0, kept0 = call(
        fine_trim, [FINE_UP.shape(3), FINE_UP.shape(7)], [], place, data0, kept0, name="trim0"
    )
    near, far, centre = call(
        middle_cut,
        [(5, 4, 32, 128)] * 2 + [(5, 8, 32, 128)],
        [],
        place,
        packed1,
        first,
        second,
        data0,
        name="cut1",
    )
    far_in = swap(far, "grp", 1)
    near_in = swap(near, "grp", 0)
    data1, saved1, packed2, kept1 = call(
        middle_down,
        [MIDDLE.shape(5), MIDDLE.shape(3), (5, 16, 128), MIDDLE.shape(7)],
        [MIDDLE.shape(3)] * 3 + [(5, 2, 32, 128), (5, 16, 256)],
        place,
        centre,
        near_in,
        far_in,
        name="down1",
    )
    block = packed2[:, 6:10]
    parts = lax.all_to_all(jnp.broadcast_to(block[None], (bricks, 5, 4, 128)), "brick", 0, 0)
    (column,) = call(column_kernel, [(5, 48, 128)], [], place, parts, name="column")
    mine = lax.all_to_all(
        jnp.broadcast_to(column[None], (count // 2, 5, 48, 128)),
        "grp",
        0,
        0,
        axis_index_groups=[list(range(core, count, 2)) for core in range(2)],
    )
    other = swap(mine, "grp", 0)
    data1, saved1, kept1 = call(
        middle_trim,
        [MIDDLE_UP.shape(3)] * 2 + [MIDDLE_UP.shape(7)],
        [],
        place,
        data1,
        saved1,
        kept1,
        name="trim1",
    )
    coarse = [COARSE.shape(5)] + [COARSE.shape(3)] * 4 + coef_shapes(COARSE)
    last = [(5, 2, 24, 256), LAST.shape(5)] + [LAST.shape(3)] * 3 + coef_shapes(LAST)
    grown = [(3, 4, 48, 128), (3, 5, 32, 128), (3, 6, 32, 128)]
    (answer,) = call(
        climb,
        [(3, 16, 16, 128)],
        coarse + last + grown + [MIDDLE_UP.shape(3)] * 3 + [FINE_UP.shape(3)] * 3,
        place,
        mine,
        other,
        data1,
        saved1,
        kept1,
        data0,
        saved0,
        kept0,
        name="climb",
    )
    return answer


def solution(mesh):
    in_specs = (P(None, "grp", "brick", None), P("grp", "brick", None), P("grp", "brick", None))
    out_specs = P(None, "grp", "brick", None)
    return jax.shard_map(
        on_device, mesh=mesh, in_specs=in_specs, out_specs=out_specs, check_vma=False
    )
```

```python
import jax
import jax.numpy as jnp
from jax import lax
from jax.experimental import pallas as pl
from jax.experimental.pallas import tpu as pltpu
from jax.sharding import PartitionSpec as P

BETA = 1.0
THETA = 1.5
DELTA = 1.0
SIGMA = 1.5
LANES = 128
HALO = 8
NEAR = 10
SKIRT = 12
REACH = 5
CUT_LIMIT = 28 * 2**20
F32 = jnp.float32


def rate_list():
    rates = [1.0 / SIGMA]
    for number in range(3):
        rates.append(1.0 / (2.0 * SIGMA - rates[-1]))
    return rates


RATES = rate_list()
STEPS = [(0.0, 1.0 / THETA)] + [
    (RATES[k] * RATES[k - 1], 2.0 * RATES[k] / DELTA) for k in (1, 2, 3)
]


def lane_of(shape):
    return lax.broadcasted_iota(jnp.int32, shape, len(shape) - 1)


def row_of(shape):
    return lax.broadcasted_iota(jnp.int32, shape, len(shape) - 2)


def ahead_y(v):
    return pltpu.roll(v, v.shape[0] - 1, 0)


def behind_y(v):
    return pltpu.roll(v, 1, 0)


def ahead_z(v):
    return pltpu.roll(v, LANES - 1, 1)


def behind_z(v):
    return pltpu.roll(v, 1, 1)


class Level:
    def __init__(self, scale, depth, rows, height, unroll=4):
        self.unroll = unroll
        self.scale = scale
        self.depth = depth
        self.groups = LANES // depth
        self.rows = rows
        self.height = height

    def shape(self, *lead):
        return (*lead, self.rows + 2, self.height, LANES)

    def lanes(self):
        z = lane_of((self.height, LANES)) % self.depth
        return z == 0, z == self.depth - 1


def ghosts(level, ref, index=()):
    if level.groups == 1:
        return
    lane = lane_of((level.height, LANES))
    first = ref[(*index, 1)]
    last = ref[(*index, level.rows)]
    ref[(*index, 0)] = jnp.where(lane < level.depth, 0.0, pltpu.roll(last, level.depth, 1))
    ref[(*index, level.rows + 1)] = jnp.where(
        lane >= LANES - level.depth, 0.0, pltpu.roll(first, LANES - level.depth, 1)
    )


def setup(level, stiff, react, coef, inside, lo, hi):
    kx, ky, kym, kz, kzm, diag, inv = coef
    half = 0.5 * level.scale
    front, back = level.lanes()
    kx[lo - 1] = half * (stiff(lo - 1) + stiff(lo))

    def body(i, _):
        centre = stiff(i)
        xp = half * (centre + stiff(i + 1))
        xm = kx[i - 1]
        yp = half * (centre + ahead_y(centre))
        ym = behind_y(yp)
        zp = half * (centre + jnp.where(back, 0.0, ahead_z(centre)))
        zm = half * (centre + jnp.where(front, 0.0, behind_z(centre)))
        total = ((xp + xm) + (yp + ym)) + (zp + zm) + react(i)
        kx[i] = xp
        ky[i] = yp
        kym[i] = ym
        kz[i] = jnp.where(back, 0.0, zp)
        kzm[i] = jnp.where(front, 0.0, zm)
        diag[i] = total
        inv[i] = jnp.where(inside(i), 1.0 / (total + 2.0 * BETA * level.scale), 0.0)
        return 0

    lax.fori_loop(lo, hi, body, 0, unroll=8 if hi - lo == 8 else 7 if hi - lo == 14 else 4)


def begin(level, src, coef, state, direction, lo, hi):
    inv = coef[6]

    def body(i, _):
        scaled = inv[i] * (1.0 / THETA)
        for c in range(3):
            value = scaled * src[c, i]
            state[c, i] = value
            direction[c, i] = value
        return 0

    lax.fori_loop(lo, hi, body, 0, unroll=8 if hi - lo == 8 else 7 if hi - lo == 14 else 4)
    for c in range(3):
        ghosts(level, state, (c,))


def sweep(level, src, coef, state, lo, hi, prepare, emit):
    kx, ky, kym, kz, kzm, diag, inv = coef
    front, back = level.lanes()
    bulk = BETA * level.scale

    def spread(i):
        ux, uy, uz = state[0, i], state[1, i], state[2, i]
        return (
            (state[0, i + 1] - ux)
            + (ahead_y(uy) - uy)
            + (jnp.where(back, 0.0, ahead_z(uz)) - uz)
        ) * bulk

    def body(i, before):
        here = spread(i)
        extra = prepare(i)
        for c in range(3):
            u = state[c, i]
            flux = kx[i] * state[c, i + 1] + kx[i - 1] * state[c, i - 1]
            flux = flux + (ky[i] * ahead_y(u) + kym[i] * behind_y(u))
            flux = flux + (kz[i] * ahead_z(u) + kzm[i] * behind_z(u))
            if c == 0:
                other = before
            elif c == 1:
                other = behind_y(here)
            else:
                other = jnp.where(front, bulk * u, behind_z(here))
            resid = src[c, i] - diag[i] * u + flux + (here - other)
            emit(i, c, u, resid, extra)
        return here

    lax.fori_loop(lo, hi, body, spread(lo - 1), unroll=level.unroll)


def step(level, number, src, coef, state, fresh, direction, lo, hi):
    keep, gain = STEPS[number]
    inv = coef[6]

    def emit(i, c, u, resid, scaled):
        move = scaled * resid
        if number > 0:
            move = move + keep * direction[c, i]
        direction[c, i] = move
        fresh[c, i] = u + move

    sweep(level, src, coef, state, lo, hi, lambda i: gain * inv[i], emit)
    for c in range(3):
        ghosts(level, fresh, (c,))


def residual(level, src, coef, state, out, lo, hi):
    def emit(i, c, u, resid, extra):
        out[c, i] = resid

    sweep(level, src, coef, state, lo, hi, lambda i: None, emit)


def pick(rows, cols, rule, value):
    shape = (rows, cols)
    return jnp.where(rule(row_of(shape), lane_of(shape)), value, 0.0).astype(F32)


def mix(values, matrix):
    return jnp.dot(values, matrix, precision=lax.Precision.HIGH, preferred_element_type=F32)


def pairs(ref, index, start, count):
    return ref[(*index, pl.ds(start, count, 2))] + ref[(*index, pl.ds(start + 1, count, 2))]


def vmem(count):
    return [pl.BlockSpec(memory_space=pltpu.VMEM)] * count


def call(kernel, outs, scratch, *args, name, aliases={}):
    smem = pl.BlockSpec(memory_space=pltpu.SMEM)
    return pl.pallas_call(
        kernel,
        out_shape=[jax.ShapeDtypeStruct(s, F32) for s in outs],
        in_specs=[smem] + vmem(len(args) - 1),
        out_specs=vmem(len(outs)),
        scratch_shapes=[pltpu.VMEM(s, F32) for s in scratch],
        compiler_params=pltpu.CompilerParams(vmem_limit_bytes=28 * 2**20),
        input_output_aliases=aliases,
        name=name,
    )(*args)


def by_parity(index, act):
    odd = index % 2

    @pl.when(odd == 0)
    def _():
        act(True)

    @pl.when(odd == 1)
    def _():
        act(False)


def cut_kernel(place, f, k, r, first, second, sems):
    def act(even):
        copies = []
        for side, out in enumerate((second, first) if even else (first, second)):
            rows = pl.ds(HALO * side, HALO)
            copies += [
                pltpu.make_async_copy(f.at[:, :, rows], out.at[0:3], sems.at[3 * side]),
                pltpu.make_async_copy(k.at[:, rows], out.at[3], sems.at[3 * side + 1]),
                pltpu.make_async_copy(r.at[:, rows], out.at[4], sems.at[3 * side + 2]),
            ]
        for copy in copies:
            copy.start()
        for copy in copies:
            copy.wait()

    by_parity(place[1], act)


def cut(place, f, k, r):
    return pl.pallas_call(
        cut_kernel,
        out_shape=[jax.ShapeDtypeStruct((5, 16, HALO, LANES), F32)] * 2,
        in_specs=[pl.BlockSpec(memory_space=pltpu.SMEM)]
        + [pl.BlockSpec(memory_space=pltpu.HBM)] * 3,
        out_specs=vmem(2),
        scratch_shapes=[pltpu.SemaphoreType.DMA((6,))],
        compiler_params=pltpu.CompilerParams(vmem_limit_bytes=CUT_LIMIT),
        name="cut0",
    )(place, f, k, r)


MESSAGE = [(0, 0, 7), (1, 7, 7), (2, 14, 7), (4, 21, 7), (3, 28, 8)]


def join_kernel(place, f, k, r, first, second, data, near, far):
    def sides(even):
        lo, hi = (second, first) if even else (first, second)
        for q in range(5):
            data[q, 8:24, 0:8] = lo[q]
            data[q, 8:24, 8:24] = f[q] if q < 3 else (k, r)[q - 3][...]
            data[q, 8:24, 24:32] = hi[q]

    by_parity(place[1], sides)

    def act(even):
        up, down = (near, far) if even else (far, near)
        for q, at, rows in MESSAGE:
            down[at : at + rows] = data[q, 8 : 8 + rows]
            up[at : at + rows] = data[q, 24 - rows : 24]

    by_parity(place[0], act)


FINE = Level(1.0, 128, 30, 32)
FINE_UP = Level(1.0, 128, 22, 24)
MIDDLE = Level(0.25, 64, 14, 32)
MIDDLE_UP = Level(0.25, 64, 10, 24, 5)
COARSE = Level(0.0625, 32, 8, 48, 8)
COARSE_UP = Level(0.0625, 32, 8, 32, 8)
LAST = Level(0.015625, 16, 2, 24)


def coef_shapes(level):
    return [level.shape()] * 7


def fine_inside(place):
    y = place[1] * 16 - HALO + row_of((32, LANES))
    fits = (y >= 0) & (y < place[3] * 16)

    def inside(i):
        x = place[0] * 16 + i - HALO
        return fits & (x >= 0) & (x < place[2] * 16)

    return inside


def fine_take(data, message, low):
    zero = jnp.zeros((32, LANES), F32)
    for q, at, rows in MESSAGE:
        start = 8 - rows if low else 24
        data[q, start : start + rows] = message[at : at + rows]
        if rows < 8:
            data[q, 0 if low else 31] = zero


def fine_pass(place, refs, pair, ranges, known):
    data, kept, s0, d0, t0, resid, wide, saved = refs
    coef = [kept.at[j] for j in range(7)]
    setup(FINE, lambda i: data[3, i], lambda i: data[4, i], coef, fine_inside(place), *ranges[0])
    begin(FINE, data, coef, s0, d0, *ranges[0])
    step(FINE, 1, data, coef, s0, t0, d0, *ranges[1])
    step(FINE, 2, data, coef, t0, s0, d0, *ranges[2])
    step(FINE, 3, data, coef, s0, t0, d0, *ranges[3])
    lo, hi = ranges[3]
    saved[:, lo - 4 : hi - 4] = t0[:, lo:hi, 4:28]
    residual(FINE, data, coef, t0, resid, *ranges[4])
    for q in range(5):
        ref = resid if q < 3 else data
        for t in known[q < 3]:
            half, i = divmod(t, 8)
            pair[t] = ref[q, 2 * t] + ref[q, 2 * t + 1]
            wide[q, i, :, half * LANES : half * LANES + LANES] = pairs(pair, (t,), 0, 16)


def fine_inner(place, given, near, *refs):
    *refs, pair = refs
    data, wide = refs[0], refs[6]
    zero = jnp.zeros((16, LANES), F32)

    def act(even):
        fine_take(data, near, not even)
        for q in range(3):
            for t in (0, 1, 2, 13, 14, 15):
                half, i = divmod(t, 8)
                wide[q, i, :, half * LANES : half * LANES + LANES] = zero
        if even:
            ranges = ((9, 31), (10, 30), (11, 29), (12, 28), (13, 26))
            known = (range(4, 16), range(7, 13))
        else:
            ranges = ((1, 23), (2, 22), (3, 21), (4, 20), (6, 19))
            known = (range(0, 12), range(3, 9))
        fine_pass(place, refs, pair, ranges, known)

    by_parity(place[0], act)


def fine_outer(place, far, *refs):
    *refs, packed, first, second, pair = refs[8:]
    data, wide = refs[0], refs[6]

    def act(even):
        fine_take(data, far, even)
        if even:
            ranges = ((1, 9), (2, 10), (3, 11), (4, 12), (6, 13))
            known = (range(0, 4), range(3, 7))
        else:
            ranges = ((23, 31), (22, 30), (21, 29), (20, 28), (19, 26))
            known = (range(12, 16), range(9, 13))
        fine_pass(place, refs, pair, ranges, known)

    by_parity(place[0], act)
    matrix = pick(
        2 * LANES, LANES, lambda a, b: (a % LANES) // 2 + 64 * (a // LANES) == b, 0.125
    )
    packed[...] = mix(wide[...].reshape(5 * 8 * 16, 2 * LANES), matrix).reshape(5, 8, 16, LANES)

    def send(even):
        left, right = (second, first) if even else (first, second)
        for q in range(5):
            skip = 1 if q < 3 else 2
            left[q] = packed[q, :, 4 + skip : 12 + skip]
            right[q] = packed[q, :, 4 - skip : 12 - skip]

    by_parity(place[1], send)


def fine_trim(place, data, kept, data_up, kept_up):
    for q in range(3):
        data_up[q] = data[q, 4:28, 4:28]
    for j in range(7):
        kept_up[j] = kept[j, 4:28, 4:28]


def middle_cut(place, own, first, second, trimmed, near, far, centre):
    low = lane_of((32, LANES)) < 64
    zero = jnp.zeros((4, LANES), F32)

    def sides(even):
        left, right = (second, first) if even else (first, second)
        for q in range(5):
            skip = 1 if q < 3 else 2
            for i in range(8):
                centre[q, i, 0 : 4 - skip] = zero[0 : 4 - skip]
                centre[q, i, 4 - skip : 12 - skip] = left[q, i]
                centre[q, i, 12 - skip : 20 + skip] = own[q, i, 4 - skip : 12 + skip]
                centre[q, i, 20 + skip : 28 + skip] = right[q, i]
                centre[q, i, 28 + skip : 32] = zero[0 : 4 - skip]

    by_parity(place[1], sides)

    def at(q, x, half):
        value = centre[q, x + 4 if x < 4 else x - 4]
        return value if (x >= 4) == (half == 1) else pltpu.roll(value, 64, 1)

    def act(even):
        up, down = (near, far) if even else (far, near)
        for q in range(5):
            skip = 1 if q < 3 else 2
            for t in range(4):
                up[q, t] = jnp.where(low, at(q, t - skip, 0), at(q, t - skip + 4, 1))
                down[q, t] = jnp.where(low, at(q, t + skip, 0), at(q, t + skip + 4, 1))

    by_parity(place[0], act)


def middle_inside(place):
    y = place[1] * 8 - SKIRT + row_of((32, LANES))
    fits = (y >= 0) & (y < place[3] * 8)
    x0 = place[0] * 8 - NEAR + 14 * (lane_of((32, LANES)) // 64)

    def inside(i):
        x = x0 + (i - 1)
        return fits & (x >= 0) & (x < place[2] * 8)

    return inside


def middle_join(centre, lo, hi, data):
    low = lane_of((32, LANES)) < 64
    zero = jnp.zeros((32, LANES), F32)

    def moved(ref, q, t, half):
        value = ref[q, t % 4]
        return value if t // 4 == half else pltpu.roll(value, 64, 1)

    for q in range(5):
        skip = 1 if q < 3 else 2
        for i in range(14):
            t = i - (2 - skip)
            if t < 0:
                a = zero
            elif t < 8:
                a = moved(lo, q, t, 0)
            else:
                a = centre[q, i - 6]
            t = i - (4 + skip)
            if t < 0:
                b = centre[q, i]
            elif t < 8:
                b = moved(hi, q, t, 1)
            else:
                b = zero
            data[q, i + 1] = jnp.where(low, a, b)
        ghosts(MIDDLE, data, (q,))


def middle_down(place, centre, near, far, data, saved, packed, kept, s1, d1, t1, pair, sums):
    coef = [kept.at[j] for j in range(7)]
    lane = lane_of((32, LANES))
    low = lane < 64
    by_parity(
        place[0],
        lambda even: middle_join(centre, *((far, near) if even else (near, far)), data),
    )
    setup(MIDDLE, lambda i: data[3, i], lambda i: data[4, i], coef, middle_inside(place), 1, 15)
    begin(MIDDLE, data, coef, s1, d1, 1, 15)
    step(MIDDLE, 1, data, coef, s1, t1, d1, 1, 15)
    step(MIDDLE, 2, data, coef, t1, s1, d1, 1, 15)
    step(MIDDLE, 3, data, coef, s1, saved, d1, 1, 15)
    residual(MIDDLE, data, coef, saved, d1, 11, 15)
    residual(MIDDLE, data, coef, saved, d1, 1, 5)
    for q in range(5):
        from_, at = (d1, q) if q < 3 else (data, q)
        for m in range(2):
            a = from_[at, 11 + 2 * m] + from_[at, 12 + 2 * m]
            b = from_[at, 1 + 2 * m] + from_[at, 2 + 2 * m]
            pair[q, m] = jnp.where(low, a, b)
            sums[q, :, m * LANES : m * LANES + LANES] = pairs(pair, (q, m), 0, 16)
    matrix = pick(
        2 * LANES,
        LANES,
        lambda a, b: (a // LANES) * 32 + ((a % LANES) // 64) * 64 + (a % 64) // 2 == b,
        0.125,
    )
    packed[...] = mix(sums[...].reshape(5 * 16, 2 * LANES), matrix).reshape(5, 16, LANES)


def middle_trim(place, data, saved, kept, data_up, saved_up, kept_up):
    low = lane_of((24, LANES)) < 64
    groups = [(data, data_up, 3), (saved, saved_up, 3), (kept, kept_up, 7)]
    for old, new, count in groups:
        for q in range(count):
            for j in range(12):
                new[q, j] = jnp.where(low, old[q, 4 + j, 2:26], old[q, j, 2:26])


def column_kernel(place, parts, out):
    zero = jnp.zeros((4, LANES), F32)
    for q in range(5):
        out[q, 0:2] = zero[0:2]
        out[q, 46:48] = zero[0:2]
    for d in range(2 * REACH + 1):
        at = place[1] + (d - REACH)
        valid = (at >= 0) & (at < place[3])
        safe = jnp.clip(at, 0, place[3] - 1)
        for q in range(5):
            block = parts[safe, q]
            out[q, 2 + 4 * d : 6 + 4 * d] = jnp.where(valid, block, zero)


def coarse_inside(place):
    sub = row_of((48, LANES))
    y = place[1] * 4 - 22 + sub
    fits = (y >= 0) & (y < place[3] * 4)
    return lambda i: fits


def last_inside(place):
    y = place[1] * 2 - 11 + row_of((24, LANES))
    fits = (y >= 0) & (y < place[3] * 2)
    return lambda i: fits


def climb(place, mine, other, data1, saved1, kept1, data0, saved0, kept0, out, *scratch):
    scratch = list(scratch)

    def take(count):
        got, scratch[:] = scratch[:count], scratch[count:]
        return got

    data2, s2, t2, d2, keep2 = take(5)
    coef2 = take(7)
    sums3 = take(1)[0]
    data3, s3, t3, d3 = take(4)
    coef3 = take(7)
    grown3, grown2, grown1 = take(3)
    s1, t1, d1 = take(3)
    s0, t0, d0 = take(3)
    coef1 = [kept1.at[j] for j in range(7)]
    coef0 = [kept0.at[j] for j in range(7)]

    group = lane_of((48, LANES)) // 32

    def act(even):
        order = (mine, other) if even else (other, mine)
        for q in range(5):
            for i in range(8):
                row = None
                for g in range(4):
                    block = order[i // 4][g, q]
                    shift = ((g - i % 4) * 32) % LANES
                    block = pltpu.roll(block, shift, 1) if shift else block
                    row = block if row is None else jnp.where(group == g, block, row)
                data2[q, i + 1] = row
            ghosts(COARSE, data2, (q,))

    by_parity(place[0], act)
    setup(COARSE, lambda i: data2[3, i], lambda i: data2[4, i], coef2, coarse_inside(place), 1, 9)
    begin(COARSE, data2, coef2, s2, d2, 1, 9)
    step(COARSE, 1, data2, coef2, s2, t2, d2, 1, 9)
    step(COARSE, 2, data2, coef2, t2, s2, d2, 1, 9)
    step(COARSE, 3, data2, coef2, s2, keep2, d2, 1, 9)
    residual(COARSE, data2, coef2, keep2, d2, 1, 9)

    pair = s2.at[0]
    for q in range(5):
        from_ = d2 if q < 3 else data2
        for t in range(4):
            half, i = divmod(t, 2)
            pair[t] = from_[q, 1 + 2 * t] + from_[q, 2 + 2 * t]
            sums3[q, i, :, half * LANES : half * LANES + LANES] = pairs(pair, (t,), 0, 24)
    matrix = pick(
        2 * LANES,
        LANES,
        lambda a, b: (2 * ((a % LANES) // 32) + a // LANES) * 16 + (a % 32) // 2 == b,
        0.125,
    )
    shrunk = mix(sums3[...].reshape(5 * 2 * 24, 2 * LANES), matrix).reshape(5, 2, 24, LANES)
    for q in range(5):
        for i in range(2):
            data3[q, i + 1] = shrunk[q, i]
        ghosts(LAST, data3, (q,))
    setup(LAST, lambda i: data3[3, i], lambda i: data3[4, i], coef3, last_inside(place), 1, 3)
    begin(LAST, data3, coef3, s3, d3, 1, 3)
    step(LAST, 1, data3, coef3, s3, t3, d3, 1, 3)
    step(LAST, 2, data3, coef3, t3, s3, d3, 1, 3)
    step(LAST, 3, data3, coef3, s3, t3, d3, 1, 3)

    data2u, s2u, t2u, d2u = (ref.at[:, :, 8:40] for ref in (data2, s2, t2, d2))
    coef2u = [ref.at[:, 8:40] for ref in coef2]
    matrix = pick(
        LANES,
        2 * LANES,
        lambda a, b: (2 * ((b % LANES) // 32) + b // LANES == a // 16) & ((b % 32) // 2 == a % 16),
        1.0,
    )
    flat = jnp.concatenate([t3[c, i + 1] for c in range(3) for i in range(2)], axis=0)
    wide = mix(flat, matrix)
    for c in range(3):
        for t in range(4):
            half, i = divmod(t, 2)
            at = (c * 2 + i) * 24
            piece = wide[at : at + 24, half * LANES : half * LANES + LANES]
            grown3[c, t, pl.ds(0, 24, 2)] = piece
            grown3[c, t, pl.ds(1, 24, 2)] = piece
            more = grown3[c, t, 8:40]
            s2u[c, 1 + 2 * t] = keep2[c, 1 + 2 * t, 8:40] + more
            s2u[c, 2 + 2 * t] = keep2[c, 2 + 2 * t, 8:40] + more
        ghosts(COARSE_UP, s2u, (c,))
    step(COARSE_UP, 0, data2u, coef2u, s2u, t2u, d2u, 1, 9)
    step(COARSE_UP, 1, data2u, coef2u, t2u, s2u, d2u, 1, 9)
    step(COARSE_UP, 2, data2u, coef2u, s2u, t2u, d2u, 1, 9)
    step(COARSE_UP, 3, data2u, coef2u, t2u, s2u, d2u, 1, 9)

    matrix = pick(
        LANES,
        LANES,
        lambda a, b: (a < 64) & (b // 64 == a // 32) & ((b % 64) // 2 == a % 32),
        1.0,
    )
    small = lane_of((16, LANES)) < 32

    def window(c, x, slot):
        valid = (x >= 0) & (x < place[2] * 4)
        safe = jnp.clip(x, 0, place[2] * 4 - 1)
        value = s2[c, 1 + safe % 8, 16:32]
        value = pltpu.roll(value, (slot * 32 + LANES - (safe // 8) * 32) % LANES, 1)
        return jnp.where(valid, value, 0.0)

    pieces = []
    for c in range(3):
        for m in range(5):
            x = place[0] * 4 - 3 + m
            pieces.append(jnp.where(small, window(c, x, 0), window(c, x + 5, 1)))
    wide = mix(jnp.concatenate(pieces, axis=0), matrix)
    for c in range(3):
        for m in range(5):
            at = (c * 5 + m) * 16
            piece = wide[at : at + 16]
            grown2[c, m, pl.ds(0, 16, 2)] = piece
            grown2[c, m, pl.ds(1, 16, 2)] = piece
            more = grown2[c, m, 2:26]
            s1[c, 1 + 2 * m] = saved1[c, 1 + 2 * m] + more
            s1[c, 2 + 2 * m] = saved1[c, 2 + 2 * m] + more
        ghosts(MIDDLE_UP, s1, (c,))
    step(MIDDLE_UP, 0, data1, coef1, s1, t1, d1, 1, 11)
    step(MIDDLE_UP, 1, data1, coef1, t1, s1, d1, 1, 11)
    step(MIDDLE_UP, 2, data1, coef1, s1, t1, d1, 1, 11)
    step(MIDDLE_UP, 3, data1, coef1, t1, s1, d1, 1, 11)

    for half in range(2):
        matrix = pick(LANES, LANES, lambda a, b: a == 64 * half + b // 2, 1.0)
        rows = [5 + t for t in range(6)] if half == 0 else [1 + t for t in range(6)]
        flat = jnp.concatenate([s1[c, i, 8:24] for c in range(3) for i in rows], axis=0)
        wide = mix(flat, matrix)
        for c in range(3):
            for t in range(6):
                at = (c * 6 + t) * 16
                piece = wide[at : at + 16]
                grown1[c, t, pl.ds(0, 16, 2)] = piece
                grown1[c, t, pl.ds(1, 16, 2)] = piece
                more = grown1[c, t, 0:24]
                row = 2 * (t + 6 * half)
                s0[c, row] = saved0[c, row] + more
                s0[c, row + 1] = saved0[c, row + 1] + more
    step(FINE_UP, 0, data0, coef0, s0, t0, d0, 1, 23)
    step(FINE_UP, 1, data0, coef0, t0, s0, d0, 2, 22)
    step(FINE_UP, 2, data0, coef0, s0, t0, d0, 3, 21)
    keep, gain = STEPS[3]

    def emit(i, c, u, resid, scaled):
        move = scaled * resid + keep * d0[c, i]
        out[c, i - 4] = (u + move)[4:20]

    sweep(FINE_UP, data0, coef0, t0, 4, 20, lambda i: gain * coef0[6][i], emit)


def swap(value, axis, first):
    count = lax.axis_size(axis)
    ends = [(i, i + 1) for i in range(first, count - 1, 2)]
    return lax.ppermute(value, axis, ends + [(b, a) for a, b in ends])


def on_device(right_side, stiffness, reaction):
    bricks = lax.axis_size("brick")
    count = lax.axis_size("grp")
    place = jnp.stack(
        [lax.axis_index("grp"), lax.axis_index("brick"), jnp.int32(count), jnp.int32(bricks)]
    ).astype(jnp.int32)
    local = (right_side, stiffness, reaction)
    first, second = cut(place, *local)
    first = swap(first, "brick", 0)
    second = swap(second, "brick", 1)
    data0, near, far = call(
        join_kernel,
        [FINE.shape(5)] + [(36, 32, 128)] * 2,
        [],
        place,
        *local,
        first,
        second,
        name="join0",
    )
    far_in = swap(far, "grp", 1)
    near_in = swap(near, "grp", 0)
    states = [FINE.shape(5), FINE.shape(7)] + [FINE.shape(3)] * 4
    states += [(5, 8, 16, 256), (3, 24, 24, 128)]
    pair = [(16, 32, 128)]
    inner = call(fine_inner, states, pair, place, data0, near_in, name="inner0", aliases={1: 0})
    data0, kept0, _, _, _, _, _, saved0, packed1, first, second = call(
        fine_outer,
        states + [(5, 8, 16, 128)] + [(5, 8, 8, 128)] * 2,
        pair,
        place,
        far_in,
        *inner,
        name="outer0",
        aliases={2 + j: j for j in range(8)},
    )
    first = swap(first, "brick", 0)
    second = swap(second, "brick", 1)
    data0, kept0 = call(
        fine_trim, [FINE_UP.shape(3), FINE_UP.shape(7)], [], place, data0, kept0, name="trim0"
    )
    near, far, centre = call(
        middle_cut,
        [(5, 4, 32, 128)] * 2 + [(5, 8, 32, 128)],
        [],
        place,
        packed1,
        first,
        second,
        data0,
        name="cut1",
    )
    far_in = swap(far, "grp", 1)
    near_in = swap(near, "grp", 0)
    data1, saved1, packed2, kept1 = call(
        middle_down,
        [MIDDLE.shape(5), MIDDLE.shape(3), (5, 16, 128), MIDDLE.shape(7)],
        [MIDDLE.shape(3)] * 3 + [(5, 2, 32, 128), (5, 16, 256)],
        place,
        centre,
        near_in,
        far_in,
        name="down1",
    )
    block = packed2[:, 6:10]
    parts = lax.all_to_all(jnp.broadcast_to(block[None], (bricks, 5, 4, 128)), "brick", 0, 0)
    (column,) = call(column_kernel, [(5, 48, 128)], [], place, parts, name="column")
    mine = lax.all_to_all(
        jnp.broadcast_to(column[None], (count // 2, 5, 48, 128)),
        "grp",
        0,
        0,
        axis_index_groups=[list(range(core, count, 2)) for core in range(2)],
    )
    other = swap(mine, "grp", 0)
    data1, saved1, kept1 = call(
        middle_trim,
        [MIDDLE_UP.shape(3)] * 2 + [MIDDLE_UP.shape(7)],
        [],
        place,
        data1,
        saved1,
        kept1,
        name="trim1",
    )
    coarse = [COARSE.shape(5)] + [COARSE.shape(3)] * 4 + coef_shapes(COARSE)
    last = [(5, 2, 24, 256), LAST.shape(5)] + [LAST.shape(3)] * 3 + coef_shapes(LAST)
    grown = [(3, 4, 48, 128), (3, 5, 32, 128), (3, 6, 32, 128)]
    (answer,) = call(
        climb,
        [(3, 16, 16, 128)],
        coarse + last + grown + [MIDDLE_UP.shape(3)] * 3 + [FINE_UP.shape(3)] * 3,
        place,
        mine,
        other,
        data1,
        saved1,
        kept1,
        data0,
        saved0,
        kept0,
        name="climb",
    )
    return answer


def solution(mesh):
    in_specs = (P(None, "grp", "brick", None), P("grp", "brick", None), P("grp", "brick", None))
    out_specs = P(None, "grp", "brick", None)
    return jax.shard_map(
        on_device, mesh=mesh, in_specs=in_specs, out_specs=out_specs, check_vma=False
    )
```

```python
import jax
import jax.numpy as jnp
from jax import lax
from jax.experimental import pallas as pl
from jax.experimental.pallas import tpu as pltpu
from jax.sharding import PartitionSpec as P

BETA = 1.0
THETA = 1.5
DELTA = 1.0
SIGMA = 1.5
LANES = 128
HALO = 8
NEAR = 10
SKIRT = 12
REACH = 5
CUT_LIMIT = 28 * 2**20
F32 = jnp.float32


def rate_list():
    rates = [1.0 / SIGMA]
    for number in range(3):
        rates.append(1.0 / (2.0 * SIGMA - rates[-1]))
    return rates


RATES = rate_list()
STEPS = [(0.0, 1.0 / THETA)] + [
    (RATES[k] * RATES[k - 1], 2.0 * RATES[k] / DELTA) for k in (1, 2, 3)
]


def lane_of(shape):
    return lax.broadcasted_iota(jnp.int32, shape, len(shape) - 1)


def row_of(shape):
    return lax.broadcasted_iota(jnp.int32, shape, len(shape) - 2)


def ahead_y(v):
    return pltpu.roll(v, v.shape[0] - 1, 0)


def behind_y(v):
    return pltpu.roll(v, 1, 0)


def ahead_z(v):
    return pltpu.roll(v, LANES - 1, 1)


def behind_z(v):
    return pltpu.roll(v, 1, 1)


class Level:
    def __init__(self, scale, depth, rows, height, unroll=4):
        self.unroll = unroll
        self.scale = scale
        self.depth = depth
        self.groups = LANES // depth
        self.rows = rows
        self.height = height

    def shape(self, *lead):
        return (*lead, self.rows + 2, self.height, LANES)

    def lanes(self):
        z = lane_of((self.height, LANES)) % self.depth
        return z == 0, z == self.depth - 1


def ghosts(level, ref, index=()):
    if level.groups == 1:
        return
    lane = lane_of((level.height, LANES))
    first = ref[(*index, 1)]
    last = ref[(*index, level.rows)]
    ref[(*index, 0)] = jnp.where(lane < level.depth, 0.0, pltpu.roll(last, level.depth, 1))
    ref[(*index, level.rows + 1)] = jnp.where(
        lane >= LANES - level.depth, 0.0, pltpu.roll(first, LANES - level.depth, 1)
    )


def setup(level, data, coef, inside, state, direction, lo, hi):
    kx, ky, kym, kz, kzm, diag, inv = coef
    half = 0.5 * level.scale
    front, back = level.lanes()
    stiff = lambda i: data[3, i]
    kx[lo - 1] = half * (stiff(lo - 1) + stiff(lo))

    def body(i, _):
        centre = stiff(i)
        xp = half * (centre + stiff(i + 1))
        xm = kx[i - 1]
        yp = half * (centre + ahead_y(centre))
        ym = behind_y(yp)
        zp = half * (centre + jnp.where(back, 0.0, ahead_z(centre)))
        zm = half * (centre + jnp.where(front, 0.0, behind_z(centre)))
        total = ((xp + xm) + (yp + ym)) + (zp + zm) + data[4, i]
        kx[i] = xp
        ky[i] = yp
        kym[i] = ym
        kz[i] = jnp.where(back, 0.0, zp)
        kzm[i] = jnp.where(front, 0.0, zm)
        diag[i] = total
        inverse = jnp.where(inside(i), 1.0 / (total + 2.0 * BETA * level.scale), 0.0)
        inv[i] = inverse
        scaled = inverse * (1.0 / THETA)
        for c in range(3):
            value = scaled * data[c, i]
            state[c, i] = value
            direction[c, i] = value
        return 0

    lax.fori_loop(lo, hi, body, 0, unroll=8 if hi - lo == 8 else 7 if hi - lo == 14 else 4)
    for c in range(3):
        ghosts(level, state, (c,))


def sweep(level, src, coef, state, lo, hi, prepare, emit):
    kx, ky, kym, kz, kzm, diag, inv = coef
    front, back = level.lanes()
    bulk = BETA * level.scale

    def spread(i):
        ux, uy, uz = state[0, i], state[1, i], state[2, i]
        return (
            (state[0, i + 1] - ux)
            + (ahead_y(uy) - uy)
            + (jnp.where(back, 0.0, ahead_z(uz)) - uz)
        ) * bulk

    def body(i, before):
        here = spread(i)
        extra = prepare(i)
        for c in range(3):
            u = state[c, i]
            flux = kx[i] * state[c, i + 1] + kx[i - 1] * state[c, i - 1]
            flux = flux + (ky[i] * ahead_y(u) + kym[i] * behind_y(u))
            flux = flux + (kz[i] * ahead_z(u) + kzm[i] * behind_z(u))
            if c == 0:
                other = before
            elif c == 1:
                other = behind_y(here)
            else:
                other = jnp.where(front, bulk * u, behind_z(here))
            resid = src[c, i] - diag[i] * u + flux + (here - other)
            emit(i, c, u, resid, extra)
        return here

    lax.fori_loop(lo, hi, body, spread(lo - 1), unroll=level.unroll)


def step(level, number, src, coef, state, fresh, direction, lo, hi):
    keep, gain = STEPS[number]
    inv = coef[6]

    def emit(i, c, u, resid, scaled):
        move = scaled * resid
        if number > 0:
            move = move + keep * direction[c, i]
        direction[c, i] = move
        fresh[c, i] = u + move

    sweep(level, src, coef, state, lo, hi, lambda i: gain * inv[i], emit)
    for c in range(3):
        ghosts(level, fresh, (c,))


def residual(level, src, coef, state, out, lo, hi):
    def emit(i, c, u, resid, extra):
        out[c, i] = resid

    sweep(level, src, coef, state, lo, hi, lambda i: None, emit)


def pick(rows, cols, rule, value):
    shape = (rows, cols)
    return jnp.where(rule(row_of(shape), lane_of(shape)), value, 0.0).astype(F32)


def mix(values, matrix):
    return jnp.dot(values, matrix, precision=lax.Precision.HIGH, preferred_element_type=F32)


def pairs(ref, index, start, count):
    return ref[(*index, pl.ds(start, count, 2))] + ref[(*index, pl.ds(start + 1, count, 2))]


def vmem(count):
    return [pl.BlockSpec(memory_space=pltpu.VMEM)] * count


def call(kernel, outs, scratch, *args, name, aliases={}):
    smem = pl.BlockSpec(memory_space=pltpu.SMEM)
    return pl.pallas_call(
        kernel,
        out_shape=[jax.ShapeDtypeStruct(s, F32) for s in outs],
        in_specs=[smem] + vmem(len(args) - 1),
        out_specs=vmem(len(outs)),
        scratch_shapes=[pltpu.VMEM(s, F32) for s in scratch],
        compiler_params=pltpu.CompilerParams(vmem_limit_bytes=28 * 2**20),
        input_output_aliases=aliases,
        name=name,
    )(*args)


def by_parity(index, act):
    odd = index % 2

    @pl.when(odd == 0)
    def _():
        act(True)

    @pl.when(odd == 1)
    def _():
        act(False)


def cut_kernel(place, f, k, r, first, second, sems):
    def act(even):
        copies = []
        for side, out in enumerate((second, first) if even else (first, second)):
            rows = pl.ds(HALO * side, HALO)
            copies += [
                pltpu.make_async_copy(f.at[:, :, rows], out.at[0:3], sems.at[3 * side]),
                pltpu.make_async_copy(k.at[:, rows], out.at[3], sems.at[3 * side + 1]),
                pltpu.make_async_copy(r.at[:, rows], out.at[4], sems.at[3 * side + 2]),
            ]
        for copy in copies:
            copy.start()
        for copy in copies:
            copy.wait()

    by_parity(place[1], act)


def cut(place, f, k, r):
    return pl.pallas_call(
        cut_kernel,
        out_shape=[jax.ShapeDtypeStruct((5, 16, HALO, LANES), F32)] * 2,
        in_specs=[pl.BlockSpec(memory_space=pltpu.SMEM)]
        + [pl.BlockSpec(memory_space=pltpu.HBM)] * 3,
        out_specs=vmem(2),
        scratch_shapes=[pltpu.SemaphoreType.DMA((6,))],
        compiler_params=pltpu.CompilerParams(vmem_limit_bytes=CUT_LIMIT),
        name="cut0",
    )(place, f, k, r)


MESSAGE = [(0, 0, 7), (1, 7, 7), (2, 14, 7), (4, 21, 7), (3, 28, 8)]


def join_kernel(place, f, k, r, first, second, data, near, far):
    def sides(even):
        lo, hi = (second, first) if even else (first, second)
        for q in range(5):
            data[q, 8:24, 0:8] = lo[q]
            data[q, 8:24, 8:24] = f[q] if q < 3 else (k, r)[q - 3][...]
            data[q, 8:24, 24:32] = hi[q]

    by_parity(place[1], sides)

    def act(even):
        up, down = (near, far) if even else (far, near)
        for q, at, rows in MESSAGE:
            down[at : at + rows] = data[q, 8 : 8 + rows]
            up[at : at + rows] = data[q, 24 - rows : 24]

    by_parity(place[0], act)


FINE = Level(1.0, 128, 30, 32)
FINE_UP = Level(1.0, 128, 22, 24)
MIDDLE = Level(0.25, 64, 14, 32)
MIDDLE_UP = Level(0.25, 64, 10, 24, 5)
COARSE = Level(0.0625, 32, 8, 48, 8)
COARSE_UP = Level(0.0625, 32, 8, 32, 8)
LAST = Level(0.015625, 16, 2, 24)


def coef_shapes(level):
    return [level.shape()] * 7


def fine_inside(place):
    y = place[1] * 16 - HALO + row_of((32, LANES))
    fits = (y >= 0) & (y < place[3] * 16)

    def inside(i):
        x = place[0] * 16 + i - HALO
        return fits & (x >= 0) & (x < place[2] * 16)

    return inside


def fine_take(data, message, low):
    zero = jnp.zeros((32, LANES), F32)
    for q, at, rows in MESSAGE:
        start = 8 - rows if low else 24
        data[q, start : start + rows] = message[at : at + rows]
        if rows < 8:
            data[q, 0 if low else 31] = zero


def fine_pass(place, refs, pair, ranges, known):
    data, kept, s0, d0, t0, resid, wide, saved = refs
    coef = [kept.at[j] for j in range(7)]
    setup(FINE, data, coef, fine_inside(place), s0, d0, *ranges[0])
    step(FINE, 1, data, coef, s0, t0, d0, *ranges[1])
    step(FINE, 2, data, coef, t0, s0, d0, *ranges[2])
    step(FINE, 3, data, coef, s0, t0, d0, *ranges[3])
    lo, hi = ranges[3]
    saved[:, lo - 4 : hi - 4] = t0[:, lo:hi, 4:28]
    residual(FINE, data, coef, t0, resid, *ranges[4])
    for q in range(5):
        ref = resid if q < 3 else data
        for t in known[q < 3]:
            half, i = divmod(t, 8)
            pair[t] = ref[q, 2 * t] + ref[q, 2 * t + 1]
            wide[q, i, :, half * LANES : half * LANES + LANES] = pairs(pair, (t,), 0, 16)


def fine_inner(place, given, near, *refs):
    *refs, pair = refs
    data, wide = refs[0], refs[6]
    zero = jnp.zeros((16, LANES), F32)

    def act(even):
        fine_take(data, near, not even)
        for q in range(3):
            for t in (0, 1, 2, 13, 14, 15):
                half, i = divmod(t, 8)
                wide[q, i, :, half * LANES : half * LANES + LANES] = zero
        if even:
            ranges = ((9, 31), (10, 30), (11, 29), (12, 28), (13, 26))
            known = (range(4, 16), range(7, 13))
        else:
            ranges = ((1, 23), (2, 22), (3, 21), (4, 20), (6, 19))
            known = (range(0, 12), range(3, 9))
        fine_pass(place, refs, pair, ranges, known)

    by_parity(place[0], act)


def fine_outer(place, far, *refs):
    *refs, packed, first, second, pair = refs[8:]
    data, wide = refs[0], refs[6]

    def act(even):
        fine_take(data, far, even)
        if even:
            ranges = ((1, 9), (2, 10), (3, 11), (4, 12), (6, 13))
            known = (range(0, 4), range(3, 7))
        else:
            ranges = ((23, 31), (22, 30), (21, 29), (20, 28), (19, 26))
            known = (range(12, 16), range(9, 13))
        fine_pass(place, refs, pair, ranges, known)

    by_parity(place[0], act)
    matrix = pick(
        2 * LANES, LANES, lambda a, b: (a % LANES) // 2 + 64 * (a // LANES) == b, 0.125
    )
    packed[...] = mix(wide[...].reshape(5 * 8 * 16, 2 * LANES), matrix).reshape(5, 8, 16, LANES)

    def send(even):
        left, right = (second, first) if even else (first, second)
        for q in range(5):
            skip = 1 if q < 3 else 2
            left[q] = packed[q, :, 4 + skip : 12 + skip]
            right[q] = packed[q, :, 4 - skip : 12 - skip]

    by_parity(place[1], send)


def fine_trim(place, data, kept, data_up, kept_up):
    for q in range(3):
        data_up[q] = data[q, 4:28, 4:28]
    for j in range(7):
        kept_up[j] = kept[j, 4:28, 4:28]


def middle_cut(place, own, first, second, trimmed, near, far, centre):
    low = lane_of((32, LANES)) < 64
    zero = jnp.zeros((4, LANES), F32)

    def sides(even):
        left, right = (second, first) if even else (first, second)
        for q in range(5):
            skip = 1 if q < 3 else 2
            for i in range(8):
                centre[q, i, 0 : 4 - skip] = zero[0 : 4 - skip]
                centre[q, i, 4 - skip : 12 - skip] = left[q, i]
                centre[q, i, 12 - skip : 20 + skip] = own[q, i, 4 - skip : 12 + skip]
                centre[q, i, 20 + skip : 28 + skip] = right[q, i]
                centre[q, i, 28 + skip : 32] = zero[0 : 4 - skip]

    by_parity(place[1], sides)

    def at(q, x, half):
        value = centre[q, x + 4 if x < 4 else x - 4]
        return value if (x >= 4) == (half == 1) else pltpu.roll(value, 64, 1)

    def act(even):
        up, down = (near, far) if even else (far, near)
        for q in range(5):
            skip = 1 if q < 3 else 2
            for t in range(4):
                up[q, t] = jnp.where(low, at(q, t - skip, 0), at(q, t - skip + 4, 1))
                down[q, t] = jnp.where(low, at(q, t + skip, 0), at(q, t + skip + 4, 1))

    by_parity(place[0], act)


def middle_inside(place):
    y = place[1] * 8 - SKIRT + row_of((32, LANES))
    fits = (y >= 0) & (y < place[3] * 8)
    x0 = place[0] * 8 - NEAR + 14 * (lane_of((32, LANES)) // 64)

    def inside(i):
        x = x0 + (i - 1)
        return fits & (x >= 0) & (x < place[2] * 8)

    return inside


def middle_join(centre, lo, hi, data):
    low = lane_of((32, LANES)) < 64
    zero = jnp.zeros((32, LANES), F32)

    def moved(ref, q, t, half):
        value = ref[q, t % 4]
        return value if t // 4 == half else pltpu.roll(value, 64, 1)

    for q in range(5):
        skip = 1 if q < 3 else 2
        for i in range(14):
            t = i - (2 - skip)
            if t < 0:
                a = zero
            elif t < 8:
                a = moved(lo, q, t, 0)
            else:
                a = centre[q, i - 6]
            t = i - (4 + skip)
            if t < 0:
                b = centre[q, i]
            elif t < 8:
                b = moved(hi, q, t, 1)
            else:
                b = zero
            data[q, i + 1] = jnp.where(low, a, b)
        ghosts(MIDDLE, data, (q,))


def middle_down(place, centre, near, far, data, saved, packed, kept, s1, d1, t1, pair, sums):
    coef = [kept.at[j] for j in range(7)]
    lane = lane_of((32, LANES))
    low = lane < 64
    by_parity(
        place[0],
        lambda even: middle_join(centre, *((far, near) if even else (near, far)), data),
    )
    setup(MIDDLE, data, coef, middle_inside(place), s1, d1, 1, 15)
    step(MIDDLE, 1, data, coef, s1, t1, d1, 1, 15)
    step(MIDDLE, 2, data, coef, t1, s1, d1, 1, 15)
    step(MIDDLE, 3, data, coef, s1, saved, d1, 1, 15)
    residual(MIDDLE, data, coef, saved, d1, 11, 15)
    residual(MIDDLE, data, coef, saved, d1, 1, 5)
    for q in range(5):
        from_, at = (d1, q) if q < 3 else (data, q)
        for m in range(2):
            a = from_[at, 11 + 2 * m] + from_[at, 12 + 2 * m]
            b = from_[at, 1 + 2 * m] + from_[at, 2 + 2 * m]
            pair[q, m] = jnp.where(low, a, b)
            sums[q, :, m * LANES : m * LANES + LANES] = pairs(pair, (q, m), 0, 16)
    matrix = pick(
        2 * LANES,
        LANES,
        lambda a, b: (a // LANES) * 32 + ((a % LANES) // 64) * 64 + (a % 64) // 2 == b,
        0.125,
    )
    packed[...] = mix(sums[...].reshape(5 * 16, 2 * LANES), matrix).reshape(5, 16, LANES)


def middle_trim(place, data, saved, kept, data_up, saved_up, kept_up):
    low = lane_of((24, LANES)) < 64
    groups = [(data, data_up, 3), (saved, saved_up, 3), (kept, kept_up, 7)]
    for old, new, count in groups:
        for q in range(count):
            for j in range(12):
                new[q, j] = jnp.where(low, old[q, 4 + j, 2:26], old[q, j, 2:26])


def column_kernel(place, parts, out):
    zero = jnp.zeros((4, LANES), F32)
    for q in range(5):
        out[q, 0:2] = zero[0:2]
        out[q, 46:48] = zero[0:2]
    for d in range(2 * REACH + 1):
        at = place[1] + (d - REACH)
        valid = (at >= 0) & (at < place[3])
        safe = jnp.clip(at, 0, place[3] - 1)
        for q in range(5):
            block = parts[safe, q]
            out[q, 2 + 4 * d : 6 + 4 * d] = jnp.where(valid, block, zero)


def coarse_inside(place):
    sub = row_of((48, LANES))
    y = place[1] * 4 - 22 + sub
    fits = (y >= 0) & (y < place[3] * 4)
    return lambda i: fits


def last_inside(place):
    y = place[1] * 2 - 11 + row_of((24, LANES))
    fits = (y >= 0) & (y < place[3] * 2)
    return lambda i: fits


def climb(place, mine, other, data1, saved1, kept1, data0, saved0, kept0, out, *scratch):
    scratch = list(scratch)

    def take(count):
        got, scratch[:] = scratch[:count], scratch[count:]
        return got

    data2, s2, t2, d2, keep2 = take(5)
    coef2 = take(7)
    sums3 = take(1)[0]
    data3, s3, t3, d3 = take(4)
    coef3 = take(7)
    grown3, grown2, grown1 = take(3)
    s1, t1, d1 = take(3)
    s0, t0, d0 = take(3)
    coef1 = [kept1.at[j] for j in range(7)]
    coef0 = [kept0.at[j] for j in range(7)]

    group = lane_of((48, LANES)) // 32

    def act(even):
        order = (mine, other) if even else (other, mine)
        for q in range(5):
            for i in range(8):
                row = None
                for g in range(4):
                    block = order[i // 4][g, q]
                    shift = ((g - i % 4) * 32) % LANES
                    block = pltpu.roll(block, shift, 1) if shift else block
                    row = block if row is None else jnp.where(group == g, block, row)
                data2[q, i + 1] = row
            ghosts(COARSE, data2, (q,))

    by_parity(place[0], act)
    setup(COARSE, data2, coef2, coarse_inside(place), s2, d2, 1, 9)
    step(COARSE, 1, data2, coef2, s2, t2, d2, 1, 9)
    step(COARSE, 2, data2, coef2, t2, s2, d2, 1, 9)
    step(COARSE, 3, data2, coef2, s2, keep2, d2, 1, 9)
    residual(COARSE, data2, coef2, keep2, d2, 1, 9)

    pair = s2.at[0]
    for q in range(5):
        from_ = d2 if q < 3 else data2
        for t in range(4):
            half, i = divmod(t, 2)
            pair[t] = from_[q, 1 + 2 * t] + from_[q, 2 + 2 * t]
            sums3[q, i, :, half * LANES : half * LANES + LANES] = pairs(pair, (t,), 0, 24)
    matrix = pick(
        2 * LANES,
        LANES,
        lambda a, b: (2 * ((a % LANES) // 32) + a // LANES) * 16 + (a % 32) // 2 == b,
        0.125,
    )
    shrunk = mix(sums3[...].reshape(5 * 2 * 24, 2 * LANES), matrix).reshape(5, 2, 24, LANES)
    for q in range(5):
        for i in range(2):
            data3[q, i + 1] = shrunk[q, i]
        ghosts(LAST, data3, (q,))
    setup(LAST, data3, coef3, last_inside(place), s3, d3, 1, 3)
    step(LAST, 1, data3, coef3, s3, t3, d3, 1, 3)
    step(LAST, 2, data3, coef3, t3, s3, d3, 1, 3)
    step(LAST, 3, data3, coef3, s3, t3, d3, 1, 3)

    data2u, s2u, t2u, d2u = (ref.at[:, :, 8:40] for ref in (data2, s2, t2, d2))
    coef2u = [ref.at[:, 8:40] for ref in coef2]
    matrix = pick(
        LANES,
        2 * LANES,
        lambda a, b: (2 * ((b % LANES) // 32) + b // LANES == a // 16) & ((b % 32) // 2 == a % 16),
        1.0,
    )
    flat = jnp.concatenate([t3[c, i + 1] for c in range(3) for i in range(2)], axis=0)
    wide = mix(flat, matrix)
    for c in range(3):
        for t in range(4):
            half, i = divmod(t, 2)
            at = (c * 2 + i) * 24
            piece = wide[at : at + 24, half * LANES : half * LANES + LANES]
            grown3[c, t, pl.ds(0, 24, 2)] = piece
            grown3[c, t, pl.ds(1, 24, 2)] = piece
            more = grown3[c, t, 8:40]
            s2u[c, 1 + 2 * t] = keep2[c, 1 + 2 * t, 8:40] + more
            s2u[c, 2 + 2 * t] = keep2[c, 2 + 2 * t, 8:40] + more
        ghosts(COARSE_UP, s2u, (c,))
    step(COARSE_UP, 0, data2u, coef2u, s2u, t2u, d2u, 1, 9)
    step(COARSE_UP, 1, data2u, coef2u, t2u, s2u, d2u, 1, 9)
    step(COARSE_UP, 2, data2u, coef2u, s2u, t2u, d2u, 1, 9)
    step(COARSE_UP, 3, data2u, coef2u, t2u, s2u, d2u, 1, 9)

    matrix = pick(
        LANES,
        LANES,
        lambda a, b: (a < 64) & (b // 64 == a // 32) & ((b % 64) // 2 == a % 32),
        1.0,
    )
    small = lane_of((16, LANES)) < 32

    def window(c, x, slot):
        valid = (x >= 0) & (x < place[2] * 4)
        safe = jnp.clip(x, 0, place[2] * 4 - 1)
        value = s2[c, 1 + safe % 8, 16:32]
        value = pltpu.roll(value, (slot * 32 + LANES - (safe // 8) * 32) % LANES, 1)
        return jnp.where(valid, value, 0.0)

    pieces = []
    for c in range(3):
        for m in range(5):
            x = place[0] * 4 - 3 + m
            pieces.append(jnp.where(small, window(c, x, 0), window(c, x + 5, 1)))
    wide = mix(jnp.concatenate(pieces, axis=0), matrix)
    for c in range(3):
        for m in range(5):
            at = (c * 5 + m) * 16
            piece = wide[at : at + 16]
            grown2[c, m, pl.ds(0, 16, 2)] = piece
            grown2[c, m, pl.ds(1, 16, 2)] = piece
            more = grown2[c, m, 2:26]
            s1[c, 1 + 2 * m] = saved1[c, 1 + 2 * m] + more
            s1[c, 2 + 2 * m] = saved1[c, 2 + 2 * m] + more
        ghosts(MIDDLE_UP, s1, (c,))
    step(MIDDLE_UP, 0, data1, coef1, s1, t1, d1, 1, 11)
    step(MIDDLE_UP, 1, data1, coef1, t1, s1, d1, 1, 11)
    step(MIDDLE_UP, 2, data1, coef1, s1, t1, d1, 1, 11)
    step(MIDDLE_UP, 3, data1, coef1, t1, s1, d1, 1, 11)

    for half in range(2):
        matrix = pick(LANES, LANES, lambda a, b: a == 64 * half + b // 2, 1.0)
        rows = [5 + t for t in range(6)] if half == 0 else [1 + t for t in range(6)]
        flat = jnp.concatenate([s1[c, i, 8:24] for c in range(3) for i in rows], axis=0)
        wide = mix(flat, matrix)
        for c in range(3):
            for t in range(6):
                at = (c * 6 + t) * 16
                piece = wide[at : at + 16]
                grown1[c, t, pl.ds(0, 16, 2)] = piece
                grown1[c, t, pl.ds(1, 16, 2)] = piece
                more = grown1[c, t, 0:24]
                row = 2 * (t + 6 * half)
                s0[c, row] = saved0[c, row] + more
                s0[c, row + 1] = saved0[c, row + 1] + more
    step(FINE_UP, 0, data0, coef0, s0, t0, d0, 1, 23)
    step(FINE_UP, 1, data0, coef0, t0, s0, d0, 2, 22)
    step(FINE_UP, 2, data0, coef0, s0, t0, d0, 3, 21)
    keep, gain = STEPS[3]

    def emit(i, c, u, resid, scaled):
        move = scaled * resid + keep * d0[c, i]
        out[c, i - 4] = (u + move)[4:20]

    sweep(FINE_UP, data0, coef0, t0, 4, 20, lambda i: gain * coef0[6][i], emit)


def swap(value, axis, first):
    count = lax.axis_size(axis)
    ends = [(i, i + 1) for i in range(first, count - 1, 2)]
    return lax.ppermute(value, axis, ends + [(b, a) for a, b in ends])


def on_device(right_side, stiffness, reaction):
    bricks = lax.axis_size("brick")
    count = lax.axis_size("grp")
    place = jnp.stack(
        [lax.axis_index("grp"), lax.axis_index("brick"), jnp.int32(count), jnp.int32(bricks)]
    ).astype(jnp.int32)
    local = (right_side, stiffness, reaction)
    first, second = cut(place, *local)
    first = swap(first, "brick", 0)
    second = swap(second, "brick", 1)
    data0, near, far = call(
        join_kernel,
        [FINE.shape(5)] + [(36, 32, 128)] * 2,
        [],
        place,
        *local,
        first,
        second,
        name="join0",
    )
    far_in = swap(far, "grp", 1)
    near_in = swap(near, "grp", 0)
    states = [FINE.shape(5), FINE.shape(7)] + [FINE.shape(3)] * 4
    states += [(5, 8, 16, 256), (3, 24, 24, 128)]
    pair = [(16, 32, 128)]
    inner = call(fine_inner, states, pair, place, data0, near_in, name="inner0", aliases={1: 0})
    data0, kept0, _, _, _, _, _, saved0, packed1, first, second = call(
        fine_outer,
        states + [(5, 8, 16, 128)] + [(5, 8, 8, 128)] * 2,
        pair,
        place,
        far_in,
        *inner,
        name="outer0",
        aliases={2 + j: j for j in range(8)},
    )
    first = swap(first, "brick", 0)
    second = swap(second, "brick", 1)
    data0, kept0 = call(
        fine_trim, [FINE_UP.shape(3), FINE_UP.shape(7)], [], place, data0, kept0, name="trim0"
    )
    near, far, centre = call(
        middle_cut,
        [(5, 4, 32, 128)] * 2 + [(5, 8, 32, 128)],
        [],
        place,
        packed1,
        first,
        second,
        data0,
        name="cut1",
    )
    far_in = swap(far, "grp", 1)
    near_in = swap(near, "grp", 0)
    data1, saved1, packed2, kept1 = call(
        middle_down,
        [MIDDLE.shape(5), MIDDLE.shape(3), (5, 16, 128), MIDDLE.shape(7)],
        [MIDDLE.shape(3)] * 3 + [(5, 2, 32, 128), (5, 16, 256)],
        place,
        centre,
        near_in,
        far_in,
        name="down1",
    )
    block = packed2[:, 6:10]
    parts = lax.all_to_all(jnp.broadcast_to(block[None], (bricks, 5, 4, 128)), "brick", 0, 0)
    (column,) = call(column_kernel, [(5, 48, 128)], [], place, parts, name="column")
    mine = lax.all_to_all(
        jnp.broadcast_to(column[None], (count // 2, 5, 48, 128)),
        "grp",
        0,
        0,
        axis_index_groups=[list(range(core, count, 2)) for core in range(2)],
    )
    other = swap(mine, "grp", 0)
    data1, saved1, kept1 = call(
        middle_trim,
        [MIDDLE_UP.shape(3)] * 2 + [MIDDLE_UP.shape(7)],
        [],
        place,
        data1,
        saved1,
        kept1,
        name="trim1",
    )
    coarse = [COARSE.shape(5)] + [COARSE.shape(3)] * 4 + coef_shapes(COARSE)
    last = [(5, 2, 24, 256), LAST.shape(5)] + [LAST.shape(3)] * 3 + coef_shapes(LAST)
    grown = [(3, 4, 48, 128), (3, 5, 32, 128), (3, 6, 32, 128)]
    (answer,) = call(
        climb,
        [(3, 16, 16, 128)],
        coarse + last + grown + [MIDDLE_UP.shape(3)] * 3 + [FINE_UP.shape(3)] * 3,
        place,
        mine,
        other,
        data1,
        saved1,
        kept1,
        data0,
        saved0,
        kept0,
        name="climb",
    )
    return answer


def solution(mesh):
    in_specs = (P(None, "grp", "brick", None), P("grp", "brick", None), P("grp", "brick", None))
    out_specs = P(None, "grp", "brick", None)
    return jax.shard_map(
        on_device, mesh=mesh, in_specs=in_specs, out_specs=out_specs, check_vma=False
    )
```
